32 devices in a mesh: section: 2 (over x), dp: 4 (over z), tensor: 4 (over y, core).
Axes of the slice: x: 2, y: 2, z: 4, core: 2. Of those that a mesh axis runs over, the one named last changes fastest.
Arguments:
- frames: bfloat16 [2, 1408, 768], P(None, ('dp', 'tensor')), may hold values from -6 to 6
- out_grad: bfloat16 [2, 1408, 768], P(None, ('dp', 'tensor')), may hold values from -6 to 6
- clip_ids: int32 [2, 1408], replicated, may hold values from 0 to 1, never falling along the last dimension, each value on 1 to 1232 neighbouring positions
- w_qkv: bfloat16 [2, 768, 3, 768], P('section', None, None, 'tensor'), may hold values from -0.21875 to 0.21875
- bias_qv: bfloat16 [2, 2, 768], P('section', None, 'tensor'), may hold values from -4 to 4
- w_out: bfloat16 [2, 768, 768], P('section', 'tensor'), may hold values from -2 to 2
- w_up: bfloat16 [2, 768, 3072], P('section', None, 'tensor'), may hold values from -0.21875 to 0.21875
- bias_up: bfloat16 [2, 3072], P('section', 'tensor'), may hold values from -4 to 4
- w_down: bfloat16 [2, 3072, 768], P('section', 'tensor'), may hold values from -0.109375 to 0.109375
- ln_gain: bfloat16 [2, 2, 768], P('section'), may hold values from 0.25 to 1.75
- shifts: bfloat16 [2, 4, 768], P('section'), may hold values from -4 to 4
Outputs:
- acts: bfloat16 [2, 2, 1408, 768], P('section', None, ('dp', 'tensor'))
- in_grads: bfloat16 [2, 2, 1408, 768], P('section', None, ('dp', 'tensor'))
- grad_qkv: float32 [2, 768, 3, 768], P('section', 'dp', None, 'tensor')
- grad_bias_qv: float32 [2, 2, 12, 64], P('section', None, 'tensor', 'dp')
- grad_out: float32 [2, 768, 768], P('section', 'tensor', 'dp')
- grad_up: float32 [2, 768, 3072], P('section', 'dp', 'tensor')
- grad_bias_up: float32 [2, 12, 256], P('section', 'tensor', 'dp')
- grad_down: float32 [2, 3072, 768], P('section', 'tensor', 'dp')
- grad_gain: float32 [2, 2, 768], P('section', None, ('dp', 'tensor'))
- grad_shift: float32 [2, 4, 768], P('section', None, ('dp', 'tensor'))
The draws below stay inside these ranges and needn't reach their ends.
Inputs may be any that keep to these rules, and one draw needn't show every extreme that they name: `clip_ids`: clip numbers never fall along a micro-batch's frames; every clip has 1 to 1232 frames.
All inputs are finite; a program needn't handle non-finite values.
Results may differ from the reference program's by a relative error of at most 0.017.
Values may be sent and summed in bfloat16 or wider, within the bound.
A program may use at most 192 MiB of HBM per device.

```python
import math
from functools import partial
import jax
import jax.numpy as jnp
import numpy as np
from jax import lax

D = 768
H = 12
FF = 3072
HD = 64
MICRO = 2
DP_ROWS = 352
TOKENS = 1408
CLIP_MOST = 1232
SEGS = 2
N_DP = 4


def shard_levels(own_key, extent, split, smallest, top_value):
    gain, own = 1.0, jax.random.fold_in(own_key, 6)
    for position, parts in split:
        draws = jnp.exp(jax.random.uniform(jax.random.fold_in(own, position), (parts,), jnp.float32, smallest / len(split), top_value / len(split)))
        gain = gain * jnp.repeat(draws, extent[position] // parts).reshape([-1 if axis == position else 1 for axis in range(len(extent))])
    return gain


def split_up(amount, total, most, slope):
    weights = [(1 << 20) // math.isqrt(rank ** slope) + 1 for rank in range(2, amount + 1)]
    rest, counts = total - most - (amount - 1), [1] * (amount - 1)
    while rest > 0:
        movable = [i for i in range(amount - 1) if counts[i] < most]
        pool, budget = sum([weights[i] for i in movable]), rest
        for i in movable:
            more = min(most - counts[i], max(1, budget * weights[i] // pool), rest)
            counts[i] = counts[i] + more
            rest = rest - more
    return np.array([most] + counts)


def uneven_parts(stream_key, amount, total, limit, slope):
    if amount == 2:
        one = jax.random.randint(stream_key, (), max(1, total - limit), min(limit, total - 1) + 1)
        return jnp.stack([one, total - one])
    lengths = jnp.asarray(split_up(amount, total, limit, slope), jnp.int32)
    twos = (amount - 1) // 2
    source_of, receiver = lengths[1:1 + 2 * twos:2], lengths[2:2 + 2 * twos:2]
    room = jnp.minimum(source_of - 1, limit - receiver)
    shifted = jax.random.randint(jax.random.fold_in(stream_key, 1), (twos,), 0, 1 << 20) % (room + 1)
    lengths = lengths.at[1:1 + 2 * twos:2].set(source_of - shifted).at[2:2 + 2 * twos:2].set(receiver + shifted)
    return lengths[jax.random.permutation(jax.random.fold_in(stream_key, 2), amount)]


def scatter_about(stream_key, shape, scale, most, shards=(), dtype=jnp.bfloat16):
    drawn = jax.random.normal(stream_key, shape, jnp.float32) * scale
    if len(shards) > 0:
        drawn = shard_levels(stream_key, shape, shards, -0.22, 0.18) * drawn
    return jnp.clip(drawn, min=-most, max=most).astype(dtype)


def setup_inputs(seed: int = 0) -> dict:
    key_list = jax.random.split(jax.random.key(seed), 12)
    frames = scatter_about(key_list[0], (MICRO, TOKENS, D), 1.0, 6.0, ((1, 16),))
    out_grad = scatter_about(key_list[1], (MICRO, TOKENS, D), 1.0, 6.0, ((1, 16),))
    clip_ids = jax.vmap(lambda own: jnp.searchsorted(jnp.cumsum(uneven_parts(own, SEGS, TOKENS, CLIP_MOST, 1)), jnp.arange(TOKENS), side="right"))(jax.random.split(key_list[2], MICRO)).reshape((MICRO, TOKENS)).astype(jnp.int32)
    w_qkv = scatter_about(key_list[3], (2, D, 3, D), D ** -0.5, 0.21875, ((0, 2), (3, 4)))
    bias_qv = scatter_about(key_list[4], (2, 2, D), 0.3, 4.0, ((0, 2), (2, 4)))
    w_out = scatter_about(key_list[5], (2, D, D), (max(D * 16 // CLIP_MOST, 1)) ** -0.5, 2.0, ((0, 2), (1, 4)))
    w_up = scatter_about(key_list[6], (2, D, FF), D ** -0.5, 0.21875, ((0, 2), (2, 4)))
    bias_up = scatter_about(key_list[7], (2, FF), 0.3, 4.0, ((0, 2), (1, 4)))
    w_down = scatter_about(key_list[8], (2, FF, D), FF ** -0.5, 0.109375, ((0, 2), (1, 4)))
    ln_gain = jnp.clip(1.0 + 0.15 * jax.random.normal(key_list[9], (2, 2, D), jnp.float32), 0.25, 1.75).astype(jnp.bfloat16)
    shifts = scatter_about(key_list[10], (2, 4, D), 0.3, 4.0, ((0, 2),))
    return dict(frames=frames, out_grad=out_grad, clip_ids=clip_ids, w_qkv=w_qkv, bias_qv=bias_qv, w_out=w_out, w_up=w_up, bias_up=bias_up, w_down=w_down, ln_gain=ln_gain, shifts=shifts)


@jax.custom_vjp
def low(v):
    return lax.optimization_barrier(v.astype(jnp.bfloat16)).astype(jnp.float32)

@jax.custom_vjp
def low_back(v):
    return v

def low_keep(v):
    return (low(v), None)

def low_pass(kept, grad):
    return (grad,)

def back_keep(v):
    return (v, None)

def back_low(kept, grad):
    return (low(grad),)
low.defvjp(low_keep, low_pass)
low_back.defvjp(back_keep, back_low)

def matmul(form, left, right):
    return jnp.einsum(form, left, right, precision=lax.Precision.HIGHEST)

def normalize(values, gain_row, shift_row):
    center = values - lax.optimization_barrier(jnp.mean(values, axis=-1, keepdims=True))
    spread = lax.optimization_barrier(jnp.mean(center * center, axis=-1, keepdims=True))
    return center * lax.rsqrt(spread + 1e-05) * gain_row + shift_row

def attend_block(block_pair, key_heads, value_heads, clip_row):
    query_blk, clip_blk = block_pair
    scores = low_back(matmul('qhd,khd->qhk', query_blk, key_heads) * 0.125)
    same_clip = clip_blk[:, None] == clip_row[None, :]
    scores = jnp.where(same_clip[:, None, :], scores, -1e+30)
    attn_prob = jax.nn.softmax(scores, axis=-1)
    return matmul('qhk,khd->qhd', low(attn_prob), value_heads)

def encoder_layer(inputs, clip_row, w_qkv, bias_qv, w_out, w_up, bias_up, w_down, ln_gain, shifts):
    row_count = inputs.shape[0]
    normed = low(normalize(inputs, ln_gain[0], shifts[0]))
    projected = matmul('td,dcf->tcf', normed, w_qkv)
    queries = low_back(low(projected[:, 0] + bias_qv[0]))
    key_rows = low_back(low(projected[:, 1]))
    value_rows = low_back(low(projected[:, 2] + bias_qv[1]))
    key_heads = key_rows.reshape(row_count, H, HD)
    value_heads = value_rows.reshape(row_count, H, HD)
    query_blocks = queries.reshape(N_DP, DP_ROWS, H, HD)
    clip_blocks = clip_row.reshape(N_DP, DP_ROWS)
    block_fn = jax.checkpoint(partial(attend_block, key_heads=key_heads, value_heads=value_heads, clip_row=clip_row))
    attended = lax.map(block_fn, (query_blocks, clip_blocks))
    attended = low_back(low(attended.reshape(row_count, D)))
    hidden = inputs + low_back(matmul('tf,fd->td', attended, w_out)) + shifts[2]
    second = low(normalize(hidden, ln_gain[1], shifts[1]))
    up_proj = low_back(matmul('td,df->tf', second, w_up) + bias_up)
    gelu_out = low(jax.nn.gelu(up_proj, approximate=False))
    return hidden + low_back(matmul('tf,fd->td', gelu_out, w_down)) + shifts[3]

def reference(frames, out_grad, clip_ids, w_qkv, bias_qv, w_out, w_up, bias_up, w_down, ln_gain, shifts):
    section_params = []
    for section_no in range(2):
        section_params.append(tuple((weight_set[section_no].astype(jnp.float32) for weight_set in (w_qkv, bias_qv, w_out, w_up, bias_up, w_down, ln_gain, shifts))))
    grad_sums = [tuple((jnp.zeros_like(weight_set) for weight_set in param_set)) for param_set in section_params]
    first_outs, second_outs, first_grads, second_grads = ([], [], [], [])
    for micro_idx in range(MICRO):
        clip_row = clip_ids[micro_idx]

        def section_fn(inputs, *weights):
            return encoder_layer(inputs, clip_row, *weights)
        first_out, first_back = jax.vjp(section_fn, frames[micro_idx].astype(jnp.float32), *section_params[0])
        first_low = first_out.astype(jnp.bfloat16)
        second_out, second_back = jax.vjp(section_fn, first_low.astype(jnp.float32), *section_params[1])
        second_terms = second_back(out_grad[micro_idx].astype(jnp.float32))
        passed = second_terms[0].astype(jnp.bfloat16)
        first_terms = first_back(passed.astype(jnp.float32))
        grad_sums[0] = tuple((running_sum + new_term for running_sum, new_term in zip(grad_sums[0], first_terms[1:])))
        grad_sums[1] = tuple((running_sum + new_term for running_sum, new_term in zip(grad_sums[1], second_terms[1:])))
        first_outs.append(first_low)
        second_outs.append(second_out.astype(jnp.bfloat16))
        first_grads.append(first_terms[0].astype(jnp.bfloat16))
        second_grads.append(passed)

    def both_sections(index_no):
        return jnp.stack([grad_sums[0][index_no], grad_sums[1][index_no]])
    acts = jnp.stack([jnp.stack(first_outs), jnp.stack(second_outs)])
    in_grads = jnp.stack([jnp.stack(first_grads), jnp.stack(second_grads)])
    return (acts, in_grads, both_sections(0), both_sections(1).reshape(2, 2, H, HD), both_sections(2), both_sections(3), both_sections(4).reshape(2, H, FF // H), both_sections(5), both_sections(6), both_sections(7))
```

```python
import functools

import jax
import jax.numpy as jnp
from jax import lax
from jax.experimental import pallas as pl
from jax.experimental.pallas import tpu as pltpu
from jax.sharding import PartitionSpec as P

HD = 64
BIG = 2.0**100
MESH = pl.DeviceIdType.MESH
BF = jnp.bfloat16
F32 = jnp.float32
RB = 16
SLOTS = 4
MOST = 4


def nt(a, b):
    return lax.dot_general(a, b, (((1,), (1,)), ((), ())), preferred_element_type=F32)


def nn(a, b):
    return lax.dot_general(a, b, (((1,), (0,)), ((), ())), preferred_element_type=F32)


def tn(a, b):
    return lax.dot_general(a, b, (((0,), (0,)), ((), ())), preferred_element_type=F32)


def scratch_plan(nd, rows, dim, head_dim, ff):
    half = nd // 2
    full = 4 * rows
    two = 2 * rows
    part = dim // nd
    wide = 640 + ff + 256 + ff
    vm = pltpu.VMEM
    dma = pltpu.SemaphoreType.DMA
    return dict(
        wqb=vm((2, 640, dim), BF),
        wob=vm((2, 256, dim), BF),
        wub=vm((2, dim, ff), BF),
        wdb=vm((2, ff, dim), BF),
        spb=vm((2, 16, dim), F32),
        xq=vm((2, rows, dim), BF),
        gq=vm((2, rows, dim), BF),
        xres=vm((two, dim), F32),
        dyf=vm((two, dim), F32),
        dyb=vm((2, 2, two, dim), BF),
        nb=vm((2, 2, two, dim), BF),
        sb=vm((2, 2, two, dim), BF),
        hid=vm((two, dim), F32),
        u1=vm((2, two, dim), F32),
        u2=vm((2, two, dim), F32),
        r1=vm((2, two, 1), F32),
        r2=vm((2, two, 1), F32),
        qa=vm((2, full, 256), BF),
        kvb=vm((2, nd, full, 384), BF),
        kt=vm((full, 256), BF),
        vt=vm((full, 256), BF),
        dgo=vm((2, full, 256), BF),
        mst=vm((3, full, 1), F32),
        lst=vm((3, full, 1), F32),
        attf=vm((2, full, 256), F32),
        attb=vm((2, 2, two, 256), BF),
        gl=vm((2, 2, two, ff), BF),
        gp=vm((2, 2, two, ff), F32),
        du=vm((2, two, ff), BF),
        dhb=vm((2, 2, two, dim), BF),
        dhf=vm((two, dim), F32),
        gm=vm((2, two, 640), BF),
        ma=vm((3, full, 256), BF),
        mb=vm((3, full, 256), BF),
        dqs=vm((full, 256), F32),
        dks=vm((full, 256), F32),
        dvs=vm((full, 256), F32),
        cs=vm((two, dim), BF),
        cr=vm((SLOTS, two, dim), BF),
        ys=vm((2, two, dim), BF),
        yr=vm((SLOTS, two, dim), BF),
        chip=vm((2, two, dim), F32),
        gr=vm((2, dim, wide), BF),
        ar=vm((2, half - 1, 2, part, wide), BF),
        bs=vm((2, part, wide), BF),
        br=vm((2, part, wide), BF),
        c2s=vm((part, wide), BF),
        c2r=vm((part, wide), BF),
        smo=vm((2, 8, dim), F32),
        smc=vm((2, 8, dim), F32),
        smr=vm((2 * nd - 1, 8, dim), F32),
        stt=vm((6, RB, dim), F32),
        oq=vm((4, rows, dim), BF),
        s_loc=dma((12,)),
        s_red=dma((4,)),
        s_xy=dma((4,)),
        s_wx=dma((2, 5)),
        s_wzs=dma((4, half)),
        s_wzr=dma((4, half)),
        s_ag=dma((2, 8)),
        s_cc=dma((2, SLOTS)),
        s_yy=dma((2, SLOTS)),
        s_kvs=dma((2, nd)),
        s_kvr=dma((2, nd)),
        s_qs=dma((2, nd)),
        s_qr=dma((2, nd)),
        s_ds=dma((2, nd)),
        s_dr=dma((2, nd)),
        s_as=dma((2, 4, half, 2)),
        s_ar=dma((2, 4, half, 2)),
        s_b=dma((2, 4)),
        s_c=dma((2, 4)),
        s_sm=dma((2,)),
        s_sms=dma((2 * nd - 1,)),
        s_smr=dma((2 * nd - 1,)),
        s_out=dma((4, 3)),
    )


def mega(nd, names, *refs):
    (fr, og, wq, wo, wu, wd, sp, kf, qf) = refs[:9]
    (acts, igs, o_q, o_u, o_o, o_d, o_s) = refs[9:16]
    b_ = dict(zip(names, refs[16:]))
    big = nd > MOST

    class Bufs:
        pass

    v = Bufs()
    v.__dict__.update(b_)
    half = nd // 2
    rows, dim = fr.shape[1:]
    two, full = 2 * rows, 4 * rows
    ff = wu.shape[1]
    part = dim // nd
    s = lax.axis_index("section")
    z = lax.axis_index("dp")
    t = lax.axis_index("tensor")
    g, zi = z // half, z % half
    c, y = t % 2, t // 2
    own_b = zi + half * s
    zo = (z + half) % nd
    me_x = (1 - s, z, t)
    me_c = (s, z, t + 1 - 2 * c)
    me_y = (s, z, (t + 2) % 4)
    me_o = (s, zo, t)

    def zpeer(d):
        return (s, g * half + (zi + d) % half, t)

    def member(k):
        zk, sk = (zi + k % half) % half, (s + k // half) % 2
        return (sk, g * half + zk, t), zk + half * sk

    def remote(src, dst, ss, rs, dev):
        return pltpu.make_async_remote_copy(
            src_ref=src, dst_ref=dst, send_sem=ss, recv_sem=rs, device_id=dev, device_id_type=MESH
        )

    late = []

    def send(src, dst, ss, rs, dev):
        cp = remote(src, dst, ss, rs, dev)
        cp.start()
        late.append(cp)
        return cp

    loads = [
        pltpu.make_async_copy(wq.at[pl.ds(0, 192)], v.wqb.at[s, pl.ds(0, 192)], v.s_loc.at[0]),
        pltpu.make_async_copy(wq.at[pl.ds(192, 384)], v.wqb.at[s, pl.ds(256, 384)], v.s_loc.at[1]),
        pltpu.make_async_copy(wo, v.wob.at[s, pl.ds(64, 192)], v.s_loc.at[2]),
        pltpu.make_async_copy(wu, v.wub.at[s], v.s_loc.at[3]),
        pltpu.make_async_copy(wd, v.wdb.at[s], v.s_loc.at[4]),
        pltpu.make_async_copy(sp, v.spb.at[s], v.s_loc.at[5]),
    ]
    for cp in loads:
        cp.start()
    v.wqb[s, pl.ds(192, 64), :] = jnp.zeros((64, dim), BF)
    v.wob[s, pl.ds(0, 64), :] = jnp.zeros((64, dim), BF)

    barrier = pltpu.get_barrier_semaphore()
    for k in range(1, 2 * nd):
        other = (s * nd + z + k) % (2 * nd)
        pl.semaphore_signal(barrier, inc=1, device_id=(other // nd, other % nd, t), device_id_type=MESH)
    for dev in (me_c, me_y):
        pl.semaphore_signal(barrier, inc=1, device_id=dev, device_id_type=MESH)
    pl.semaphore_wait(barrier, 2 * nd + 1)

    keeps = g == s

    def red(src, dst, i):
        @pl.when(keeps)
        def _():
            pltpu.make_async_copy(src.at[g], dst.at[0], v.s_loc.at[6 + i]).start()
            remote(src.at[1 - g], dst.at[0], v.s_red.at[i], v.s_red.at[2 + i], me_o).start()

    def red_wait(src, dst, i):
        @pl.when(keeps)
        def _():
            pltpu.make_async_copy(src.at[g], dst.at[0], v.s_loc.at[6 + i]).wait()

        @pl.when(jnp.logical_not(keeps))
        def _():
            remote(src.at[1 - g], dst.at[0], v.s_red.at[i], v.s_red.at[2 + i], me_o).wait_recv()

    red(fr, v.xq, 0)
    for cp in loads[:2]:
        cp.wait()
    loads[5].wait()
    mats = (v.wqb, v.wob, v.wub, v.wdb)

    def w_rows(i, p):
        n = mats[i].shape[1] // half
        return pl.ds(pl.multiple_of(p * n, 16), n)

    def ship(i):
        src = mats[i].at[s, w_rows(i, zi)]
        send(src, src, v.s_wx.at[0, i], v.s_wx.at[1, i], me_x)

    send(v.spb.at[s], v.spb.at[s], v.s_wx.at[0, 4], v.s_wx.at[1, 4], me_x)
    ship(0)
    loads[2].wait()
    ship(1)
    loads[3].wait()
    ship(2)
    loads[4].wait()
    ship(3)
    red(og, v.gq, 1)

    def forward_w(i):
        src = mats[i].at[1 - s, w_rows(i, zi)]
        remote(src, src, v.s_wx.at[0, i], v.s_wx.at[1, i], me_x).wait_recv()
        for d in range(1, half):
            send(src, src, v.s_wzs.at[i, d], v.s_wzr.at[i, d], zpeer(d))

    def gather_w(i, layer):
        @pl.when(s != layer)
        def _():
            for d in range(1, half):
                src = mats[i].at[1 - s, w_rows(i, (zi + half - d) % half)]
                remote(src, src, v.s_wzs.at[i, d], v.s_wzr.at[i, d], zpeer(d)).wait_recv()

    red_wait(fr, v.xq, 0)
    send(v.xq.at[0], v.xq.at[1], v.s_xy.at[0], v.s_xy.at[1], me_y)
    remote(v.spb.at[s], v.spb.at[s], v.s_wx.at[0, 4], v.s_wx.at[1, 4], me_x).wait_recv()
    q_own = pl.ds(pl.multiple_of(rows * y, 8), rows)
    q_oth = pl.ds(pl.multiple_of(rows * (1 - y), 8), rows)
    v.xres[q_own, :] = v.xq[0].astype(F32)
    remote(v.xq.at[0], v.xq.at[1], v.s_xy.at[0], v.s_xy.at[1], me_y).wait_recv()
    v.xres[q_oth, :] = v.xq[1].astype(F32)

    def prow(layer, i):
        return v.spb[layer, i : i + 1, :]

    def row_loop(fn, n=two):
        def step(i, carry):
            fn(pl.ds(pl.multiple_of(i * RB, RB), RB))
            return carry

        lax.fori_loop(0, n // RB, step, 0)

    def unit(x):
        cen = x - jnp.mean(x, axis=-1, keepdims=True)
        r = lax.rsqrt(jnp.mean(cen * cen, axis=-1, keepdims=True) + 1e-05)
        return cen * r, r

    def share(buf, layer, i):
        src = buf.at[layer, c]
        send(src, src, v.s_ag.at[0, i], v.s_ag.at[1, i], me_c)

    def share_wait(buf, layer, i):
        src = buf.at[layer, 1 - c]
        remote(src, src, v.s_ag.at[0, i], v.s_ag.at[1, i], me_c).wait_recv()

    def norm_one(layer):
        gain, shift = prow(layer, 0), prow(layer, 2)

        def body(rs):
            u, r = unit(v.xres[rs, :])
            v.u1[layer, rs, :] = u
            v.r1[layer, rs, :] = r
            v.nb[layer, c, rs, :] = (u * gain + shift).astype(BF)

        row_loop(body)
        share(v.nb, layer, layer)

    def sum_begin(j, term):
        k = j % SLOTS
        v.cs[...] = term(1 - c).astype(BF)
        cp = remote(v.cs, v.cr.at[k], v.s_cc.at[0, k], v.s_cc.at[1, k], me_c)
        cp.start()
        v.chip[j % 2] = term(c)
        cp.wait()

        def body(rs):
            tot = v.chip[j % 2, rs, :] + v.cr[k, rs, :].astype(F32)
            v.chip[j % 2, rs, :] = tot
            v.ys[j % 2, rs, :] = tot.astype(BF)

        row_loop(body)
        remote(v.ys.at[j % 2], v.yr.at[k], v.s_yy.at[0, k], v.s_yy.at[1, k], me_y).start()

    def sum_end(j):
        k = j % SLOTS
        remote(v.ys.at[j % 2], v.yr.at[k], v.s_yy.at[0, k], v.s_yy.at[1, k], me_y).wait()

    def sum_rows(j, rs):
        k = j % SLOTS
        return v.chip[j % 2, rs, :] + v.yr[k, rs, :].astype(F32)

    lane_f = lax.broadcasted_iota(jnp.int32, (full, 256), 1)
    lane = lax.broadcasted_iota(jnp.int32, (full, 128), 1)

    def k_mask(h):
        return (
            ((lane_f >= 64 * h) & (lane_f < 64 * h + 64))
            | ((lane_f >= 192 + 3 * h) & (lane_f < 195 + 3 * h))
            | (lane_f >= 208)
        )

    def v_mask(h):
        return ((lane_f >= 64 * h + 64) & (lane_f < 64 * h + 128)) | (
            (lane_f >= 3 * h) & (lane_f < 3 * h + 3)
        )

    def by_head_k(a):
        return jnp.where(lane_f < 64, a[0], jnp.where(lane_f < 128, a[1], a[2]))

    def by_head_v(a):
        return jnp.where(lane_f < 128, a[0], jnp.where(lane_f < 192, a[1], a[2]))

    def put_masked(dst, val, mask):
        val = val.astype(F32)
        for h in range(3):
            dst[h] = jnp.where(mask(h), val, 0.0).astype(BF)

    def build_kv(layer, bk):
        v.kt[:, 0:128] = v.kvb[layer, bk, :, 0:128]
        mid = v.kvb[layer, bk, :, 128:256].astype(F32)
        v.kt[:, 128:256] = jnp.where(lane < 64, mid, kf[bk].astype(F32)).astype(BF)
        v.vt[:, 0:128] = jnp.where(lane < 64, jnp.where(lane < 9, 1.0, 0.0), mid).astype(BF)
        v.vt[:, 128:256] = v.kvb[layer, bk, :, 256:384]

    def splits(x):
        hi = x.astype(BF).astype(F32)
        mid = (x - hi).astype(BF).astype(F32)
        return hi, mid, (x - hi) - mid

    def group_send(src, dst, ss, rs):
        for k in range(1, nd):
            dev, _ = member(k)
            send(src, dst, ss.at[k], rs.at[own_b], dev)

    def group_wait(buf, layer, rs, k, ss):
        dev, bk = member(k)
        dst = buf.at[layer, bk]
        remote(dst, dst, ss.at[0], rs.at[bk], dev).wait_recv()

    halves = (lambda i: c, lambda i: 1 - c)

    def forward(layer):
        bias_q, bias_kv = v.spb[layer, 7:8, 0:256], v.spb[layer, 8:9, 0:384]

        def qkv(hf):
            r = nt(v.nb[layer, hf], v.wqb[layer])
            rs = pl.ds(pl.multiple_of(hf * two, 16), two)
            q = (r[:, 0:256] + bias_q).astype(BF).astype(F32) * 0.125
            v.qa[layer, rs, 0:128] = q[:, 0:128].astype(BF)
            v.qa[layer, rs, 128:256] = (q[:, 128:256] + qf[rs, :].astype(F32)).astype(BF)
            v.kvb[layer, own_b, rs, :] = (r[:, 256:640] + bias_kv).astype(BF)

        if layer == 0:
            forward_w(0)
        gather_w(0, layer)
        qkv(c)
        share_wait(v.nb, layer, layer)
        qkv(1 - c)
        group_send(v.kvb.at[layer, own_b], v.kvb.at[layer, own_b], v.s_kvs.at[layer], v.s_kvr.at[layer])

        put_masked(v.ma, v.qa[layer], k_mask)
        v.mst[...] = jnp.full(v.mst.shape, -3e38, F32)
        v.lst[...] = jnp.zeros(v.lst.shape, F32)
        v.dqs[...] = jnp.zeros(v.dqs.shape, F32)

        def block(k, carry):
            zk, sk = (zi + k % half) % half, (s + k // half) % 2
            bk = zk + half * sk

            @pl.when(k > 0)
            def _():
                dst = v.kvb.at[layer, bk]
                remote(dst, dst, v.s_kvs.at[layer, 0], v.s_kvr.at[layer, bk], me_x).wait_recv()

            build_kv(layer, bk)
            kt, vt = v.kt[...], v.vt[...]
            alphas, news = [], []
            for h in range(3):
                sc = nt(v.ma[h], kt)
                old = v.mst[h]
                new = jnp.maximum(old, jnp.max(sc, axis=1, keepdims=True))
                alpha = jnp.exp(old - new)
                p = jnp.exp(sc - new)
                v.mst[h] = new
                v.lst[h] = v.lst[h] * alpha + jnp.sum(p, axis=1, keepdims=True)
                hi = p.astype(BF)
                lo = (p - hi.astype(F32)).astype(BF)
                news.append(nn(hi, vt) + nn(lo, vt))
                alphas.append(alpha)
            v.dqs[...] = v.dqs[...] * by_head_v(alphas) + by_head_v(news)
            return carry

        block(0, 0)
        if layer == 0:
            forward_w(1)
            forward_w(2)
        lax.fori_loop(1, nd, block, 0)

        att = v.dqs[...] * by_head_v([1.0 / v.lst[h] for h in range(3)])
        v.attf[layer] = att
        v.attb[layer] = att.astype(BF).reshape(2, two, 256)
        tile = v.qa[layer, :, 128:256].astype(F32)
        for h in range(3):
            for i, piece in enumerate(splits(-(v.mst[h] + jnp.log(v.lst[h])))):
                tile = jnp.where(lane == 64 + 3 * h + i, piece, tile)
        v.qa[layer, :, 128:256] = tile.astype(BF)
        if layer == 0:
            forward_w(3)
        gather_w(1, layer)
        sum_begin(2 * layer, lambda hf: nn(v.attb[layer, hf], v.wob[layer]))
        group_send(v.qa.at[layer], v.qg.at[layer, own_b], v.s_qs.at[layer], v.s_qr.at[layer])
        sum_end(2 * layer)
        out_bias, gain2, shift2 = prow(layer, 4), prow(layer, 1), prow(layer, 3)

        def body(rs):
            hid = v.xres[rs, :] + sum_rows(2 * layer, rs) + out_bias
            v.hid[rs, :] = hid
            u, r = unit(hid)
            v.u2[layer, rs, :] = u
            v.r2[layer, rs, :] = r
            v.sb[layer, c, rs, :] = (u * gain2 + shift2).astype(BF)

        row_loop(body)
        share(v.sb, layer, 2 + layer)
        gather_w(2, layer)
        bias_up = prow(layer, 6)

        def up(hf):
            v.gp[layer, hf] = nn(v.sb[layer, hf], v.wub[layer]) + bias_up

            def gelu(rs):
                u = v.gp[layer, hf, rs, :]
                phi = 0.5 * (1.0 + lax.erf(u * 0.7071067811865476))
                v.gl[layer, hf, rs, :] = (u * phi).astype(BF)
                v.gp[layer, hf, rs, :] = phi + u * (jnp.exp(-0.5 * u * u) * 0.3989422804014327)

            row_loop(gelu)

        up(c)
        share_wait(v.sb, layer, 2 + layer)
        up(1 - c)
        gather_w(3, layer)
        sum_begin(2 * layer + 1, lambda hf: nn(v.gl[layer, hf], v.wdb[layer]))

    def forward_end(layer):
        sum_end(2 * layer + 1)
        out_bias = prow(layer, 5)

        def body(rs):
            out = v.hid[rs, :] + sum_rows(2 * layer + 1, rs) + out_bias
            v.xres[rs, :] = out.astype(BF).astype(F32)

        row_loop(body)
        if layer == 0:
            norm_one(1)
        put_out(layer, layer, v.xres, acts)

    def put_out(i, layer, src, dst):
        v.oq[i] = src[q_own, :].astype(BF)
        here = keeps & (s == layer)

        @pl.when(here)
        def _():
            pltpu.make_async_copy(v.oq.at[i], dst.at[g], v.s_loc.at[8 + i]).start()

        @pl.when(jnp.logical_not(here))
        def _():
            remote(v.oq.at[i], dst.at[g], v.s_out.at[i, 0], v.s_out.at[i, 1 + g], (layer, own_b, t)).start()

    def put_out_wait(i, layer, dst):
        here = keeps & (s == layer)

        @pl.when(here)
        def _():
            pltpu.make_async_copy(v.oq.at[i], dst.at[g], v.s_loc.at[8 + i]).wait()

        @pl.when(jnp.logical_not(here))
        def _():
            remote(v.oq.at[i], dst.at[g], v.s_out.at[i, 0], v.s_out.at[i, 1 + g], (layer, own_b, t)).wait_send()

        @pl.when(s == layer)
        def _():
            def got(m):
                remote(v.oq.at[i], dst.at[m], v.s_out.at[i, 0], v.s_out.at[i, 1 + m], me_x).wait_recv()

            got(1 - g)

            @pl.when(g != s)
            def _():
                got(g)

    col = dict(d=0, u=ff, o=2 * ff, q=2 * ff + 256)
    width = dict(d=ff, u=ff, o=256, q=640)

    def grad_of(layer, key, left, right):
        o, n = col[key], width[key]
        for i in range(dim // 256):
            lo = i * 256
            v.gr[layer, lo : lo + 256, o : o + n] = tn(left[:, lo : lo + 256], right).astype(BF)
        i = "duoq".index(key)
        for d in range(1, half):
            zp = (zi + d) % half
            for k in range(2):
                rs = pl.ds(pl.multiple_of((zp + half * k) * part, 16), part)
                send(
                    v.gr.at[layer, rs, pl.ds(o, n)],
                    v.ar.at[layer, d - 1, k, :, pl.ds(o, n)],
                    v.s_as.at[layer, i, d, k],
                    v.s_ar.at[layer, i, d, k],
                    zpeer(d),
                )

    def rows_of(buf, layer):
        x = buf[layer]
        return x.reshape(full, x.shape[-1])

    def back_rows(layer, j, u_buf, r_buf, gain, base, at, extra=None):
        v.stt[...] = jnp.zeros(v.stt.shape, F32)

        def body(rs):
            gsec = sum_rows(j, rs)
            u, r = u_buf[layer, rs, :], r_buf[layer, rs, :]
            gg = gsec * gain
            res = r * (
                gg - jnp.mean(gg, axis=-1, keepdims=True) - u * jnp.mean(gg * u, axis=-1, keepdims=True)
            )
            inn = base[rs, :]
            out = inn + res
            at(rs, out)
            v.stt[0] += gsec * u
            v.stt[1] += gsec
            v.stt[2] += out
            v.stt[3] += inn

        row_loop(body)

    def backward_begin(layer):
        def d_second(hf):
            dgel = nt(v.dyb[layer, hf], v.wdb[layer])
            v.du[hf] = (dgel * v.gp[layer, hf]).astype(BF)
            return nt(v.du[hf], v.wub[layer])

        sum_begin(4 + 2 * (1 - layer), d_second)

    def backward(layer):
        j = 4 + 2 * (1 - layer)
        grad_of(layer, "d", rows_of(v.dyb, layer), rows_of(v.gl, layer))
        grad_of(layer, "u", rows_of(v.sb, layer), v.du[...].reshape(full, ff))
        ones = jnp.ones((8, full), BF)
        v.smo[layer, 6:7, :] = nn(ones, v.du[...].reshape(full, ff))[0:1]
        sum_end(j)

        def at_two(rs, out):
            v.dhf[rs, :] = out
            v.dhb[layer, c, rs, :] = out.astype(BF)

        back_rows(layer, j, v.u2, v.r2, prow(layer, 1), v.dyf, at_two)
        share(v.dhb, layer, 4 + layer)
        for i, row in ((0, 1), (1, 3), (2, 4), (3, 5)):
            v.smo[layer, row : row + 1, :] = jnp.sum(v.stt[i], axis=0, keepdims=True)

        def d_att(hf):
            rs = pl.ds(pl.multiple_of(hf * two, 16), two)
            v.dgo[layer, rs, :] = nt(v.dhb[layer, hf], v.wob[layer]).astype(BF)

        d_att(c)
        share_wait(v.dhb, layer, 4 + layer)
        d_att(1 - c)
        dat = v.dgo[layer].astype(F32)
        prod = dat * v.attf[layer]
        tile = dat[:, 0:128]
        for h in range(3):
            real = (lane_f >= 64 * h + 64) & (lane_f < 64 * h + 128)
            delta = jnp.sum(jnp.where(real, prod, 0.0), axis=1, keepdims=True)
            for i, piece in enumerate(splits(-delta)):
                tile = jnp.where(lane == 3 * h + i, piece, tile)
        v.dgo[layer, :, 0:128] = tile.astype(BF)
        group_send(v.dgo.at[layer], v.dg.at[layer, own_b], v.s_ds.at[layer], v.s_dr.at[layer])
        grad_of(layer, "o", rows_of(v.dhb, layer), rows_of(v.attb, layer))

        put_masked(v.ma, v.qa[layer], k_mask)
        put_masked(v.mb, v.dgo[layer], v_mask)
        v.dqs[...] = jnp.zeros(v.dqs.shape, F32)

        def query_block(bk, carry):
            build_kv(layer, bk)
            kt, vt = v.kt[...], v.vt[...]
            terms = []
            for h in range(3):
                p = jnp.exp(nt(v.ma[h], kt))
                ds = (p * nt(v.mb[h], vt)).astype(BF)
                terms.append(nn(ds, kt))
            v.dqs[...] += by_head_k(terms)
            return carry

        lax.fori_loop(0, nd, query_block, 0)

        build_kv(layer, own_b)
        put_masked(v.ma, v.kt[...], k_mask)
        put_masked(v.mb, v.vt[...], v_mask)
        v.dks[...] = jnp.zeros(v.dks.shape, F32)
        v.dvs[...] = jnp.zeros(v.dvs.shape, F32)

        def key_block(k, carry):
            zk, sk = (zi + k % half) % half, (s + k // half) % 2
            bk = zk + half * sk
            q_at, d_at = v.qg.at[layer, bk], v.dg.at[layer, bk]
            remote(q_at, q_at, v.s_qs.at[layer, 0], v.s_qr.at[layer, bk], me_x).wait_recv()
            remote(d_at, d_at, v.s_ds.at[layer, 0], v.s_dr.at[layer, bk], me_x).wait_recv()
            if big:
                cps = (
                    pltpu.make_async_copy(q_at, v.kt, v.s_loc.at[0]),
                    pltpu.make_async_copy(d_at, v.vt, v.s_loc.at[1]),
                )
                for cp in cps:
                    cp.start()
                for cp in cps:
                    cp.wait()
                key_terms(v.kt[...], v.vt[...])
            else:
                key_terms(q_at[...], d_at[...])
            return carry

        def key_terms(qt, dt):
            tk, tv = [], []
            for h in range(3):
                p = jnp.exp(nt(v.ma[h], qt))
                ds = (p * nt(v.mb[h], dt)).astype(BF)
                tv.append(nn(p.astype(BF), dt))
                tk.append(nn(ds, qt))
            v.dks[...] += by_head_k(tk)
            v.dvs[...] += by_head_v(tv)

        key_terms(v.qa[layer], v.dgo[layer])
        lax.fori_loop(1, nd, key_block, 0)

        for i in range(2):
            rs = slice(i * two, (i + 1) * two)
            v.gm[i, :, 0:128] = (v.dqs[rs, 0:128] * 0.125).astype(BF)
            v.gm[i, :, 128:256] = jnp.where(lane[rs] < 64, v.dqs[rs, 128:256] * 0.125, 0.0).astype(BF)
            v.gm[i, :, 256:384] = v.dks[rs, 0:128].astype(BF)
            v.gm[i, :, 384:512] = jnp.where(lane[rs] < 64, v.dks[rs, 128:256], v.dvs[rs, 0:128]).astype(BF)
            v.gm[i, :, 512:640] = v.dvs[rs, 128:256].astype(BF)
        sum_begin(j + 1, lambda hf: nn(v.gm[hf], v.wqb[layer]))
        grad_of(layer, "q", rows_of(v.nb, layer), v.gm[...].reshape(full, 640))
        v.smo[layer, 7:8, :] = jnp.zeros((1, dim), F32)
        v.smo[layer, 7:8, 0:640] = nn(ones, v.gm[...].reshape(full, 640))[0:1]
        sum_end(j + 1)

        def at_one(rs, out):
            low = out.astype(BF)
            v.dyf[rs, :] = low.astype(F32)
            if layer == 1:
                v.dyb[0, c, rs, :] = low

        back_rows(layer, j + 1, v.u1, v.r1, prow(layer, 0), v.dhf, at_one)
        for i, row in ((0, 0), (1, 2)):
            v.smo[layer, row : row + 1, :] = jnp.sum(v.stt[i], axis=0, keepdims=True)
        if layer == 1:
            share(v.dyb, 0, 7)
        put_out(2 + layer, layer, v.dyf, igs)

    norm_one(0)
    forward(0)
    forward_end(0)
    red_wait(og, v.gq, 1)
    send(v.gq.at[0], v.gq.at[1], v.s_xy.at[2], v.s_xy.at[3], me_y)
    forward(1)
    v.dyf[q_own, :] = v.gq[0].astype(F32)
    remote(v.gq.at[0], v.gq.at[1], v.s_xy.at[2], v.s_xy.at[3], me_y).wait_recv()
    v.dyf[q_oth, :] = v.gq[1].astype(F32)
    v.dyb[1, c] = v.dyf[...].astype(BF)
    share(v.dyb, 1, 6)
    share_wait(v.dyb, 1, 6)
    backward_begin(1)
    forward_end(1)
    backward(1)
    share_wait(v.dyb, 0, 7)
    backward_begin(0)
    backward(0)

    for layer in (1, 0):
        for i in range(4):
            key = "duoq"[i]
            for d in range(1, half):
                for k in range(2):
                    dst = v.ar.at[layer, d - 1, k, :, pl.ds(col[key], width[key])]
                    remote(dst, dst, v.s_as.at[layer, i, d, k], v.s_ar.at[layer, i, d, k], zpeer(d)).wait_recv()

    def pair_sum(layer, k, rs):
        own = pl.ds(pl.multiple_of((zi + half * k) * part + rs.start, 16), RB)
        tot = v.gr[layer, own, :].astype(F32)
        for d in range(1, half):
            tot = tot + v.ar[layer, d - 1, k, rs, :].astype(F32)
        return tot

    for k in range(2):

        def send_rows(rs, k=k):
            v.bs[k, rs, :] = pair_sum(1 - s, k, rs).astype(BF)

        row_loop(send_rows, part)
        send(v.bs.at[k], v.br.at[k], v.s_b.at[0, k], v.s_b.at[1, k], me_x)
    send(v.smo, v.smc, v.s_sm.at[0], v.s_sm.at[1], me_c).wait_recv()
    for layer in range(2):
        rowid = lax.broadcasted_iota(jnp.int32, (8, dim), 0)
        v.smc[layer] = v.smo[layer] + jnp.where(rowid < 6, v.smc[layer], 0.0)
    for k in range(1, 2 * nd):
        other = (s * nd + z + k) % (2 * nd)
        so = other // nd
        send(v.smc.at[so], v.smr.at[k - 1], v.s_sms.at[k - 1], v.s_smr.at[k - 1], (so, other % nd, t))

    def put(rs, tot):
        for o_ref, key in ((o_d, "d"), (o_u, "u"), (o_o, "o"), (o_q, "q")):
            o_ref[rs, :] = tot[:, col[key] : col[key] + width[key]]

    for k in (1, 0):
        kk = (g + k) % 2
        remote(v.bs.at[kk], v.br.at[kk], v.s_b.at[0, kk], v.s_b.at[1, kk], me_x).wait_recv()

        def add_rows(rs, k=k, kk=kk):
            tot = pair_sum(s, kk, rs) + v.br[kk, rs, :].astype(F32)
            if k == 1:
                v.c2s[rs, :] = tot.astype(BF)
            else:
                put(rs, tot)

        row_loop(add_rows, part)
        if k == 1:
            send(v.c2s, v.c2r, v.s_c.at[0, 0], v.s_c.at[1, 0], me_o)
    for k in range(1, 2 * nd):
        remote(v.smr.at[0], v.smr.at[k - 1], v.s_sms.at[k - 1], v.s_smr.at[k - 1], me_x).wait_recv()
    tot = v.smc[s]
    for k in range(1, 2 * nd):
        tot = tot + v.smr[k - 1]
    o_s[...] = tot
    remote(v.c2s, v.c2r, v.s_c.at[0, 0], v.s_c.at[1, 0], me_o).wait_recv()

    def last_rows(rs):
        for o_ref, key in ((o_d, "d"), (o_u, "u"), (o_o, "o"), (o_q, "q")):
            o_ref[rs, :] += v.c2r[rs, col[key] : col[key] + width[key]].astype(F32)

    row_loop(last_rows, part)

    for cp in late:
        cp.wait_send()
    for i, src, dst in ((0, fr, v.xq), (1, og, v.gq)):

        @pl.when(keeps)
        def _(i=i, src=src, dst=dst):
            remote(src.at[1 - g], dst.at[0], v.s_red.at[i], v.s_red.at[2 + i], me_o).wait_send()

    put_out_wait(0, 0, acts)
    put_out_wait(1, 1, acts)
    put_out_wait(2, 0, igs)
    put_out_wait(3, 1, igs)


def local(frames, out_grad, clip_ids, w_qkv, bias_qv, w_out, w_up, bias_up, w_down, ln_gain, shifts):
    rows, dim = frames.shape[1:]
    nd = lax.axis_size("dp")
    half = nd // 2
    z, t, s = lax.axis_index("dp"), lax.axis_index("tensor"), lax.axis_index("section")
    hl = w_qkv.shape[3]
    ff = w_up.shape[2]
    part = dim // nd
    wide = w_qkv[0].transpose(1, 2, 0).reshape(3 * hl, dim)
    zeros = functools.partial(jnp.zeros, dtype=F32)
    params = jnp.concatenate(
        [
            ln_gain[0].astype(F32),
            shifts[0].astype(F32),
            bias_up.astype(F32),
            jnp.pad(bias_qv[0, 0].astype(F32), (0, dim - hl))[None],
            jnp.pad(bias_qv[0, 1].astype(F32), (hl, dim - 2 * hl))[None],
            zeros((7, dim)),
        ]
    )
    clip = lax.dynamic_index_in_dim(clip_ids, z // half, 0, keepdims=False)
    clip = clip.reshape(nd, 4, rows)
    clip = jnp.stack([clip[:, 0], clip[:, 2], clip[:, 1], clip[:, 3]], axis=1).reshape(nd, 4 * rows)
    lane = jnp.arange(128)
    same = clip[:, :, None] == (lane - 80)[None, None, :]
    spot = lane >= 80
    k_feat = jnp.where(
        (lane >= 64) & (lane < 73), 1.0, jnp.where(spot & jnp.logical_not(same), -BIG, 0.0)
    ).astype(BF)
    own_b = z % half + half * s
    q_feat = jnp.where(spot & lax.dynamic_index_in_dim(same, own_b, 0, keepdims=False), 1.0, 0.0).astype(BF)

    plan = scratch_plan(nd, rows, dim, hl, ff)
    shape = jax.ShapeDtypeStruct
    anyspec = pl.BlockSpec(memory_space=pl.ANY)
    vspec = pl.BlockSpec(memory_space=pltpu.VMEM)
    gathered = {name: (2, nd, 4 * rows, 256) for name in ("qg", "dg")}
    big = nd > MOST
    if not big:
        plan.update({name: pltpu.VMEM(dims, BF) for name, dims in gathered.items()})
    outs = pl.pallas_call(
        functools.partial(mega, nd, (*gathered, *plan) if big else tuple(plan)),
        out_shape=(
            shape((2, rows, dim), BF),
            shape((2, rows, dim), BF),
            shape((part, 640), F32),
            shape((part, ff), F32),
            shape((part, 256), F32),
            shape((part, ff), F32),
            shape((8, dim), F32),
        )
        + tuple(shape(dims, BF) for dims in gathered.values()) * big,
        in_specs=[anyspec] * 7 + [vspec] * 2,
        out_specs=(anyspec,) * 2 + (vspec,) * 5 + (anyspec,) * (2 * big),
        scratch_shapes=list(plan.values()),
        compiler_params=pltpu.CompilerParams(
            collective_id=0, has_side_effects=True, vmem_limit_bytes=63 * 1024 * 1024
        ),
    )(frames, out_grad, wide, w_out[0], w_up[0], w_down[0], params, k_feat, q_feat)

    acts, igs, g_q, g_u, g_o, g_d, small = outs[:7]
    g_qkv = jnp.stack([g_q[:, 0:hl], g_q[:, 256 : 256 + hl], g_q[:, 256 + hl : 256 + 2 * hl]], axis=1)
    bias = small[7]
    bias = jnp.stack([bias[0:hl], bias[256 + hl : 256 + 2 * hl]]).reshape(2, hl // HD, HD)
    bias = lax.dynamic_slice_in_dim(bias, z * (HD // nd), HD // nd, 2)
    upb = small[6].reshape(hl // HD, ff // (hl // HD))
    upb = lax.dynamic_slice_in_dim(upb, z * (upb.shape[1] // nd), upb.shape[1] // nd, 1)
    own = dim // (4 * nd)
    norms = lax.dynamic_slice_in_dim(small, (z * 4 + t) * own, own, 1)
    return (
        acts[None],
        igs[None],
        g_qkv[None],
        bias[None],
        g_o[:, 64 : 64 + hl].T[None],
        g_u[None],
        upb[None],
        g_d.T[None],
        norms[None, 0:2],
        norms[None, 2:6],
    )


def solution(mesh):
    in_specs = (
        P(None, ("dp", "tensor"), None),
        P(None, ("dp", "tensor"), None),
        P(),
        P("section", None, None, "tensor"),
        P("section", None, "tensor"),
        P("section", "tensor", None),
        P("section", None, "tensor"),
        P("section", "tensor"),
        P("section", "tensor", None),
        P("section", None, None),
        P("section", None, None),
    )
    out_specs = (
        P("section", None, ("dp", "tensor"), None),
        P("section", None, ("dp", "tensor"), None),
        P("section", "dp", None, "tensor"),
        P("section", None, "tensor", "dp"),
        P("section", "tensor", "dp"),
        P("section", "dp", "tensor"),
        P("section", "tensor", "dp"),
        P("section", "tensor", "dp"),
        P("section", None, ("dp", "tensor")),
        P("section", None, ("dp", "tensor")),
    )
    return jax.shard_map(local, mesh=mesh, in_specs=in_specs, out_specs=out_specs, check_vma=False)
```

```python
import functools

import jax
import jax.numpy as jnp
from jax import lax
from jax.experimental import pallas as pl
from jax.experimental.pallas import tpu as pltpu
from jax.sharding import PartitionSpec as P

HD = 64
BIG = 2.0**100
MESH = pl.DeviceIdType.MESH
BF = jnp.bfloat16
F32 = jnp.float32
RB = 16
SLOTS = 4
MOST = 4


def nt(a, b):
    return lax.dot_general(a, b, (((1,), (1,)), ((), ())), preferred_element_type=F32)


def nn(a, b):
    return lax.dot_general(a, b, (((1,), (0,)), ((), ())), preferred_element_type=F32)


def tn(a, b):
    return lax.dot_general(a, b, (((0,), (0,)), ((), ())), preferred_element_type=F32)


def shares(key, ff):
    return {
        "d": (0, ff, ff // 2, ff // 2),
        "u": (ff, ff, ff // 2, ff // 2),
        "o": (2 * ff, 256, 128, 128),
        "q": (2 * ff + 256, 640, 256, 384),
    }[key]


MODES = {
    (1, "d"): "swap",
    (1, "u"): "run",
    (1, "o"): "swap",
    (1, "q"): "swap",
    (0, "d"): "run",
    (0, "u"): "swap",
    (0, "o"): "swap",
    (0, "q"): "swap",
}


def scratch_plan(nd, rows, dim, head_dim, ff):
    half = nd // 2
    full = 4 * rows
    two = 2 * rows
    part = dim // nd
    wide = 640 + ff + 256 + ff
    vm = pltpu.VMEM
    dma = pltpu.SemaphoreType.DMA
    plan = dict(
        wqb=vm((2, 640, dim), BF),
        wob=vm((2, 256, dim), BF),
        wub=vm((2, dim, ff), BF),
        wdb=vm((2, ff, dim), BF),
        spb=vm((2, 16, dim), F32),
        xq=vm((2, rows, dim), BF),
        gq=vm((2, rows, dim), BF),
        xres=vm((two, dim), F32),
        dyf=vm((two, dim), F32),
        dyb=vm((2, 2, two, dim), BF),
        nb=vm((2, 2, two, dim), BF),
        sb=vm((2, 2, two, dim), BF),
        hid=vm((two, dim), F32),
        u1=vm((2, two, dim), F32),
        u2=vm((2, two, dim), F32),
        r1=vm((2, two, 1), F32),
        r2=vm((2, two, 1), F32),
        qa=vm((2, full, 256), BF),
        kvb=vm((2, nd, full, 384), BF),
        kt=vm((full, 256), BF),
        vt=vm((full, 256), BF),
        dgo=vm((2, full, 256), BF),
        mst=vm((3, full, 1), F32),
        lst=vm((3, full, 1), F32),
        attf=vm((2, full, 256), F32),
        attb=vm((2, 2, two, 256), BF),
        gl=vm((2, 2, two, ff), BF),
        gp=vm((2, 2, two, ff), F32),
        du=vm((2, two, ff), BF),
        dhb=vm((2, 2, two, dim), BF),
        dhf=vm((two, dim), F32),
        gm=vm((2, two, 640), BF),
        ma=vm((3, full, 256), BF),
        mb=vm((3, full, 256), BF),
        dqs=vm((full, 256), F32),
        dks=vm((full, 256), F32),
        dvs=vm((full, 256), F32),
        cs=vm((two, dim), BF),
        cr=vm((SLOTS, two, dim), BF),
        ys=vm((2, two, dim), BF),
        yr=vm((SLOTS, two, dim), BF),
        chip=vm((2, two, dim), F32),
        gr=vm((2, dim, wide), BF),
        smo=vm((2, 8, dim), F32),
        smc=vm((2, 8, dim), F32),
        smr=vm((2 * nd - 1, 8, dim), F32),
        stt=vm((6, RB, dim), F32),
        oq=vm((4, rows, dim), BF),
        s_loc=dma((12,)),
        s_red=dma((4,)),
        s_xy=dma((4,)),
        s_wx=dma((2, 9)),
        s_wzs=dma((8, half)),
        s_wzr=dma((8, half)),
        s_ag=dma((2, 8)),
        s_cc=dma((2, SLOTS)),
        s_yy=dma((2, SLOTS)),
        s_kvs=dma((2, nd)),
        s_kvr=dma((2, nd)),
        s_qs=dma((2, nd)),
        s_qr=dma((2, nd)),
        s_ds=dma((2, nd)),
        s_dr=dma((2, nd)),
        s_sm=dma((2,)),
        s_sms=dma((2 * nd - 1,)),
        s_smr=dma((2 * nd - 1,)),
        s_out=dma((4, 3)),
    )
    for (layer, key), mode in MODES.items():
        n = shares(key, ff)[1 if mode == "run" else 3]
        tag = f"{layer}{key}"
        if mode == "swap":
            plan["xr" + tag] = vm((dim, n), BF)
            plan["s_x" + tag] = dma((2,))
        else:
            plan["bs" + tag] = vm((2, part, n), BF)
            plan["br" + tag] = vm((2, part, n), BF)
            plan["s_b" + tag] = dma((2,))
        plan["ar" + tag] = vm((half - 1, 2, part, n), BF)
        plan["s_a" + tag] = dma((2, half, 2))
        plan["cs" + tag] = vm((part, n), BF)
        plan["cr" + tag] = vm((part, n), BF)
        plan["s_c" + tag] = dma((2,))
        if mode == "swap":
            plan["es" + tag] = vm((part, n), BF)
            plan["er" + tag] = vm((part, n), BF)
            plan["s_e" + tag] = dma((2,))
    return plan


def mega(nd, names, *refs):
    (fr, og, wq, wo, wu, wd, sp, kf, qf) = refs[:9]
    (acts, igs, o_q, o_u, o_o, o_d, o_s) = refs[9:16]
    b_ = dict(zip(names, refs[16:]))
    big = nd > MOST

    class Bufs:
        pass

    v = Bufs()
    v.__dict__.update(b_)
    half = nd // 2
    rows, dim = fr.shape[1:]
    two, full = 2 * rows, 4 * rows
    ff = wu.shape[1]
    part = dim // nd
    s = lax.axis_index("section")
    z = lax.axis_index("dp")
    t = lax.axis_index("tensor")
    g, zi = z // half, z % half
    c, y = t % 2, t // 2
    own_b = zi + half * s
    zo = (z + half) % nd
    me_x = (1 - s, z, t)
    me_c = (s, z, t + 1 - 2 * c)
    me_y = (s, z, (t + 2) % 4)
    me_o = (s, zo, t)

    def zpeer(d):
        return (s, g * half + (zi + d) % half, t)

    def member(k):
        zk, sk = (zi + k % half) % half, (s + k // half) % 2
        return (sk, g * half + zk, t), zk + half * sk

    def remote(src, dst, ss, rs, dev):
        return pltpu.make_async_remote_copy(
            src_ref=src, dst_ref=dst, send_sem=ss, recv_sem=rs, device_id=dev, device_id_type=MESH
        )

    late = []

    def send(src, dst, ss, rs, dev):
        cp = remote(src, dst, ss, rs, dev)
        cp.start()
        late.append(cp)
        return cp

    loads = [
        pltpu.make_async_copy(wq.at[pl.ds(0, 192)], v.wqb.at[s, pl.ds(0, 192)], v.s_loc.at[0]),
        pltpu.make_async_copy(wq.at[pl.ds(192, 384)], v.wqb.at[s, pl.ds(256, 384)], v.s_loc.at[1]),
        pltpu.make_async_copy(wo, v.wob.at[s, pl.ds(64, 192)], v.s_loc.at[2]),
        pltpu.make_async_copy(wu, v.wub.at[s], v.s_loc.at[3]),
        pltpu.make_async_copy(wd, v.wdb.at[s], v.s_loc.at[4]),
        pltpu.make_async_copy(sp, v.spb.at[s], v.s_loc.at[5]),
    ]
    for cp in loads:
        cp.start()
    v.wqb[s, pl.ds(192, 64), :] = jnp.zeros((64, dim), BF)
    v.wob[s, pl.ds(0, 64), :] = jnp.zeros((64, dim), BF)

    barrier = pltpu.get_barrier_semaphore()
    for k in range(1, 2 * nd):
        other = (s * nd + z + k) % (2 * nd)
        pl.semaphore_signal(barrier, inc=1, device_id=(other // nd, other % nd, t), device_id_type=MESH)
    for dev in (me_c, me_y):
        pl.semaphore_signal(barrier, inc=1, device_id=dev, device_id_type=MESH)
    pl.semaphore_wait(barrier, 2 * nd + 1)

    keeps = g == s

    def red(src, dst, i):
        @pl.when(keeps)
        def _():
            pltpu.make_async_copy(src.at[g], dst.at[0], v.s_loc.at[6 + i]).start()
            remote(src.at[1 - g], dst.at[0], v.s_red.at[i], v.s_red.at[2 + i], me_o).start()

    def red_wait(src, dst, i):
        @pl.when(keeps)
        def _():
            pltpu.make_async_copy(src.at[g], dst.at[0], v.s_loc.at[6 + i]).wait()

        @pl.when(jnp.logical_not(keeps))
        def _():
            remote(src.at[1 - g], dst.at[0], v.s_red.at[i], v.s_red.at[2 + i], me_o).wait_recv()

    red(fr, v.xq, 0)
    for cp in loads[:2]:
        cp.wait()
    loads[5].wait()
    mats = (v.wqb, v.wob, v.wub, v.wdb)

    def w_parts(i):
        return 2 if mats[i].shape[1] // half % 32 == 0 else 1

    def w_rows(i, p, e):
        n = mats[i].shape[1] // half
        m = n // w_parts(i)
        return pl.ds(pl.multiple_of(p * n + e * m, 16), m)

    def ship(i):
        for e in range(w_parts(i)):
            src = mats[i].at[s, w_rows(i, zi, e)]
            send(src, src, v.s_wx.at[0, 2 * i + e], v.s_wx.at[1, 2 * i + e], me_x)

    send(v.spb.at[s], v.spb.at[s], v.s_wx.at[0, 8], v.s_wx.at[1, 8], me_x)
    ship(0)
    loads[2].wait()
    ship(1)
    loads[3].wait()
    ship(2)
    loads[4].wait()

    def w_copy(i, e, d, back=0):
        src = mats[i].at[1 - s, w_rows(i, (zi + back) % half, e)]
        return remote(src, src, v.s_wzs.at[2 * i + e, d], v.s_wzr.at[2 * i + e, d], zpeer(d))

    def forward_w(i, e=None):
        for e in range(w_parts(i)) if e is None else (e,):
            if e < w_parts(i):
                src = mats[i].at[1 - s, w_rows(i, zi, e)]
                remote(src, src, v.s_wx.at[0, 2 * i + e], v.s_wx.at[1, 2 * i + e], me_x).wait_recv()
                for d in range(1, half):
                    w_copy(i, e, d).start()

    def forward_w_end(i):
        for e in range(w_parts(i)):
            for d in range(1, half):
                w_copy(i, e, d).wait_send()

    def gather_w(i, layer):
        @pl.when(s != layer)
        def _():
            for e in range(w_parts(i)):
                for d in range(1, half):
                    w_copy(i, e, d, half - d).wait_recv()

    red_wait(fr, v.xq, 0)
    send(v.xq.at[0], v.xq.at[1], v.s_xy.at[0], v.s_xy.at[1], me_y)
    remote(v.spb.at[s], v.spb.at[s], v.s_wx.at[0, 8], v.s_wx.at[1, 8], me_x).wait_recv()
    q_own = pl.ds(pl.multiple_of(rows * y, 8), rows)
    q_oth = pl.ds(pl.multiple_of(rows * (1 - y), 8), rows)
    v.xres[q_own, :] = v.xq[0].astype(F32)
    forward_w(0, 0)
    remote(v.xq.at[0], v.xq.at[1], v.s_xy.at[0], v.s_xy.at[1], me_y).wait_recv()
    v.xres[q_oth, :] = v.xq[1].astype(F32)

    def prow(layer, i):
        return v.spb[layer, i : i + 1, :]

    def row_loop(fn, n=two):
        def step(i, carry):
            fn(pl.ds(pl.multiple_of(i * RB, RB), RB))
            return carry

        lax.fori_loop(0, n // RB, step, 0)

    def unit(x):
        cen = x - jnp.mean(x, axis=-1, keepdims=True)
        r = lax.rsqrt(jnp.mean(cen * cen, axis=-1, keepdims=True) + 1e-05)
        return cen * r, r

    def share(buf, layer, i):
        src = buf.at[layer, c]
        send(src, src, v.s_ag.at[0, i], v.s_ag.at[1, i], me_c)

    def share_wait(buf, layer, i):
        src = buf.at[layer, 1 - c]
        remote(src, src, v.s_ag.at[0, i], v.s_ag.at[1, i], me_c).wait_recv()

    def norm_one(layer):
        gain, shift = prow(layer, 0), prow(layer, 2)

        def body(rs):
            u, r = unit(v.xres[rs, :])
            v.u1[layer, rs, :] = u
            v.r1[layer, rs, :] = r
            v.nb[layer, c, rs, :] = (u * gain + shift).astype(BF)

        row_loop(body)
        share(v.nb, layer, layer)

    def sum_begin(j, term):
        k = j % SLOTS
        v.cs[...] = term(1 - c).astype(BF)
        cp = remote(v.cs, v.cr.at[k], v.s_cc.at[0, k], v.s_cc.at[1, k], me_c)
        cp.start()
        v.chip[j % 2] = term(c)
        cp.wait()

        def body(rs):
            tot = v.chip[j % 2, rs, :] + v.cr[k, rs, :].astype(F32)
            v.chip[j % 2, rs, :] = tot
            v.ys[j % 2, rs, :] = tot.astype(BF)

        row_loop(body)
        remote(v.ys.at[j % 2], v.yr.at[k], v.s_yy.at[0, k], v.s_yy.at[1, k], me_y).start()

    def sum_end(j):
        k = j % SLOTS
        remote(v.ys.at[j % 2], v.yr.at[k], v.s_yy.at[0, k], v.s_yy.at[1, k], me_y).wait()

    def sum_rows(j, rs):
        k = j % SLOTS
        return v.chip[j % 2, rs, :] + v.yr[k, rs, :].astype(F32)

    lane_f = lax.broadcasted_iota(jnp.int32, (full, 256), 1)
    lane = lax.broadcasted_iota(jnp.int32, (full, 128), 1)

    def k_mask(h):
        return (
            ((lane_f >= 64 * h) & (lane_f < 64 * h + 64))
            | ((lane_f >= 192 + 3 * h) & (lane_f < 195 + 3 * h))
            | (lane_f >= 208)
        )

    def v_mask(h):
        return ((lane_f >= 64 * h + 64) & (lane_f < 64 * h + 128)) | (
            (lane_f >= 3 * h) & (lane_f < 3 * h + 3)
        )

    def by_head_k(a):
        return jnp.where(lane_f < 64, a[0], jnp.where(lane_f < 128, a[1], a[2]))

    def by_head_v(a):
        return jnp.where(lane_f < 128, a[0], jnp.where(lane_f < 192, a[1], a[2]))

    def put_masked(dst, val, mask):
        val = val.astype(F32)
        for h in range(3):
            dst[h] = jnp.where(mask(h), val, 0.0).astype(BF)

    def build_kv(layer, bk):
        v.kt[:, 0:128] = v.kvb[layer, bk, :, 0:128]
        mid = v.kvb[layer, bk, :, 128:256].astype(F32)
        v.kt[:, 128:256] = jnp.where(lane < 64, mid, kf[bk].astype(F32)).astype(BF)
        v.vt[:, 0:128] = jnp.where(lane < 64, jnp.where(lane < 9, 1.0, 0.0), mid).astype(BF)
        v.vt[:, 128:256] = v.kvb[layer, bk, :, 256:384]

    def splits(x):
        hi = x.astype(BF).astype(F32)
        mid = (x - hi).astype(BF).astype(F32)
        return hi, mid, (x - hi) - mid

    def group_send(src, dst, ss, rs):
        for k in range(1, nd):
            dev, _ = member(k)
            send(src, dst, ss.at[k], rs.at[own_b], dev)

    def group_wait(buf, layer, rs, k, ss):
        dev, bk = member(k)
        dst = buf.at[layer, bk]
        remote(dst, dst, ss.at[0], rs.at[bk], dev).wait_recv()

    halves = (lambda i: c, lambda i: 1 - c)

    def forward(layer):
        bias_q, bias_kv = v.spb[layer, 7:8, 0:256], v.spb[layer, 8:9, 0:384]

        def qkv(hf):
            r = nt(v.nb[layer, hf], v.wqb[layer])
            rs = pl.ds(pl.multiple_of(hf * two, 16), two)
            q = (r[:, 0:256] + bias_q).astype(BF).astype(F32) * 0.125
            v.qa[layer, rs, 0:128] = q[:, 0:128].astype(BF)
            v.qa[layer, rs, 128:256] = (q[:, 128:256] + qf[rs, :].astype(F32)).astype(BF)
            v.kvb[layer, own_b, rs, :] = (r[:, 256:640] + bias_kv).astype(BF)

        if layer == 0:
            forward_w(0, 1)
        gather_w(0, layer)
        qkv(c)
        share_wait(v.nb, layer, layer)
        qkv(1 - c)
        group_send(v.kvb.at[layer, own_b], v.kvb.at[layer, own_b], v.s_kvs.at[layer], v.s_kvr.at[layer])

        put_masked(v.ma, v.qa[layer], k_mask)
        v.mst[...] = jnp.full(v.mst.shape, -3e38, F32)
        v.lst[...] = jnp.zeros(v.lst.shape, F32)
        v.dqs[...] = jnp.zeros(v.dqs.shape, F32)

        def block(k, carry):
            zk, sk = (zi + k % half) % half, (s + k // half) % 2
            bk = zk + half * sk

            @pl.when(k > 0)
            def _():
                dst = v.kvb.at[layer, bk]
                remote(dst, dst, v.s_kvs.at[layer, 0], v.s_kvr.at[layer, bk], me_x).wait_recv()

            if layer == 0:
                for i in (1, 2):

                    @pl.when(k == i)
                    def _(i=i):
                        forward_w(i)

            build_kv(layer, bk)
            kt, vt = v.kt[...], v.vt[...]
            alphas, news = [], []
            for h in range(3):
                sc = nt(v.ma[h], kt)
                old = v.mst[h]
                new = jnp.maximum(old, jnp.max(sc, axis=1, keepdims=True))
                alpha = jnp.exp(old - new)
                p = jnp.exp(sc - new)
                v.mst[h] = new
                v.lst[h] = v.lst[h] * alpha + jnp.sum(p, axis=1, keepdims=True)
                hi = p.astype(BF)
                lo = (p - hi.astype(F32)).astype(BF)
                news.append(nn(hi, vt) + nn(lo, vt))
                alphas.append(alpha)
            v.dqs[...] = v.dqs[...] * by_head_v(alphas) + by_head_v(news)
            return carry

        block(0, 0)
        if layer == 0:
            ship(3)
        lax.fori_loop(1, nd, block, 0)

        att = v.dqs[...] * by_head_v([1.0 / v.lst[h] for h in range(3)])
        v.attf[layer] = att
        v.attb[layer] = att.astype(BF).reshape(2, two, 256)
        tile = v.qa[layer, :, 128:256].astype(F32)
        for h in range(3):
            for i, piece in enumerate(splits(-(v.mst[h] + jnp.log(v.lst[h])))):
                tile = jnp.where(lane == 64 + 3 * h + i, piece, tile)
        v.qa[layer, :, 128:256] = tile.astype(BF)
        gather_w(1, layer)
        sum_begin(2 * layer, lambda hf: nn(v.attb[layer, hf], v.wob[layer]))
        if layer == 1:
            for one in (1, 0):
                group_send(v.qa.at[one], v.qg.at[one, own_b], v.s_qs.at[one], v.s_qr.at[one])
        if layer == 0:
            forward_w(3, 0)
        sum_end(2 * layer)
        out_bias, gain2, shift2 = prow(layer, 4), prow(layer, 1), prow(layer, 3)

        def body(rs):
            hid = v.xres[rs, :] + sum_rows(2 * layer, rs) + out_bias
            v.hid[rs, :] = hid
            u, r = unit(hid)
            v.u2[layer, rs, :] = u
            v.r2[layer, rs, :] = r
            v.sb[layer, c, rs, :] = (u * gain2 + shift2).astype(BF)

        row_loop(body)
        share(v.sb, layer, 2 + layer)
        if layer == 0:
            forward_w(3, 1)
        gather_w(2, layer)
        bias_up = prow(layer, 6)

        def up(hf):
            v.gp[layer, hf] = nn(v.sb[layer, hf], v.wub[layer]) + bias_up

            def gelu(rs):
                u = v.gp[layer, hf, rs, :]
                phi = 0.5 * (1.0 + lax.erf(u * 0.7071067811865476))
                v.gl[layer, hf, rs, :] = (u * phi).astype(BF)
                v.gp[layer, hf, rs, :] = phi + u * (jnp.exp(-0.5 * u * u) * 0.3989422804014327)

            row_loop(gelu)

        up(c)
        share_wait(v.sb, layer, 2 + layer)
        up(1 - c)
        gather_w(3, layer)
        sum_begin(2 * layer + 1, lambda hf: nn(v.gl[layer, hf], v.wdb[layer]))

    def forward_end(layer):
        sum_end(2 * layer + 1)
        out_bias = prow(layer, 5)

        def body(rs):
            out = v.hid[rs, :] + sum_rows(2 * layer + 1, rs) + out_bias
            v.xres[rs, :] = out.astype(BF).astype(F32)

        row_loop(body)
        if layer == 0:
            norm_one(1)
        put_out(layer, layer, v.xres, acts)

    def put_out(i, layer, src, dst):
        v.oq[i] = src[q_own, :].astype(BF)
        here = keeps & (s == layer)

        @pl.when(here)
        def _():
            pltpu.make_async_copy(v.oq.at[i], dst.at[g], v.s_loc.at[8 + i]).start()

        @pl.when(jnp.logical_not(here))
        def _():
            remote(v.oq.at[i], dst.at[g], v.s_out.at[i, 0], v.s_out.at[i, 1 + g], (layer, own_b, t)).start()

    def put_out_wait(i, layer, dst):
        here = keeps & (s == layer)

        @pl.when(here)
        def _():
            pltpu.make_async_copy(v.oq.at[i], dst.at[g], v.s_loc.at[8 + i]).wait()

        @pl.when(jnp.logical_not(here))
        def _():
            remote(v.oq.at[i], dst.at[g], v.s_out.at[i, 0], v.s_out.at[i, 1 + g], (layer, own_b, t)).wait_send()

        @pl.when(s == layer)
        def _():
            def got(m):
                remote(v.oq.at[i], dst.at[m], v.s_out.at[i, 0], v.s_out.at[i, 1 + m], me_x).wait_recv()

            got(1 - g)

            @pl.when(g != s)
            def _():
                got(g)

    def grad_of(layer, key, left, right):
        first, n = shares(key, ff)[:2]
        for i in range(dim // 256):
            lo = i * 256
            v.gr[layer, lo : lo + 256, first : first + n] = tn(left[:, lo : lo + 256], right).astype(BF)

    def buf(name, layer, key):
        return b_[f"{name}{layer}{key}"]

    def swaps(layer, key):
        return MODES[layer, key] == "swap"

    def all_cols(key):
        return pl.ds(*shares(key, ff)[:2])

    def share_cols(key, e):
        first, _, stride, n = shares(key, ff)
        return pl.ds(pl.multiple_of(first + e * stride, 128), n)

    def slice_rows(k, d=0):
        return pl.multiple_of(((zi + d) % half + half * k) * part, 16)

    def swap_copy(layer, key):
        sem = buf("s_x", layer, key)
        return remote(
            v.gr.at[layer, :, share_cols(key, 1 - s)], buf("xr", layer, key), sem.at[0], sem.at[1], me_x
        )

    def run_copy(layer, key, d, k):
        sem, rs = buf("s_a", layer, key), pl.ds(slice_rows(k, d), part)
        if swaps(layer, key):
            src = buf("xr", layer, key).at[rs]
        else:
            src = v.gr.at[layer, rs, all_cols(key)]
        return remote(src, buf("ar", layer, key).at[d - 1, k], sem.at[0, d, k], sem.at[1, d, k], zpeer(d))

    def run_copies(layer, key):
        return [run_copy(layer, key, d, k) for d in range(1, half) for k in range(2)]

    def cross_copy(layer, key):
        sem = buf("s_b", layer, key)
        return remote(buf("bs", layer, key), buf("br", layer, key), sem.at[0], sem.at[1], me_x)

    def last_copy(layer, key):
        sem = buf("s_c", layer, key)
        return remote(buf("cs", layer, key), buf("cr", layer, key), sem.at[0], sem.at[1], me_o)

    def home_copy(layer, key):
        sem = buf("s_e", layer, key)
        return remote(buf("es", layer, key), buf("er", layer, key), sem.at[0], sem.at[1], me_x)

    def run_sum(layer, key, k, rs):
        own = pl.ds(pl.multiple_of(slice_rows(k) + rs.start, 16), RB)
        if swaps(layer, key):
            tot = buf("xr", layer, key)[own, :].astype(F32)
        else:
            tot = v.gr[layer, own, all_cols(key)].astype(F32)
        for d in range(1, half):
            tot = tot + buf("ar", layer, key)[d - 1, k, rs, :].astype(F32)
        return tot

    def out_of(key, e=0):
        _, n, stride, m = shares(key, ff)
        return dict(d=o_d, u=o_u, o=o_o, q=o_q)[key], e * stride

    def give(layer, key):
        if swaps(layer, key):
            swap_copy(layer, key).start()
        else:
            for cp in run_copies(layer, key):
                cp.start()

    def second(layer, key):
        if swaps(layer, key):
            swap_copy(layer, key).wait_recv()
            xr = buf("xr", layer, key)

            def body(rs):
                xr[rs, :] = (v.gr[layer, rs, share_cols(key, s)].astype(F32) + xr[rs, :].astype(F32)).astype(BF)

            row_loop(body, dim)
            for cp in run_copies(layer, key):
                cp.start()
            return

        for cp in run_copies(layer, key):
            cp.wait_recv()

        @pl.when(s != layer)
        def _():
            for k in range(2):

                def body(rs, k=k):
                    buf("bs", layer, key)[k, rs, :] = run_sum(layer, key, k, rs).astype(BF)

                row_loop(body, part)
            cross_copy(layer, key).start()

    def third(layer, key):
        cs = buf("cs", layer, key)
        if swaps(layer, key):
            for cp in run_copies(layer, key):
                cp.wait_recv()

            def body(rs):
                cs[rs, :] = run_sum(layer, key, 1 - g, rs).astype(BF)

            row_loop(body, part)
            last_copy(layer, key).start()
            return

        @pl.when(s == layer)
        def _():
            cross_copy(layer, key).wait_recv()
            br = buf("br", layer, key)

            def body(rs):
                cs[rs, :] = (run_sum(layer, key, 1 - g, rs) + br[1 - g, rs, :].astype(F32)).astype(BF)

            row_loop(body, part)
            last_copy(layer, key).start()

    def fourth(layer, key):
        cr = buf("cr", layer, key)
        out, at = out_of(key, layer)

        @pl.when(s == layer)
        def _():
            last_copy(layer, key).wait_recv()

            def body(rs):
                tot = run_sum(layer, key, g, rs) + cr[rs, :].astype(F32)
                if swaps(layer, key):
                    out[rs, at : at + tot.shape[1]] = tot
                else:
                    out[rs, :] = tot + buf("br", layer, key)[g, rs, :].astype(F32)

            row_loop(body, part)

        if swaps(layer, key):

            @pl.when(s != layer)
            def _():
                last_copy(layer, key).wait_recv()

                def body(rs):
                    tot = run_sum(layer, key, g, rs) + cr[rs, :].astype(F32)
                    buf("es", layer, key)[rs, :] = tot.astype(BF)

                row_loop(body, part)
                home_copy(layer, key).start()

    def fifth(layer, key):
        if swaps(layer, key):
            out, at = out_of(key, 1 - layer)

            @pl.when(s == layer)
            def _():
                home_copy(layer, key).wait_recv()

                def body(rs):
                    got = buf("er", layer, key)[rs, :].astype(F32)
                    out[rs, at : at + got.shape[1]] = got

                row_loop(body, part)

    def grads_close():
        for (layer, key), mode in MODES.items():
            for cp in run_copies(layer, key):
                cp.wait_send()
            if mode == "swap":
                swap_copy(layer, key).wait_send()
                last_copy(layer, key).wait_send()

            @pl.when(s == layer)
            def _(layer=layer, key=key, mode=mode):
                if mode == "run":
                    last_copy(layer, key).wait_send()

            @pl.when(s != layer)
            def _(layer=layer, key=key, mode=mode):
                (home_copy if mode == "swap" else cross_copy)(layer, key).wait_send()

    def rows_of(buf, layer):
        x = buf[layer]
        return x.reshape(full, x.shape[-1])

    stages = (give, second, third, fourth, fifth)
    spots = {
        (1, 0): ("1 1du",),
        (1, 1): ("1 1o", "2 1du"),
        (1, 2): ("1 1q", "3 1d", "2 1o"),
        (0, 0): ("1 0d", "3 1u", "2 1q", "3 1o"),
        (0, 1): ("1 0uo", "4 1d", "2 0d", "3 1q", "4 1uo"),
        (0, 2): ("1 0q", "3 0d", "5 1d", "2 0u", "5 1o", "4 1q"),
        (0, 3): ("2 0o", "3 0u", "4 0d", "2 0q", "3 0o", "4 0u", "5 1q", "3 0q"),
        (0, 4): ("4 0o", "5 0u", "4 0q", "5 0oq"),
    }

    def serve(layer, spot):
        for line in spots.get((layer, spot), ()):
            for key in line[3:]:
                stages[int(line[0]) - 1](int(line[2]), key)

    def back_rows(layer, j, u_buf, r_buf, gain, base, at, extra=None):
        v.stt[...] = jnp.zeros(v.stt.shape, F32)

        def body(rs):
            gsec = sum_rows(j, rs)
            u, r = u_buf[layer, rs, :], r_buf[layer, rs, :]
            gg = gsec * gain
            res = r * (
                gg - jnp.mean(gg, axis=-1, keepdims=True) - u * jnp.mean(gg * u, axis=-1, keepdims=True)
            )
            inn = base[rs, :]
            out = inn + res
            at(rs, out)
            v.stt[0] += gsec * u
            v.stt[1] += gsec
            v.stt[2] += out
            v.stt[3] += inn

        row_loop(body)

    def backward_begin(layer):
        def d_second(hf):
            dgel = nt(v.dyb[layer, hf], v.wdb[layer])
            v.du[hf] = (dgel * v.gp[layer, hf]).astype(BF)
            return nt(v.du[hf], v.wub[layer])

        sum_begin(4 + 2 * (1 - layer), d_second)

    def backward(layer):
        j = 4 + 2 * (1 - layer)
        grad_of(layer, "d", rows_of(v.dyb, layer), rows_of(v.gl, layer))
        grad_of(layer, "u", rows_of(v.sb, layer), v.du[...].reshape(full, ff))
        ones = jnp.ones((8, full), BF)
        v.smo[layer, 6:7, :] = nn(ones, v.du[...].reshape(full, ff))[0:1]
        serve(layer, 0)
        sum_end(j)

        def at_two(rs, out):
            v.dhf[rs, :] = out
            v.dhb[layer, c, rs, :] = out.astype(BF)

        back_rows(layer, j, v.u2, v.r2, prow(layer, 1), v.dyf, at_two)
        share(v.dhb, layer, 4 + layer)
        for i, row in ((0, 1), (1, 3), (2, 4), (3, 5)):
            v.smo[layer, row : row + 1, :] = jnp.sum(v.stt[i], axis=0, keepdims=True)

        def d_att(hf):
            rs = pl.ds(pl.multiple_of(hf * two, 16), two)
            v.dgo[layer, rs, :] = nt(v.dhb[layer, hf], v.wob[layer]).astype(BF)

        d_att(c)
        share_wait(v.dhb, layer, 4 + layer)
        d_att(1 - c)
        dat = v.dgo[layer].astype(F32)
        prod = dat * v.attf[layer]
        tile = dat[:, 0:128]
        for h in range(3):
            real = (lane_f >= 64 * h + 64) & (lane_f < 64 * h + 128)
            delta = jnp.sum(jnp.where(real, prod, 0.0), axis=1, keepdims=True)
            for i, piece in enumerate(splits(-delta)):
                tile = jnp.where(lane == 3 * h + i, piece, tile)
        v.dgo[layer, :, 0:128] = tile.astype(BF)
        group_send(v.dgo.at[layer], v.dg.at[layer, own_b], v.s_ds.at[layer], v.s_dr.at[layer])
        grad_of(layer, "o", rows_of(v.dhb, layer), rows_of(v.attb, layer))
        serve(layer, 1)

        put_masked(v.ma, v.qa[layer], k_mask)
        put_masked(v.mb, v.dgo[layer], v_mask)
        v.dqs[...] = jnp.zeros(v.dqs.shape, F32)

        def query_block(bk, carry):
            build_kv(layer, bk)
            kt, vt = v.kt[...], v.vt[...]
            terms = []
            for h in range(3):
                p = jnp.exp(nt(v.ma[h], kt))
                ds = (p * nt(v.mb[h], vt)).astype(BF)
                terms.append(nn(ds, kt))
            v.dqs[...] += by_head_k(terms)
            return carry

        lax.fori_loop(0, nd, query_block, 0)

        build_kv(layer, own_b)
        put_masked(v.ma, v.kt[...], k_mask)
        put_masked(v.mb, v.vt[...], v_mask)
        v.dks[...] = jnp.zeros(v.dks.shape, F32)
        v.dvs[...] = jnp.zeros(v.dvs.shape, F32)

        def key_block(k, carry):
            zk, sk = (zi + k % half) % half, (s + k // half) % 2
            bk = zk + half * sk
            q_at, d_at = v.qg.at[layer, bk], v.dg.at[layer, bk]
            remote(q_at, q_at, v.s_qs.at[layer, 0], v.s_qr.at[layer, bk], me_x).wait_recv()
            remote(d_at, d_at, v.s_ds.at[layer, 0], v.s_dr.at[layer, bk], me_x).wait_recv()
            if big:
                cps = (
                    pltpu.make_async_copy(q_at, v.kt, v.s_loc.at[0]),
                    pltpu.make_async_copy(d_at, v.vt, v.s_loc.at[1]),
                )
                for cp in cps:
                    cp.start()
                for cp in cps:
                    cp.wait()
                key_terms(v.kt[...], v.vt[...])
            else:
                key_terms(q_at[...], d_at[...])
            return carry

        def key_terms(qt, dt):
            tk, tv = [], []
            for h in range(3):
                p = jnp.exp(nt(v.ma[h], qt))
                ds = (p * nt(v.mb[h], dt)).astype(BF)
                tv.append(nn(p.astype(BF), dt))
                tk.append(nn(ds, qt))
            v.dks[...] += by_head_k(tk)
            v.dvs[...] += by_head_v(tv)

        key_terms(v.qa[layer], v.dgo[layer])
        lax.fori_loop(1, nd, key_block, 0)

        for i in range(2):
            rs = slice(i * two, (i + 1) * two)
            v.gm[i, :, 0:128] = (v.dqs[rs, 0:128] * 0.125).astype(BF)
            v.gm[i, :, 128:256] = jnp.where(lane[rs] < 64, v.dqs[rs, 128:256] * 0.125, 0.0).astype(BF)
            v.gm[i, :, 256:384] = v.dks[rs, 0:128].astype(BF)
            v.gm[i, :, 384:512] = jnp.where(lane[rs] < 64, v.dks[rs, 128:256], v.dvs[rs, 0:128]).astype(BF)
            v.gm[i, :, 512:640] = v.dvs[rs, 128:256].astype(BF)
        sum_begin(j + 1, lambda hf: nn(v.gm[hf], v.wqb[layer]))
        grad_of(layer, "q", rows_of(v.nb, layer), v.gm[...].reshape(full, 640))
        v.smo[layer, 7:8, :] = jnp.zeros((1, dim), F32)
        v.smo[layer, 7:8, 0:640] = nn(ones, v.gm[...].reshape(full, 640))[0:1]
        serve(layer, 2)
        sum_end(j + 1)

        def at_one(rs, out):
            low = out.astype(BF)
            v.dyf[rs, :] = low.astype(F32)
            if layer == 1:
                v.dyb[0, c, rs, :] = low

        back_rows(layer, j + 1, v.u1, v.r1, prow(layer, 0), v.dhf, at_one)
        for i, row in ((0, 0), (1, 2)):
            v.smo[layer, row : row + 1, :] = jnp.sum(v.stt[i], axis=0, keepdims=True)
        if layer == 1:
            share(v.dyb, 0, 7)
        put_out(2 + layer, layer, v.dyf, igs)

    norm_one(0)
    forward(0)
    forward_end(0)
    red(og, v.gq, 1)
    forward(1)
    red_wait(og, v.gq, 1)
    send(v.gq.at[0], v.gq.at[1], v.s_xy.at[2], v.s_xy.at[3], me_y)
    v.dyf[q_own, :] = v.gq[0].astype(F32)
    remote(v.gq.at[0], v.gq.at[1], v.s_xy.at[2], v.s_xy.at[3], me_y).wait_recv()
    v.dyf[q_oth, :] = v.gq[1].astype(F32)
    v.dyb[1, c] = v.dyf[...].astype(BF)
    share(v.dyb, 1, 6)
    share_wait(v.dyb, 1, 6)
    backward_begin(1)
    forward_end(1)
    backward(1)
    share_wait(v.dyb, 0, 7)
    backward_begin(0)
    backward(0)

    send(v.smo, v.smc, v.s_sm.at[0], v.s_sm.at[1], me_c)
    remote(v.smo, v.smc, v.s_sm.at[0], v.s_sm.at[1], me_c).wait_recv()
    rowid = lax.broadcasted_iota(jnp.int32, (8, dim), 0)
    for layer in range(2):
        v.smc[layer] = v.smo[layer] + jnp.where(rowid < 6, v.smc[layer], 0.0)
    for k in range(1, 2 * nd):
        other = (s * nd + z + k) % (2 * nd)
        so = other // nd
        send(v.smc.at[so], v.smr.at[k - 1], v.s_sms.at[k - 1], v.s_smr.at[k - 1], (so, other % nd, t))
    serve(0, 3)
    for k in range(1, 2 * nd):
        remote(v.smr.at[0], v.smr.at[k - 1], v.s_sms.at[k - 1], v.s_smr.at[k - 1], me_x).wait_recv()
    tot = v.smc[s]
    for k in range(1, 2 * nd):
        tot = tot + v.smr[k - 1]
    o_s[...] = tot
    serve(0, 4)

    for cp in late:
        cp.wait_send()

    grads_close()
    for i, src, dst in ((0, fr, v.xq), (1, og, v.gq)):

        @pl.when(keeps)
        def _(i=i, src=src, dst=dst):
            remote(src.at[1 - g], dst.at[0], v.s_red.at[i], v.s_red.at[2 + i], me_o).wait_send()

    for i in range(4):
        forward_w_end(i)
    put_out_wait(0, 0, acts)
    put_out_wait(1, 1, acts)
    put_out_wait(2, 0, igs)
    put_out_wait(3, 1, igs)


def local(frames, out_grad, clip_ids, w_qkv, bias_qv, w_out, w_up, bias_up, w_down, ln_gain, shifts):
    rows, dim = frames.shape[1:]
    nd = lax.axis_size("dp")
    half = nd // 2
    z, t, s = lax.axis_index("dp"), lax.axis_index("tensor"), lax.axis_index("section")
    hl = w_qkv.shape[3]
    ff = w_up.shape[2]
    part = dim // nd
    wide = w_qkv[0].transpose(1, 2, 0).reshape(3 * hl, dim)
    zeros = functools.partial(jnp.zeros, dtype=F32)
    params = jnp.concatenate(
        [
            ln_gain[0].astype(F32),
            shifts[0].astype(F32),
            bias_up.astype(F32),
            jnp.pad(bias_qv[0, 0].astype(F32), (0, dim - hl))[None],
            jnp.pad(bias_qv[0, 1].astype(F32), (hl, dim - 2 * hl))[None],
            zeros((7, dim)),
        ]
    )
    clip = lax.dynamic_index_in_dim(clip_ids, z // half, 0, keepdims=False)
    clip = clip.reshape(nd, 4, rows)
    clip = jnp.stack([clip[:, 0], clip[:, 2], clip[:, 1], clip[:, 3]], axis=1).reshape(nd, 4 * rows)
    lane = jnp.arange(128)
    same = clip[:, :, None] == (lane - 80)[None, None, :]
    spot = lane >= 80
    k_feat = jnp.where(
        (lane >= 64) & (lane < 73), 1.0, jnp.where(spot & jnp.logical_not(same), -BIG, 0.0)
    ).astype(BF)
    own_b = z % half + half * s
    q_feat = jnp.where(spot & lax.dynamic_index_in_dim(same, own_b, 0, keepdims=False), 1.0, 0.0).astype(BF)

    plan = scratch_plan(nd, rows, dim, hl, ff)
    shape = jax.ShapeDtypeStruct
    anyspec = pl.BlockSpec(memory_space=pl.ANY)
    vspec = pl.BlockSpec(memory_space=pltpu.VMEM)
    gathered = {name: (2, nd, 4 * rows, 256) for name in ("qg", "dg")}
    big = nd > MOST
    if not big:
        plan.update({name: pltpu.VMEM(dims, BF) for name, dims in gathered.items()})
    outs = pl.pallas_call(
        functools.partial(mega, nd, (*gathered, *plan) if big else tuple(plan)),
        out_shape=(
            shape((2, rows, dim), BF),
            shape((2, rows, dim), BF),
            shape((part, 640), F32),
            shape((part, ff), F32),
            shape((part, 256), F32),
            shape((part, ff), F32),
            shape((8, dim), F32),
        )
        + tuple(shape(dims, BF) for dims in gathered.values()) * big,
        in_specs=[anyspec] * 7 + [vspec] * 2,
        out_specs=(anyspec,) * 2 + (vspec,) * 5 + (anyspec,) * (2 * big),
        scratch_shapes=list(plan.values()),
        compiler_params=pltpu.CompilerParams(
            collective_id=0, has_side_effects=True, vmem_limit_bytes=63 * 1024 * 1024
        ),
    )(frames, out_grad, wide, w_out[0], w_up[0], w_down[0], params, k_feat, q_feat)

    acts, igs, g_q, g_u, g_o, g_d, small = outs[:7]
    g_qkv = jnp.stack([g_q[:, 0:hl], g_q[:, 256 : 256 + hl], g_q[:, 256 + hl : 256 + 2 * hl]], axis=1)
    bias = small[7]
    bias = jnp.stack([bias[0:hl], bias[256 + hl : 256 + 2 * hl]]).reshape(2, hl // HD, HD)
    bias = lax.dynamic_slice_in_dim(bias, z * (HD // nd), HD // nd, 2)
    upb = small[6].reshape(hl // HD, ff // (hl // HD))
    upb = lax.dynamic_slice_in_dim(upb, z * (upb.shape[1] // nd), upb.shape[1] // nd, 1)
    own = dim // (4 * nd)
    norms = lax.dynamic_slice_in_dim(small, (z * 4 + t) * own, own, 1)
    return (
        acts[None],
        igs[None],
        g_qkv[None],
        bias[None],
        g_o[:, 64 : 64 + hl].T[None],
        g_u[None],
        upb[None],
        g_d.T[None],
        norms[None, 0:2],
        norms[None, 2:6],
    )


def solution(mesh):
    in_specs = (
        P(None, ("dp", "tensor"), None),
        P(None, ("dp", "tensor"), None),
        P(),
        P("section", None, None, "tensor"),
        P("section", None, "tensor"),
        P("section", "tensor", None),
        P("section", None, "tensor"),
        P("section", "tensor"),
        P("section", "tensor", None),
        P("section", None, None),
        P("section", None, None),
    )
    out_specs = (
        P("section", None, ("dp", "tensor"), None),
        P("section", None, ("dp", "tensor"), None),
        P("section", "dp", None, "tensor"),
        P("section", None, "tensor", "dp"),
        P("section", "tensor", "dp"),
        P("section", "dp", "tensor"),
        P("section", "tensor", "dp"),
        P("section", "tensor", "dp"),
        P("section", None, ("dp", "tensor")),
        P("section", None, ("dp", "tensor")),
    )
    return jax.shard_map(local, mesh=mesh, in_specs=in_specs, out_specs=out_specs, check_vma=False)
```

```python
import functools

import jax
import jax.numpy as jnp
from jax import lax
from jax.experimental import pallas as pl
from jax.experimental.pallas import tpu as pltpu
from jax.sharding import PartitionSpec as P

HD = 64
BIG = 2.0**100
MESH = pl.DeviceIdType.MESH
BF = jnp.bfloat16
F32 = jnp.float32
RB = 16
SLOTS = 4
MOST = 4


def nt(a, b):
    return lax.dot_general(a, b, (((1,), (1,)), ((), ())), preferred_element_type=F32)


def nn(a, b):
    return lax.dot_general(a, b, (((1,), (0,)), ((), ())), preferred_element_type=F32)


def tn(a, b):
    return lax.dot_general(a, b, (((0,), (0,)), ((), ())), preferred_element_type=F32)


def shares(key, ff):
    return {
        "d": (0, ff, ff // 2, ff // 2),
        "u": (ff, ff, ff // 2, ff // 2),
        "o": (2 * ff, 256, 128, 128),
        "q": (2 * ff + 256, 256, 128, 128),
        "k": (2 * ff + 512, 384, 0, 0),
    }[key]


MODES = {
    (1, "d"): "swap",
    (1, "u"): "run",
    (1, "o"): "swap",
    (1, "q"): "run",
    (1, "k"): "run",
    (0, "d"): "run",
    (0, "u"): "swap",
    (0, "o"): "swap",
    (0, "q"): "run",
    (0, "k"): "run",
}


def scratch_plan(nd, rows, dim, head_dim, ff):
    half = nd // 2
    full = 4 * rows
    two = 2 * rows
    part = dim // nd
    wide = 640 + ff + 256 + ff
    vm = pltpu.VMEM
    dma = pltpu.SemaphoreType.DMA
    plan = dict(
        wqb=vm((2, 640, dim), BF),
        wob=vm((2, 256, dim), BF),
        wub=vm((2, dim, ff), BF),
        wdb=vm((2, ff, dim), BF),
        spb=vm((2, 16, dim), F32),
        xq=vm((2, rows, dim), BF),
        gq=vm((2, rows, dim), BF),
        xres=vm((two, dim), F32),
        dyf=vm((two, dim), F32),
        dyb=vm((2, 2, two, dim), BF),
        nb=vm((2, 2, two, dim), BF),
        sb=vm((2, 2, two, dim), BF),
        hid=vm((two, dim), F32),
        u1=vm((2, two, dim), F32),
        u2=vm((2, two, dim), F32),
        r1=vm((2, two, 1), F32),
        r2=vm((2, two, 1), F32),
        qa=vm((2, full, 256), BF),
        kvb=vm((2, nd, full, 384), BF),
        kt=vm((full, 256), BF),
        vt=vm((full, 256), BF),
        dgo=vm((2, full, 256), BF),
        mst=vm((3, full, 1), F32),
        lst=vm((3, full, 1), F32),
        attf=vm((2, full, 256), F32),
        attb=vm((2, 2, two, 256), BF),
        gl=vm((2, 2, two, ff), BF),
        gp=vm((2, 2, two, ff), F32),
        du=vm((2, two, ff), BF),
        dhb=vm((2, 2, two, dim), BF),
        dhf=vm((two, dim), F32),
        gm=vm((2, two, 640), BF),
        ma=vm((3, full, 256), BF),
        mb=vm((3, full, 256), BF),
        dqs=vm((full, 256), F32),
        dks=vm((full, 256), F32),
        dvs=vm((full, 256), F32),
        cs=vm((two, dim), BF),
        cr=vm((SLOTS, two, dim), BF),
        ys=vm((2, two, dim), BF),
        yr=vm((SLOTS, two, dim), BF),
        chip=vm((2, two, dim), F32),
        gr=vm((2, dim, wide), BF),
        smo=vm((2, 8, dim), F32),
        smc=vm((2, 8, dim), F32),
        smr=vm((2 * nd - 1, 8, dim), F32),
        stt=vm((6, RB, dim), F32),
        oq=vm((4, rows, dim), BF),
        s_loc=dma((12,)),
        s_red=dma((4,)),
        s_xy=dma((4,)),
        s_wx=dma((2, 9)),
        s_wzs=dma((8, half)),
        s_wzr=dma((8, half)),
        s_ag=dma((2, 8)),
        s_cc=dma((2, SLOTS)),
        s_yy=dma((2, SLOTS)),
        s_kvs=dma((2, nd)),
        s_kvr=dma((2, nd)),
        s_qs=dma((2, nd)),
        s_qr=dma((2, nd)),
        s_ds=dma((2, nd)),
        s_dr=dma((2, nd)),
        s_sm=dma((2,)),
        s_sms=dma((2 * nd - 1,)),
        s_smr=dma((2 * nd - 1,)),
        s_out=dma((4, 3)),
    )
    for (layer, key), mode in MODES.items():
        n = shares(key, ff)[1 if mode == "run" else 3]
        tag = f"{layer}{key}"
        if mode == "swap":
            plan["xr" + tag] = vm((dim, n), BF)
            plan["s_x" + tag] = dma((2,))
        else:
            plan["bs" + tag] = vm((2, part, n), BF)
            plan["br" + tag] = vm((2, part, n), BF)
            plan["s_b" + tag] = dma((2,))
        plan["ar" + tag] = vm((half - 1, 2, part, n), BF)
        plan["s_a" + tag] = dma((2, half, 2))
        plan["cs" + tag] = vm((part, n), BF)
        plan["cr" + tag] = vm((part, n), BF)
        plan["s_c" + tag] = dma((2,))
        if mode == "swap":
            plan["es" + tag] = vm((part, n), BF)
            plan["er" + tag] = vm((part, n), BF)
            plan["s_e" + tag] = dma((2,))
    return plan


def mega(nd, names, *refs):
    (fr, og, wq, wo, wu, wd, gains, moves, bup, bqv, kf) = refs[:11]
    (acts, igs, o_q, o_u, o_o, o_d, o_s) = refs[11:18]
    b_ = dict(zip(names, refs[18:]))
    big = nd > MOST

    class Bufs:
        pass

    v = Bufs()
    v.__dict__.update(b_)
    half = nd // 2
    rows, dim = fr.shape[1:]
    two, full = 2 * rows, 4 * rows
    ff = wu.shape[1]
    part = dim // nd
    s = lax.axis_index("section")
    z = lax.axis_index("dp")
    t = lax.axis_index("tensor")
    g, zi = z // half, z % half
    c, y = t % 2, t // 2
    own_b = zi + half * s
    zo = (z + half) % nd
    me_x = (1 - s, z, t)
    me_c = (s, z, t + 1 - 2 * c)
    me_y = (s, z, (t + 2) % 4)
    me_o = (s, zo, t)

    def zpeer(d):
        return (s, g * half + (zi + d) % half, t)

    def member(k):
        zk, sk = (zi + k % half) % half, (s + k // half) % 2
        return (sk, g * half + zk, t), zk + half * sk

    def remote(src, dst, ss, rs, dev):
        return pltpu.make_async_remote_copy(
            src_ref=src, dst_ref=dst, send_sem=ss, recv_sem=rs, device_id=dev, device_id_type=MESH
        )

    late = []

    def send(src, dst, ss, rs, dev):
        cp = remote(src, dst, ss, rs, dev)
        cp.start()
        late.append(cp)
        return cp

    loads = [
        pltpu.make_async_copy(wq.at[pl.ds(0, 192)], v.wqb.at[s, pl.ds(0, 192)], v.s_loc.at[0]),
        pltpu.make_async_copy(wq.at[pl.ds(192, 384)], v.wqb.at[s, pl.ds(256, 384)], v.s_loc.at[1]),
        pltpu.make_async_copy(wo, v.wob.at[s, pl.ds(64, 192)], v.s_loc.at[2]),
        pltpu.make_async_copy(wu, v.wub.at[s], v.s_loc.at[3]),
        pltpu.make_async_copy(wd, v.wdb.at[s], v.s_loc.at[4]),
    ]
    for cp in loads:
        cp.start()
    v.wqb[s, pl.ds(192, 64), :] = jnp.zeros((64, dim), BF)
    v.wob[s, pl.ds(0, 64), :] = jnp.zeros((64, dim), BF)
    hl = bqv.shape[1]
    v.spb[s, 0:2, :] = gains[...].astype(F32)
    v.spb[s, 2:6, :] = moves[...].astype(F32)
    v.spb[s, 6:7, :] = bup[...].astype(F32)
    v.spb[s, 7:16, :] = jnp.zeros((9, dim), F32)
    v.spb[s, 7:9, 0:hl] = bqv[...].astype(F32)
    v.spb[s, 8:16, :] = pltpu.roll(v.spb[s, 8:16, :], hl, 1)

    barrier = pltpu.get_barrier_semaphore()
    for k in range(1, 2 * nd):
        other = (s * nd + z + k) % (2 * nd)
        pl.semaphore_signal(barrier, inc=1, device_id=(other // nd, other % nd, t), device_id_type=MESH)
    for dev in (me_c, me_y):
        pl.semaphore_signal(barrier, inc=1, device_id=dev, device_id_type=MESH)
    pl.semaphore_wait(barrier, 2 * nd + 1)

    keeps = g == s

    def red(src, dst, i):
        @pl.when(keeps)
        def _():
            pltpu.make_async_copy(src.at[g], dst.at[0], v.s_loc.at[6 + i]).start()
            remote(src.at[1 - g], dst.at[0], v.s_red.at[i], v.s_red.at[2 + i], me_o).start()

    def red_wait(src, dst, i):
        @pl.when(keeps)
        def _():
            pltpu.make_async_copy(src.at[g], dst.at[0], v.s_loc.at[6 + i]).wait()

        @pl.when(jnp.logical_not(keeps))
        def _():
            remote(src.at[1 - g], dst.at[0], v.s_red.at[i], v.s_red.at[2 + i], me_o).wait_recv()

    red(fr, v.xq, 0)
    for cp in loads[:2]:
        cp.wait()
    mats = (v.wqb, v.wob, v.wub, v.wdb)

    def w_parts(i):
        return 2 if mats[i].shape[1] // half % 32 == 0 else 1

    def w_rows(i, p, e):
        n = mats[i].shape[1] // half
        m = n // w_parts(i)
        return pl.ds(pl.multiple_of(p * n + e * m, 16), m)

    def ship(i):
        for e in range(w_parts(i)):
            src = mats[i].at[s, w_rows(i, zi, e)]
            send(src, src, v.s_wx.at[0, 2 * i + e], v.s_wx.at[1, 2 * i + e], me_x)

    send(v.spb.at[s], v.spb.at[s], v.s_wx.at[0, 8], v.s_wx.at[1, 8], me_x)
    ship(0)
    loads[2].wait()
    ship(1)
    loads[3].wait()
    ship(2)
    loads[4].wait()

    def w_copy(i, e, d, back=0):
        src = mats[i].at[1 - s, w_rows(i, (zi + back) % half, e)]
        return remote(src, src, v.s_wzs.at[2 * i + e, d], v.s_wzr.at[2 * i + e, d], zpeer(d))

    def forward_w(i, e=None):
        for e in range(w_parts(i)) if e is None else (e,):
            if e < w_parts(i):
                src = mats[i].at[1 - s, w_rows(i, zi, e)]
                remote(src, src, v.s_wx.at[0, 2 * i + e], v.s_wx.at[1, 2 * i + e], me_x).wait_recv()
                for d in range(1, half):
                    w_copy(i, e, d).start()

    def forward_w_end(i):
        for e in range(w_parts(i)):
            for d in range(1, half):
                w_copy(i, e, d).wait_send()

    def gather_w(i, layer):
        @pl.when(s != layer)
        def _():
            for e in range(w_parts(i)):
                for d in range(1, half):
                    w_copy(i, e, d, half - d).wait_recv()

    red_wait(fr, v.xq, 0)
    send(v.xq.at[0], v.xq.at[1], v.s_xy.at[0], v.s_xy.at[1], me_y)
    remote(v.spb.at[s], v.spb.at[s], v.s_wx.at[0, 8], v.s_wx.at[1, 8], me_x).wait_recv()
    q_own = pl.ds(pl.multiple_of(rows * y, 8), rows)
    q_oth = pl.ds(pl.multiple_of(rows * (1 - y), 8), rows)
    v.xres[q_own, :] = v.xq[0].astype(F32)
    forward_w(0, 0)
    remote(v.xq.at[0], v.xq.at[1], v.s_xy.at[0], v.s_xy.at[1], me_y).wait_recv()
    v.xres[q_oth, :] = v.xq[1].astype(F32)

    def prow(layer, i):
        return v.spb[layer, i : i + 1, :]

    def row_loop(fn, n=two):
        def step(i, carry):
            fn(pl.ds(pl.multiple_of(i * RB, RB), RB))
            return carry

        lax.fori_loop(0, n // RB, step, 0, unroll=n // RB if n == two else 4)

    def unit(x):
        cen = x - jnp.mean(x, axis=-1, keepdims=True)
        r = lax.rsqrt(jnp.mean(cen * cen, axis=-1, keepdims=True) + 1e-05)
        return cen * r, r

    def share(buf, layer, i):
        src = buf.at[layer, c]
        send(src, src, v.s_ag.at[0, i], v.s_ag.at[1, i], me_c)

    def share_wait(buf, layer, i):
        src = buf.at[layer, 1 - c]
        remote(src, src, v.s_ag.at[0, i], v.s_ag.at[1, i], me_c).wait_recv()

    def norm_one(layer):
        gain, shift = prow(layer, 0), prow(layer, 2)

        def body(rs):
            u, r = unit(v.xres[rs, :])
            v.u1[layer, rs, :] = u
            v.r1[layer, rs, :] = r
            v.nb[layer, c, rs, :] = (u * gain + shift).astype(BF)

        row_loop(body)
        share(v.nb, layer, layer)

    def sum_begin(j, term):
        k = j % SLOTS
        v.cs[...] = term(1 - c).astype(BF)
        cp = remote(v.cs, v.cr.at[k], v.s_cc.at[0, k], v.s_cc.at[1, k], me_c)
        cp.start()
        v.chip[j % 2] = term(c)
        cp.wait()

        def body(rs):
            tot = v.chip[j % 2, rs, :] + v.cr[k, rs, :].astype(F32)
            v.chip[j % 2, rs, :] = tot
            v.ys[j % 2, rs, :] = tot.astype(BF)

        row_loop(body)
        remote(v.ys.at[j % 2], v.yr.at[k], v.s_yy.at[0, k], v.s_yy.at[1, k], me_y).start()

    def sum_end(j):
        k = j % SLOTS
        remote(v.ys.at[j % 2], v.yr.at[k], v.s_yy.at[0, k], v.s_yy.at[1, k], me_y).wait()

    def sum_rows(j, rs):
        k = j % SLOTS
        return v.chip[j % 2, rs, :] + v.yr[k, rs, :].astype(F32)

    lane_f = lax.broadcasted_iota(jnp.int32, (full, 256), 1)
    lane = lax.broadcasted_iota(jnp.int32, (full, 128), 1)

    def k_mask(h):
        return (
            ((lane_f >= 64 * h) & (lane_f < 64 * h + 64))
            | ((lane_f >= 192 + 3 * h) & (lane_f < 195 + 3 * h))
            | (lane_f >= 208)
        )

    def v_mask(h):
        return ((lane_f >= 64 * h + 64) & (lane_f < 64 * h + 128)) | (
            (lane_f >= 3 * h) & (lane_f < 3 * h + 3)
        )

    def by_head_k(a):
        return jnp.where(lane_f < 64, a[0], jnp.where(lane_f < 128, a[1], a[2]))

    def by_head_v(a):
        return jnp.where(lane_f < 128, a[0], jnp.where(lane_f < 192, a[1], a[2]))

    def put_masked(dst, val, mask):
        val = val.astype(F32)
        for h in range(3):
            dst[h] = jnp.where(mask(h), val, 0.0).astype(BF)

    def build_kv(layer, bk):
        v.kt[:, 0:128] = v.kvb[layer, bk, :, 0:128]
        mid = v.kvb[layer, bk, :, 128:256].astype(F32)
        v.kt[:, 128:256] = jnp.where(lane < 64, mid, kf[bk].astype(F32)).astype(BF)
        v.vt[:, 0:128] = jnp.where(lane < 64, jnp.where(lane < 9, 1.0, 0.0), mid).astype(BF)
        v.vt[:, 128:256] = v.kvb[layer, bk, :, 256:384]

    def splits(x):
        hi = x.astype(BF).astype(F32)
        mid = (x - hi).astype(BF).astype(F32)
        return hi, mid, (x - hi) - mid

    def group_send(src, dst, ss, rs):
        for k in range(1, nd):
            dev, _ = member(k)
            send(src, dst, ss.at[k], rs.at[own_b], dev)

    def group_wait(buf, layer, rs, k, ss):
        dev, bk = member(k)
        dst = buf.at[layer, bk]
        remote(dst, dst, ss.at[0], rs.at[bk], dev).wait_recv()

    halves = (lambda i: c, lambda i: 1 - c)

    def forward(layer):
        bias_q, bias_kv = v.spb[layer, 7:8, 0:256], v.spb[layer, 8:9, 0:384]

        def qkv(hf):
            r = nt(v.nb[layer, hf], v.wqb[layer])
            rs = pl.ds(pl.multiple_of(hf * two, 16), two)
            q = (r[:, 0:256] + bias_q).astype(BF).astype(F32) * 0.125
            v.qa[layer, rs, 0:128] = q[:, 0:128].astype(BF)
            clip = kf[own_b, rs, :].astype(F32) * (1.0 / BIG) + 1.0
            clip = jnp.where(lane[0:two] >= 80, clip, 0.0)
            v.qa[layer, rs, 128:256] = (q[:, 128:256] + clip).astype(BF)
            v.kvb[layer, own_b, rs, :] = (r[:, 256:640] + bias_kv).astype(BF)

        if layer == 0:
            forward_w(0, 1)
        gather_w(0, layer)
        qkv(c)
        share_wait(v.nb, layer, layer)
        qkv(1 - c)
        group_send(v.kvb.at[layer, own_b], v.kvb.at[layer, own_b], v.s_kvs.at[layer], v.s_kvr.at[layer])

        put_masked(v.ma, v.qa[layer], k_mask)
        v.mst[...] = jnp.full(v.mst.shape, -3e38, F32)
        v.lst[...] = jnp.zeros(v.lst.shape, F32)
        v.dqs[...] = jnp.zeros(v.dqs.shape, F32)

        def block(k, carry):
            zk, sk = (zi + k % half) % half, (s + k // half) % 2
            bk = zk + half * sk

            @pl.when(k > 0)
            def _():
                dst = v.kvb.at[layer, bk]
                remote(dst, dst, v.s_kvs.at[layer, 0], v.s_kvr.at[layer, bk], me_x).wait_recv()

            if layer == 0:
                for i in (1, 2):

                    @pl.when(k == i)
                    def _(i=i):
                        forward_w(i)

            build_kv(layer, bk)
            kt, vt = v.kt[...], v.vt[...]
            alphas, news = [], []
            for h in range(3):
                sc = nt(v.ma[h], kt)
                old = v.mst[h]
                new = jnp.maximum(old, jnp.max(sc, axis=1, keepdims=True))
                alpha = jnp.exp(old - new)
                p = jnp.exp(sc - new)
                v.mst[h] = new
                v.lst[h] = v.lst[h] * alpha + jnp.sum(p, axis=1, keepdims=True)
                hi = p.astype(BF)
                lo = (p - hi.astype(F32)).astype(BF)
                news.append(nn(hi, vt) + nn(lo, vt))
                alphas.append(alpha)
            v.dqs[...] = v.dqs[...] * by_head_v(alphas) + by_head_v(news)
            return carry

        block(0, 0)
        if layer == 0:
            ship(3)
        lax.fori_loop(1, nd, block, 0)

        att = v.dqs[...] * by_head_v([1.0 / v.lst[h] for h in range(3)])
        v.attf[layer] = att
        v.attb[layer] = att.astype(BF).reshape(2, two, 256)
        tile = v.qa[layer, :, 128:256].astype(F32)
        for h in range(3):
            for i, piece in enumerate(splits(-(v.mst[h] + jnp.log(v.lst[h])))):
                tile = jnp.where(lane == 64 + 3 * h + i, piece, tile)
        v.qa[layer, :, 128:256] = tile.astype(BF)
        gather_w(1, layer)
        sum_begin(2 * layer, lambda hf: nn(v.attb[layer, hf], v.wob[layer]))
        if layer == 1:
            for one in (1, 0):
                group_send(v.qa.at[one], v.qg.at[one, own_b], v.s_qs.at[one], v.s_qr.at[one])
        if layer == 0:
            forward_w(3, 0)
        sum_end(2 * layer)
        out_bias, gain2, shift2 = prow(layer, 4), prow(layer, 1), prow(layer, 3)

        def body(rs):
            hid = v.xres[rs, :] + sum_rows(2 * layer, rs) + out_bias
            v.hid[rs, :] = hid
            u, r = unit(hid)
            v.u2[layer, rs, :] = u
            v.r2[layer, rs, :] = r
            v.sb[layer, c, rs, :] = (u * gain2 + shift2).astype(BF)

        row_loop(body)
        share(v.sb, layer, 2 + layer)
        if layer == 0:
            forward_w(3, 1)
        gather_w(2, layer)
        bias_up = prow(layer, 6)

        def up(hf):
            v.gp[layer, hf] = nn(v.sb[layer, hf], v.wub[layer]) + bias_up

            def gelu(rs):
                u = v.gp[layer, hf, rs, :]
                phi = 0.5 * (1.0 + lax.erf(u * 0.7071067811865476))
                v.gl[layer, hf, rs, :] = (u * phi).astype(BF)
                v.gp[layer, hf, rs, :] = phi + u * (jnp.exp(-0.5 * u * u) * 0.3989422804014327)

            row_loop(gelu)

        up(c)
        share_wait(v.sb, layer, 2 + layer)
        up(1 - c)
        gather_w(3, layer)
        sum_begin(2 * layer + 1, lambda hf: nn(v.gl[layer, hf], v.wdb[layer]))

    def forward_end(layer):
        sum_end(2 * layer + 1)
        out_bias = prow(layer, 5)

        def body(rs):
            out = v.hid[rs, :] + sum_rows(2 * layer + 1, rs) + out_bias
            v.xres[rs, :] = out.astype(BF).astype(F32)

        row_loop(body)
        if layer == 0:
            norm_one(1)
        put_out(layer, layer, v.xres, acts)

    def put_out(i, layer, src, dst):
        v.oq[i] = src[q_own, :].astype(BF)
        here = keeps & (s == layer)

        @pl.when(here)
        def _():
            pltpu.make_async_copy(v.oq.at[i], dst.at[g], v.s_loc.at[8 + i]).start()

        @pl.when(jnp.logical_not(here))
        def _():
            remote(v.oq.at[i], dst.at[g], v.s_out.at[i, 0], v.s_out.at[i, 1 + g], (layer, own_b, t)).start()

    def put_out_wait(i, layer, dst):
        here = keeps & (s == layer)

        @pl.when(here)
        def _():
            pltpu.make_async_copy(v.oq.at[i], dst.at[g], v.s_loc.at[8 + i]).wait()

        @pl.when(jnp.logical_not(here))
        def _():
            remote(v.oq.at[i], dst.at[g], v.s_out.at[i, 0], v.s_out.at[i, 1 + g], (layer, own_b, t)).wait_send()

        @pl.when(s == layer)
        def _():
            def got(m):
                remote(v.oq.at[i], dst.at[m], v.s_out.at[i, 0], v.s_out.at[i, 1 + m], me_x).wait_recv()

            got(1 - g)

            @pl.when(g != s)
            def _():
                got(g)

    def grad_of(layer, key, left, right):
        first, n = shares(key, ff)[:2]
        for i in range(dim // 256):
            lo = i * 256
            v.gr[layer, lo : lo + 256, first : first + n] = tn(left[:, lo : lo + 256], right).astype(BF)

    def buf(name, layer, key):
        return b_[f"{name}{layer}{key}"]

    def swaps(layer, key):
        return MODES[layer, key] == "swap"

    def all_cols(key):
        return pl.ds(*shares(key, ff)[:2])

    def share_cols(key, e):
        first, _, stride, n = shares(key, ff)
        return pl.ds(pl.multiple_of(first + e * stride, 128), n)

    def slice_rows(k, d=0):
        return pl.multiple_of(((zi + d) % half + half * k) * part, 16)

    def swap_copy(layer, key):
        sem = buf("s_x", layer, key)
        return remote(
            v.gr.at[layer, :, share_cols(key, 1 - s)], buf("xr", layer, key), sem.at[0], sem.at[1], me_x
        )

    def run_copy(layer, key, d, k):
        sem, rs = buf("s_a", layer, key), pl.ds(slice_rows(k, d), part)
        if swaps(layer, key):
            src = buf("xr", layer, key).at[rs]
        else:
            src = v.gr.at[layer, rs, all_cols(key)]
        return remote(src, buf("ar", layer, key).at[d - 1, k], sem.at[0, d, k], sem.at[1, d, k], zpeer(d))

    def run_copies(layer, key):
        return [run_copy(layer, key, d, k) for d in range(1, half) for k in range(2)]

    def cross_copy(layer, key):
        sem = buf("s_b", layer, key)
        return remote(buf("bs", layer, key), buf("br", layer, key), sem.at[0], sem.at[1], me_x)

    def last_copy(layer, key):
        sem = buf("s_c", layer, key)
        return remote(buf("cs", layer, key), buf("cr", layer, key), sem.at[0], sem.at[1], me_o)

    def home_copy(layer, key):
        sem = buf("s_e", layer, key)
        return remote(buf("es", layer, key), buf("er", layer, key), sem.at[0], sem.at[1], me_x)

    def run_sum(layer, key, k, rs):
        own = pl.ds(pl.multiple_of(slice_rows(k) + rs.start, 16), RB)
        if swaps(layer, key):
            tot = buf("xr", layer, key)[own, :].astype(F32)
        else:
            tot = v.gr[layer, own, all_cols(key)].astype(F32)
        for d in range(1, half):
            tot = tot + buf("ar", layer, key)[d - 1, k, rs, :].astype(F32)
        return tot

    def out_of(layer, key, e):
        base = e * shares(key, ff)[2] if swaps(layer, key) else 0
        return dict(d=o_d, u=o_u, o=o_o, q=o_q, k=o_q)[key], base + 256 * (key == "k")

    def give(layer, key):
        if swaps(layer, key):
            swap_copy(layer, key).start()
        else:
            for cp in run_copies(layer, key):
                cp.start()

    def second(layer, key):
        if swaps(layer, key):
            swap_copy(layer, key).wait_recv()
            xr = buf("xr", layer, key)

            def body(rs):
                xr[rs, :] = (v.gr[layer, rs, share_cols(key, s)].astype(F32) + xr[rs, :].astype(F32)).astype(BF)

            row_loop(body, dim)
            for cp in run_copies(layer, key):
                cp.start()
            return

        for cp in run_copies(layer, key):
            cp.wait_recv()

        @pl.when(s != layer)
        def _():
            for k in range(2):

                def body(rs, k=k):
                    buf("bs", layer, key)[k, rs, :] = run_sum(layer, key, k, rs).astype(BF)

                row_loop(body, part)
            cross_copy(layer, key).start()

    def third(layer, key):
        cs = buf("cs", layer, key)
        if swaps(layer, key):
            for cp in run_copies(layer, key):
                cp.wait_recv()

            def body(rs):
                cs[rs, :] = run_sum(layer, key, 1 - g, rs).astype(BF)

            row_loop(body, part)
            last_copy(layer, key).start()
            return

        @pl.when(s == layer)
        def _():
            cross_copy(layer, key).wait_recv()
            br = buf("br", layer, key)

            def body(rs):
                cs[rs, :] = (run_sum(layer, key, 1 - g, rs) + br[1 - g, rs, :].astype(F32)).astype(BF)

            row_loop(body, part)
            last_copy(layer, key).start()

    def fourth(layer, key):
        cr = buf("cr", layer, key)
        out, at = out_of(layer, key, layer)

        @pl.when(s == layer)
        def _():
            last_copy(layer, key).wait_recv()

            def body(rs):
                tot = run_sum(layer, key, g, rs) + cr[rs, :].astype(F32)
                if not swaps(layer, key):
                    tot = tot + buf("br", layer, key)[g, rs, :].astype(F32)
                out[rs, at : at + tot.shape[1]] = tot

            row_loop(body, part)

        if swaps(layer, key):

            @pl.when(s != layer)
            def _():
                last_copy(layer, key).wait_recv()

                def body(rs):
                    tot = run_sum(layer, key, g, rs) + cr[rs, :].astype(F32)
                    buf("es", layer, key)[rs, :] = tot.astype(BF)

                row_loop(body, part)
                home_copy(layer, key).start()

    def fifth(layer, key):
        if swaps(layer, key):
            out, at = out_of(layer, key, 1 - layer)

            @pl.when(s == layer)
            def _():
                home_copy(layer, key).wait_recv()

                def body(rs):
                    got = buf("er", layer, key)[rs, :].astype(F32)
                    out[rs, at : at + got.shape[1]] = got

                row_loop(body, part)

    def grads_close():
        for (layer, key), mode in MODES.items():
            for cp in run_copies(layer, key):
                cp.wait_send()
            if mode == "swap":
                swap_copy(layer, key).wait_send()
                last_copy(layer, key).wait_send()

            @pl.when(s == layer)
            def _(layer=layer, key=key, mode=mode):
                if mode == "run":
                    last_copy(layer, key).wait_send()

            @pl.when(s != layer)
            def _(layer=layer, key=key, mode=mode):
                (home_copy if mode == "swap" else cross_copy)(layer, key).wait_send()

    def rows_of(buf, layer):
        x = buf[layer]
        return x.reshape(full, x.shape[-1])

    stages = (give, second, third, fourth, fifth)
    spots = {
        (1, 0): ("1 1du",),
        (1, 1): ("1 1o",),
        (1, 5): ("2 1du", "1 1q"),
        (1, 2): ("1 1k", "2 1o"),
        (0, 0): ("1 0du",),
        (0, 1): ("1 0o", "2 1qk", "3 1d"),
        (0, 5): ("1 0q", "2 0du", "3 1o"),
        (0, 2): ("1 0k", "2 0o", "3 1u", "2 0q"),
        (0, 3): ("3 0u", "2 0k", "3 0odq", "4 0u", "3 0k", "4 1d", "3 1qk", "4 1uo", "4 0doq", "5 1do"),
        (0, 4): ("5 0uo", "4 0k", "4 1qk"),
    }

    def serve(layer, spot):
        for line in spots.get((layer, spot), ()):
            for key in line[3:]:
                stages[int(line[0]) - 1](int(line[2]), key)

    def back_rows(layer, j, u_buf, r_buf, gain, base, at, extra=None):
        v.stt[...] = jnp.zeros(v.stt.shape, F32)

        def body(rs):
            gsec = sum_rows(j, rs)
            u, r = u_buf[layer, rs, :], r_buf[layer, rs, :]
            gg = gsec * gain
            res = r * (
                gg - jnp.mean(gg, axis=-1, keepdims=True) - u * jnp.mean(gg * u, axis=-1, keepdims=True)
            )
            inn = base[rs, :]
            out = inn + res
            at(rs, out)
            v.stt[0] += gsec * u
            v.stt[1] += gsec
            v.stt[2] += out
            v.stt[3] += inn

        row_loop(body)

    def backward_begin(layer):
        def d_second(hf):
            dgel = nt(v.dyb[layer, hf], v.wdb[layer])
            v.du[hf] = (dgel * v.gp[layer, hf]).astype(BF)
            return nt(v.du[hf], v.wub[layer])

        sum_begin(4 + 2 * (1 - layer), d_second)

    def backward(layer):
        j = 4 + 2 * (1 - layer)
        grad_of(layer, "d", rows_of(v.dyb, layer), rows_of(v.gl, layer))
        grad_of(layer, "u", rows_of(v.sb, layer), v.du[...].reshape(full, ff))
        ones = jnp.ones((8, full), BF)
        v.smo[layer, 6:7, :] = nn(ones, v.du[...].reshape(full, ff))[0:1]
        serve(layer, 0)
        sum_end(j)

        def at_two(rs, out):
            v.dhf[rs, :] = out
            v.dhb[layer, c, rs, :] = out.astype(BF)

        back_rows(layer, j, v.u2, v.r2, prow(layer, 1), v.dyf, at_two)
        share(v.dhb, layer, 4 + layer)
        for i, row in ((0, 1), (1, 3), (2, 4), (3, 5)):
            v.smo[layer, row : row + 1, :] = jnp.sum(v.stt[i], axis=0, keepdims=True)

        def d_att(hf):
            rs = pl.ds(pl.multiple_of(hf * two, 16), two)
            v.dgo[layer, rs, :] = nt(v.dhb[layer, hf], v.wob[layer]).astype(BF)

        d_att(c)
        share_wait(v.dhb, layer, 4 + layer)
        d_att(1 - c)
        dat = v.dgo[layer].astype(F32)
        prod = dat * v.attf[layer]
        tile = dat[:, 0:128]
        for h in range(3):
            real = (lane_f >= 64 * h + 64) & (lane_f < 64 * h + 128)
            delta = jnp.sum(jnp.where(real, prod, 0.0), axis=1, keepdims=True)
            for i, piece in enumerate(splits(-delta)):
                tile = jnp.where(lane == 3 * h + i, piece, tile)
        v.dgo[layer, :, 0:128] = tile.astype(BF)
        group_send(v.dgo.at[layer], v.dg.at[layer, own_b], v.s_ds.at[layer], v.s_dr.at[layer])
        grad_of(layer, "o", rows_of(v.dhb, layer), rows_of(v.attb, layer))
        serve(layer, 1)

        put_masked(v.ma, v.qa[layer], k_mask)
        put_masked(v.mb, v.dgo[layer], v_mask)
        v.dqs[...] = jnp.zeros(v.dqs.shape, F32)

        def query_block(bk, carry):
            build_kv(layer, bk)
            kt, vt = v.kt[...], v.vt[...]
            terms = []
            for h in range(3):
                p = jnp.exp(nt(v.ma[h], kt))
                ds = (p * nt(v.mb[h], vt)).astype(BF)
                terms.append(nn(ds, kt))
            v.dqs[...] += by_head_k(terms)
            return carry

        lax.fori_loop(0, nd, query_block, 0)
        for i in range(2):
            rs = slice(i * two, (i + 1) * two)
            v.gm[i, :, 0:128] = (v.dqs[rs, 0:128] * 0.125).astype(BF)
            v.gm[i, :, 128:256] = jnp.where(lane[rs] < 64, v.dqs[rs, 128:256] * 0.125, 0.0).astype(BF)
        grad_of(layer, "q", rows_of(v.nb, layer), v.gm[:, :, 0:256].reshape(full, 256))
        serve(layer, 5)

        build_kv(layer, own_b)
        put_masked(v.ma, v.kt[...], k_mask)
        put_masked(v.mb, v.vt[...], v_mask)
        v.dks[...] = jnp.zeros(v.dks.shape, F32)
        v.dvs[...] = jnp.zeros(v.dvs.shape, F32)

        def key_block(k, carry):
            zk, sk = (zi + k % half) % half, (s + k // half) % 2
            bk = zk + half * sk
            q_at, d_at = v.qg.at[layer, bk], v.dg.at[layer, bk]
            remote(q_at, q_at, v.s_qs.at[layer, 0], v.s_qr.at[layer, bk], me_x).wait_recv()
            remote(d_at, d_at, v.s_ds.at[layer, 0], v.s_dr.at[layer, bk], me_x).wait_recv()
            if big:
                cps = (
                    pltpu.make_async_copy(q_at, v.kt, v.s_loc.at[0]),
                    pltpu.make_async_copy(d_at, v.vt, v.s_loc.at[1]),
                )
                for cp in cps:
                    cp.start()
                for cp in cps:
                    cp.wait()
                key_terms(v.kt[...], v.vt[...])
            else:
                key_terms(q_at[...], d_at[...])
            return carry

        def key_terms(qt, dt):
            tk, tv = [], []
            for h in range(3):
                p = jnp.exp(nt(v.ma[h], qt))
                ds = (p * nt(v.mb[h], dt)).astype(BF)
                tv.append(nn(p.astype(BF), dt))
                tk.append(nn(ds, qt))
            v.dks[...] += by_head_k(tk)
            v.dvs[...] += by_head_v(tv)

        key_terms(v.qa[layer], v.dgo[layer])
        lax.fori_loop(1, nd, key_block, 0)

        for i in range(2):
            rs = slice(i * two, (i + 1) * two)
            v.gm[i, :, 256:384] = v.dks[rs, 0:128].astype(BF)
            v.gm[i, :, 384:512] = jnp.where(lane[rs] < 64, v.dks[rs, 128:256], v.dvs[rs, 0:128]).astype(BF)
            v.gm[i, :, 512:640] = v.dvs[rs, 128:256].astype(BF)
        sum_begin(j + 1, lambda hf: nn(v.gm[hf], v.wqb[layer]))
        grad_of(layer, "k", rows_of(v.nb, layer), v.gm[:, :, 256:640].reshape(full, 384))
        v.smo[layer, 7:8, :] = jnp.zeros((1, dim), F32)
        v.smo[layer, 7:8, 0:640] = nn(ones, v.gm[...].reshape(full, 640))[0:1]
        serve(layer, 2)
        sum_end(j + 1)

        def at_one(rs, out):
            low = out.astype(BF)
            v.dyf[rs, :] = low.astype(F32)
            if layer == 1:
                v.dyb[0, c, rs, :] = low

        back_rows(layer, j + 1, v.u1, v.r1, prow(layer, 0), v.dhf, at_one)
        for i, row in ((0, 0), (1, 2)):
            v.smo[layer, row : row + 1, :] = jnp.sum(v.stt[i], axis=0, keepdims=True)
        if layer == 1:
            share(v.dyb, 0, 7)
        put_out(2 + layer, layer, v.dyf, igs)

    norm_one(0)
    forward(0)
    forward_end(0)
    red(og, v.gq, 1)
    forward(1)
    red_wait(og, v.gq, 1)
    send(v.gq.at[0], v.gq.at[1], v.s_xy.at[2], v.s_xy.at[3], me_y)
    v.dyf[q_own, :] = v.gq[0].astype(F32)
    remote(v.gq.at[0], v.gq.at[1], v.s_xy.at[2], v.s_xy.at[3], me_y).wait_recv()
    v.dyf[q_oth, :] = v.gq[1].astype(F32)
    v.dyb[1, c] = v.dyf[...].astype(BF)
    share(v.dyb, 1, 6)
    share_wait(v.dyb, 1, 6)
    backward_begin(1)
    forward_end(1)
    backward(1)
    share_wait(v.dyb, 0, 7)
    backward_begin(0)
    backward(0)

    send(v.smo, v.smc, v.s_sm.at[0], v.s_sm.at[1], me_c)
    remote(v.smo, v.smc, v.s_sm.at[0], v.s_sm.at[1], me_c).wait_recv()
    rowid = lax.broadcasted_iota(jnp.int32, (8, dim), 0)
    for layer in range(2):
        v.smc[layer] = v.smo[layer] + jnp.where(rowid < 6, v.smc[layer], 0.0)
    for k in range(1, 2 * nd):
        other = (s * nd + z + k) % (2 * nd)
        so = other // nd
        send(v.smc.at[so], v.smr.at[k - 1], v.s_sms.at[k - 1], v.s_smr.at[k - 1], (so, other % nd, t))
    serve(0, 3)
    for k in range(1, 2 * nd):
        remote(v.smr.at[0], v.smr.at[k - 1], v.s_sms.at[k - 1], v.s_smr.at[k - 1], me_x).wait_recv()
    tot = v.smc[s]
    for k in range(1, 2 * nd):
        tot = tot + v.smr[k - 1]
    o_s[...] = tot
    serve(0, 4)

    for cp in late:
        cp.wait_send()

    grads_close()
    for i, src, dst in ((0, fr, v.xq), (1, og, v.gq)):

        @pl.when(keeps)
        def _(i=i, src=src, dst=dst):
            remote(src.at[1 - g], dst.at[0], v.s_red.at[i], v.s_red.at[2 + i], me_o).wait_send()

    for i in range(4):
        forward_w_end(i)
    put_out_wait(0, 0, acts)
    put_out_wait(1, 1, acts)
    put_out_wait(2, 0, igs)
    put_out_wait(3, 1, igs)


def lay_out(nd, a_in, i_in, q_in, u_in, o_in, d_in, sums, acts, igs, g_q, bias, g_o, g_u, upb, g_d, gain, shift, sq):
    for src, dst in ((a_in, acts), (i_in, igs), (u_in, g_u), (d_in, g_d)):
        dst[...] = src[...]
    z, t = lax.axis_index("dp"), lax.axis_index("tensor")
    part, dim = u_in.shape[0], sums.shape[1]
    hl = g_q.shape[2]
    heads, _, hw = bias.shape
    g_q[0] = q_in[:, 0:hl]
    g_q[1] = q_in[:, 256 : 256 + hl]
    g_q[2] = pltpu.roll(q_in[:, 384:640], 192, 1)[:, 0:hl]
    sq[0:part, :] = o_in[...]
    g_o[...] = sq[...].T[64 : 64 + hl, 0:part]

    def from_lane(lo, n):
        return pltpu.roll(sums[...], (dim - lo) % dim, 1)[:, 0:n]

    for h in range(heads):
        bias[h, 0:1, :] = from_lane(h * HD + z * hw, hw)[7:8]
        bias[h, 1:2, :] = from_lane(256 + hl + h * HD + z * hw, hw)[7:8]
        uw = upb.shape[2]
        upb[h] = from_lane((h * nd + z) * uw, uw)[6:7]
    norms = from_lane((z * 4 + t) * gain.shape[1], gain.shape[1])
    gain[...] = norms[0:2]
    shift[...] = norms[2:6]


def local(frames, out_grad, clip_ids, w_qkv, bias_qv, w_out, w_up, bias_up, w_down, ln_gain, shifts):
    rows, dim = frames.shape[1:]
    nd = lax.axis_size("dp")
    half = nd // 2
    z, t, s = lax.axis_index("dp"), lax.axis_index("tensor"), lax.axis_index("section")
    hl = w_qkv.shape[3]
    ff = w_up.shape[2]
    part = dim // nd
    wide = w_qkv[0].transpose(1, 2, 0).reshape(3 * hl, dim)
    clip = lax.dynamic_index_in_dim(clip_ids, z // half, 0, keepdims=False)
    clip = clip.reshape(nd, 4, rows)
    clip = jnp.stack([clip[:, 0], clip[:, 2], clip[:, 1], clip[:, 3]], axis=1).reshape(nd, 4 * rows)
    lane = jnp.arange(128)
    same = clip[:, :, None] == (lane - 80)[None, None, :]
    spot = lane >= 80
    k_feat = jnp.where(
        (lane >= 64) & (lane < 73), 1.0, jnp.where(spot & jnp.logical_not(same), -BIG, 0.0)
    ).astype(BF)
    plan = scratch_plan(nd, rows, dim, hl, ff)
    shape = jax.ShapeDtypeStruct
    anyspec = pl.BlockSpec(memory_space=pl.ANY)
    vspec = pl.BlockSpec(memory_space=pltpu.VMEM)
    gathered = {name: (2, nd, 4 * rows, 256) for name in ("qg", "dg")}
    big = nd > MOST
    if not big:
        plan.update({name: pltpu.VMEM(dims, BF) for name, dims in gathered.items()})
    outs = pl.pallas_call(
        functools.partial(mega, nd, (*gathered, *plan) if big else tuple(plan)),
        out_shape=(
            shape((2, rows, dim), BF),
            shape((2, rows, dim), BF),
            shape((part, 640), F32),
            shape((part, ff), F32),
            shape((part, 256), F32),
            shape((part, ff), F32),
            shape((8, dim), F32),
        )
        + tuple(shape(dims, BF) for dims in gathered.values()) * big,
        in_specs=[anyspec] * 6 + [vspec] * 5,
        out_specs=(anyspec,) * 2 + (vspec,) * 5 + (anyspec,) * (2 * big),
        scratch_shapes=list(plan.values()),
        compiler_params=pltpu.CompilerParams(
            collective_id=0, has_side_effects=True, vmem_limit_bytes=63 * 1024 * 1024
        ),
    )(frames, out_grad, wide, w_out[0], w_up[0], w_down[0], ln_gain[0], shifts[0], bias_up, bias_qv[0], k_feat)

    own, hw, uw = dim // (4 * nd), HD // nd, ff // (hl // HD) // nd
    heads = hl // HD
    acts, igs, g_q, bias, g_o, g_u, upb, g_d, gain, shift = pl.pallas_call(
        functools.partial(lay_out, nd),
        out_shape=(
            shape((2, rows, dim), BF),
            shape((2, rows, dim), BF),
            shape((3, part, hl), F32),
            shape((heads, 2, hw), F32),
            shape((hl, part), F32),
            shape((part, ff), F32),
            shape((heads, 1, uw), F32),
            shape((part, ff), F32),
            shape((2, own), F32),
            shape((4, own), F32),
        ),
        in_specs=[vspec] * 7,
        out_specs=(vspec,) * 10,
        scratch_shapes=[pltpu.VMEM((256, 256), F32)],
    )(*outs[:7])
    return (
        acts[None],
        igs[None],
        g_q.transpose(1, 0, 2)[None],
        bias.transpose(1, 0, 2)[None],
        g_o[None],
        g_u[None],
        upb.transpose(1, 0, 2),
        g_d.T[None],
        gain[None],
        shift[None],
    )


def solution(mesh):
    in_specs = (
        P(None, ("dp", "tensor"), None),
        P(None, ("dp", "tensor"), None),
        P(),
        P("section", None, None, "tensor"),
        P("section", None, "tensor"),
        P("section", "tensor", None),
        P("section", None, "tensor"),
        P("section", "tensor"),
        P("section", "tensor", None),
        P("section", None, None),
        P("section", None, None),
    )
    out_specs = (
        P("section", None, ("dp", "tensor"), None),
        P("section", None, ("dp", "tensor"), None),
        P("section", "dp", None, "tensor"),
        P("section", None, "tensor", "dp"),
        P("section", "tensor", "dp"),
        P("section", "dp", "tensor"),
        P("section", "tensor", "dp"),
        P("section", "tensor", "dp"),
        P("section", None, ("dp", "tensor")),
        P("section", None, ("dp", "tensor")),
    )
    return jax.shard_map(local, mesh=mesh, in_specs=in_specs, out_specs=out_specs, check_vma=False)
```

```python
import functools

import jax
import jax.numpy as jnp
from jax import lax
from jax.experimental import pallas as pl
from jax.experimental.pallas import tpu as pltpu
from jax.sharding import PartitionSpec as P

HD = 64
BIG = 2.0**100
MESH = pl.DeviceIdType.MESH
BF = jnp.bfloat16
F32 = jnp.float32
RB = 16
SLOTS = 4
MOST = 4


def nt(a, b):
    return lax.dot_general(a, b, (((1,), (1,)), ((), ())), preferred_element_type=F32)


def nn(a, b):
    return lax.dot_general(a, b, (((1,), (0,)), ((), ())), preferred_element_type=F32)


def tn(a, b):
    return lax.dot_general(a, b, (((0,), (0,)), ((), ())), preferred_element_type=F32)


def shares(key, ff):
    return {
        "d": (0, ff, ff // 2, ff // 2),
        "u": (ff, ff, ff // 2, ff // 2),
        "o": (2 * ff, 256, 128, 128),
        "q": (2 * ff + 256, 256, 128, 128),
        "k": (2 * ff + 512, 384, 0, 0),
    }[key]


MODES = {
    (1, "d"): "swap",
    (1, "u"): "run",
    (1, "o"): "swap",
    (1, "q"): "run",
    (1, "k"): "run",
    (0, "d"): "run",
    (0, "u"): "swap",
    (0, "o"): "swap",
    (0, "q"): "run",
    (0, "k"): "run",
}


def scratch_plan(nd, rows, dim, head_dim, ff):
    half = nd // 2
    full = 4 * rows
    two = 2 * rows
    part = dim // nd
    wide = 640 + ff + 256 + ff
    vm = pltpu.VMEM
    dma = pltpu.SemaphoreType.DMA
    plan = dict(
        wqb=vm((2, 640, dim), BF),
        wob=vm((2, 256, dim), BF),
        wub=vm((2, dim, ff), BF),
        wdb=vm((2, ff, dim), BF),
        spb=vm((2, 16, dim), F32),
        xq=vm((2, rows, dim), BF),
        gq=vm((2, rows, dim), BF),
        xres=vm((two, dim), F32),
        dyf=vm((two, dim), F32),
        dyb=vm((2, 2, two, dim), BF),
        nb=vm((2, 2, two, dim), BF),
        sb=vm((2, 2, two, dim), BF),
        hid=vm((two, dim), F32),
        u1=vm((2, two, dim), F32),
        u2=vm((2, two, dim), F32),
        r1=vm((2, two, 1), F32),
        r2=vm((2, two, 1), F32),
        qa=vm((2, full, 256), BF),
        kvb=vm((2, nd, full, 384), BF),
        kt=vm((full, 256), BF),
        vt=vm((full, 256), BF),
        dgo=vm((2, full, 256), BF),
        mst=vm((3, full, 1), F32),
        lst=vm((3, full, 1), F32),
        attf=vm((2, full, 256), F32),
        attb=vm((2, 2, two, 256), BF),
        gl=vm((2, 2, two, ff), BF),
        gp=vm((2, 2, two, ff), F32),
        du=vm((2, two, ff), BF),
        dhb=vm((2, 2, two, dim), BF),
        dhf=vm((two, dim), F32),
        gm=vm((2, two, 640), BF),
        ma=vm((3, full, 256), BF),
        mb=vm((3, full, 256), BF),
        dqs=vm((full, 256), F32),
        dks=vm((full, 256), F32),
        dvs=vm((full, 256), F32),
        cs=vm((two, dim), BF),
        cr=vm((SLOTS, two, dim), BF),
        ys=vm((2, two, dim), BF),
        yr=vm((SLOTS, two, dim), BF),
        chip=vm((2, two, dim), F32),
        gr=vm((2, dim, wide), BF),
        smo=vm((2, 8, dim), F32),
        smc=vm((2, 8, dim), F32),
        smr=vm((2 * nd - 1, 8, dim), F32),
        stt=vm((6, RB, dim), F32),
        oq=vm((4, rows, dim), BF),
        s_loc=dma((12,)),
        s_red=dma((4,)),
        s_xy=dma((4,)),
        s_wx=dma((2, 13)),
        s_wzs=dma((12, half)),
        s_wzr=dma((12, half)),
        s_ag=dma((2, 8)),
        s_cc=dma((2, SLOTS)),
        s_yy=dma((2, SLOTS)),
        s_kvs=dma((2, nd)),
        s_kvr=dma((2, nd)),
        s_qs=dma((2, nd)),
        s_qr=dma((2, nd)),
        s_ds=dma((2, nd)),
        s_dr=dma((2, nd)),
        s_sm=dma((2,)),
        s_sms=dma((2 * nd - 1,)),
        s_smr=dma((2 * nd - 1,)),
        s_out=dma((4, 3)),
    )
    for (layer, key), mode in MODES.items():
        n = shares(key, ff)[1 if mode == "run" else 3]
        tag = f"{layer}{key}"
        if mode == "swap":
            plan["xr" + tag] = vm((dim, n), BF)
            plan["s_x" + tag] = dma((2,))
        else:
            plan["bs" + tag] = vm((2, part, n), BF)
            plan["br" + tag] = vm((2, part, n), BF)
            plan["s_b" + tag] = dma((2,))
        plan["ar" + tag] = vm((half - 1, 2, part, n), BF)
        plan["s_a" + tag] = dma((2, half, 2))
        plan["cs" + tag] = vm((part, n), BF)
        plan["cr" + tag] = vm((part, n), BF)
        plan["s_c" + tag] = dma((2,))
        if mode == "swap":
            plan["es" + tag] = vm((part, n), BF)
            plan["er" + tag] = vm((part, n), BF)
            plan["s_e" + tag] = dma((2,))
    return plan


def mega(nd, names, *refs):
    (fr, og, wq, wo, wu, wd, gains, moves, bup, bqv, kf) = refs[:11]
    (acts, igs, o_q, o_u, o_o, o_d, o_s) = refs[11:18]
    b_ = dict(zip(names, refs[18:]))
    big = nd > MOST

    class Bufs:
        pass

    v = Bufs()
    v.__dict__.update(b_)
    half = nd // 2
    rows, dim = fr.shape[1:]
    two, full = 2 * rows, 4 * rows
    ff = wu.shape[1]
    part = dim // nd
    s = lax.axis_index("section")
    z = lax.axis_index("dp")
    t = lax.axis_index("tensor")
    g, zi = z // half, z % half
    c, y = t % 2, t // 2
    own_b = zi + half * s
    zo = (z + half) % nd
    me_x = (1 - s, z, t)
    me_c = (s, z, t + 1 - 2 * c)
    me_y = (s, z, (t + 2) % 4)
    me_o = (s, zo, t)

    def zpeer(d):
        return (s, g * half + (zi + d) % half, t)

    def member(k):
        zk, sk = (zi + k % half) % half, (s + k // half) % 2
        return (sk, g * half + zk, t), zk + half * sk

    def remote(src, dst, ss, rs, dev):
        return pltpu.make_async_remote_copy(
            src_ref=src, dst_ref=dst, send_sem=ss, recv_sem=rs, device_id=dev, device_id_type=MESH
        )

    late = []

    def send(src, dst, ss, rs, dev):
        cp = remote(src, dst, ss, rs, dev)
        cp.start()
        late.append(cp)
        return cp

    loads = [
        pltpu.make_async_copy(wq.at[pl.ds(0, 192)], v.wqb.at[s, pl.ds(0, 192)], v.s_loc.at[0]),
        pltpu.make_async_copy(wq.at[pl.ds(192, 384)], v.wqb.at[s, pl.ds(256, 384)], v.s_loc.at[1]),
        pltpu.make_async_copy(wo, v.wob.at[s, pl.ds(64, 192)], v.s_loc.at[2]),
        pltpu.make_async_copy(wu, v.wub.at[s], v.s_loc.at[3]),
        pltpu.make_async_copy(wd, v.wdb.at[s], v.s_loc.at[4]),
    ]
    for cp in loads:
        cp.start()
    v.wqb[s, pl.ds(192, 64), :] = jnp.zeros((64, dim), BF)
    v.wob[s, pl.ds(0, 64), :] = jnp.zeros((64, dim), BF)
    hl = bqv.shape[1]
    v.spb[s, 0:2, :] = gains[...].astype(F32)
    v.spb[s, 2:6, :] = moves[...].astype(F32)
    v.spb[s, 6:7, :] = bup[...].astype(F32)
    v.spb[s, 7:16, :] = jnp.zeros((9, dim), F32)
    v.spb[s, 7:9, 0:hl] = bqv[...].astype(F32)
    v.spb[s, 8:16, :] = pltpu.roll(v.spb[s, 8:16, :], hl, 1)

    barrier = pltpu.get_barrier_semaphore()
    for k in range(1, 2 * nd):
        other = (s * nd + z + k) % (2 * nd)
        pl.semaphore_signal(barrier, inc=1, device_id=(other // nd, other % nd, t), device_id_type=MESH)
    for dev in (me_c, me_y):
        pl.semaphore_signal(barrier, inc=1, device_id=dev, device_id_type=MESH)
    pl.semaphore_wait(barrier, 2 * nd + 1)

    keeps = g == s

    def red(src, dst, i):
        @pl.when(keeps)
        def _():
            pltpu.make_async_copy(src.at[g], dst.at[0], v.s_loc.at[6 + i]).start()
            remote(src.at[1 - g], dst.at[0], v.s_red.at[i], v.s_red.at[2 + i], me_o).start()

    def red_wait(src, dst, i):
        @pl.when(keeps)
        def _():
            pltpu.make_async_copy(src.at[g], dst.at[0], v.s_loc.at[6 + i]).wait()

        @pl.when(jnp.logical_not(keeps))
        def _():
            remote(src.at[1 - g], dst.at[0], v.s_red.at[i], v.s_red.at[2 + i], me_o).wait_recv()

    red(fr, v.xq, 0)
    for cp in loads[:2]:
        cp.wait()
    mats = (v.wqb, v.wob, v.wub, v.wdb)

    def w_parts(i):
        n = (2, 2, 2, 3)[i]
        return n if mats[i].shape[1] // half % (16 * n) == 0 else 1

    def straight(i, e):
        return i == 3 and e == 2

    def w_rows(i, p, e):
        n = mats[i].shape[1] // half
        m = n // w_parts(i)
        return pl.ds(pl.multiple_of(p * n + e * m, 16), m)

    def ship(i):
        for e in range(w_parts(i)):
            src = mats[i].at[s, w_rows(i, zi, e)]
            send(src, src, v.s_wx.at[0, 3 * i + e], v.s_wx.at[1, 3 * i + e], me_x)
        for e in range(w_parts(i)):
            for d in range(1, half) if straight(i, e) else ():
                src = mats[i].at[s, w_rows(i, (zi + half - d) % half, e)]
                remote(src, src, v.s_wzs.at[3 * i + e, d], v.s_wzr.at[3 * i + e, d], me_x).start()

    send(v.spb.at[s], v.spb.at[s], v.s_wx.at[0, 12], v.s_wx.at[1, 12], me_x)
    ship(0)
    loads[2].wait()
    ship(1)
    loads[3].wait()
    ship(2)
    loads[4].wait()

    def w_copy(i, e, d, back=0):
        src = mats[i].at[1 - s, w_rows(i, (zi + back) % half, e)]
        return remote(src, src, v.s_wzs.at[3 * i + e, d], v.s_wzr.at[3 * i + e, d], zpeer(d))

    def forward_w(i, e=None):
        for e in range(w_parts(i)) if e is None else (e,):
            if e < w_parts(i):
                src = mats[i].at[1 - s, w_rows(i, zi, e)]
                remote(src, src, v.s_wx.at[0, 3 * i + e], v.s_wx.at[1, 3 * i + e], me_x).wait_recv()
                for d in () if straight(i, e) else range(1, half):
                    w_copy(i, e, d).start()

    def forward_w_end(i):
        for e in range(w_parts(i)):
            for d in range(1, half):
                w_copy(i, e, d).wait_send()

    def gather_w(i, layer):
        @pl.when(s != layer)
        def _():
            for e in range(w_parts(i)):
                for d in range(1, half):
                    w_copy(i, e, d, half - d).wait_recv()

    red_wait(fr, v.xq, 0)
    send(v.xq.at[0], v.xq.at[1], v.s_xy.at[0], v.s_xy.at[1], me_y)
    remote(v.spb.at[s], v.spb.at[s], v.s_wx.at[0, 12], v.s_wx.at[1, 12], me_x).wait_recv()
    q_own = pl.ds(pl.multiple_of(rows * y, 8), rows)
    q_oth = pl.ds(pl.multiple_of(rows * (1 - y), 8), rows)
    v.xres[q_own, :] = v.xq[0].astype(F32)
    forward_w(0, 0)
    remote(v.xq.at[0], v.xq.at[1], v.s_xy.at[0], v.s_xy.at[1], me_y).wait_recv()
    v.xres[q_oth, :] = v.xq[1].astype(F32)

    def prow(layer, i):
        return v.spb[layer, i : i + 1, :]

    def row_loop(fn, n=two):
        def step(i, carry):
            fn(pl.ds(pl.multiple_of(i * RB, RB), RB))
            return carry

        lax.fori_loop(0, n // RB, step, 0, unroll=n // RB if n == two else 4)

    def unit(x):
        cen = x - jnp.mean(x, axis=-1, keepdims=True)
        r = lax.rsqrt(jnp.mean(cen * cen, axis=-1, keepdims=True) + 1e-05)
        return cen * r, r

    def share(buf, layer, i):
        src = buf.at[layer, c]
        send(src, src, v.s_ag.at[0, i], v.s_ag.at[1, i], me_c)

    def share_wait(buf, layer, i):
        src = buf.at[layer, 1 - c]
        remote(src, src, v.s_ag.at[0, i], v.s_ag.at[1, i], me_c).wait_recv()

    def norm_one(layer):
        gain, shift = prow(layer, 0), prow(layer, 2)

        def body(rs):
            u, r = unit(v.xres[rs, :])
            v.u1[layer, rs, :] = u
            v.r1[layer, rs, :] = r
            v.nb[layer, c, rs, :] = (u * gain + shift).astype(BF)

        row_loop(body)
        share(v.nb, layer, layer)

    def sum_begin(j, term):
        k = j % SLOTS
        v.cs[...] = term(1 - c).astype(BF)
        cp = remote(v.cs, v.cr.at[k], v.s_cc.at[0, k], v.s_cc.at[1, k], me_c)
        cp.start()
        v.chip[j % 2] = term(c)
        cp.wait()

        def body(rs):
            tot = v.chip[j % 2, rs, :] + v.cr[k, rs, :].astype(F32)
            v.chip[j % 2, rs, :] = tot
            v.ys[j % 2, rs, :] = tot.astype(BF)

        row_loop(body)
        remote(v.ys.at[j % 2], v.yr.at[k], v.s_yy.at[0, k], v.s_yy.at[1, k], me_y).start()

    def sum_end(j):
        k = j % SLOTS
        remote(v.ys.at[j % 2], v.yr.at[k], v.s_yy.at[0, k], v.s_yy.at[1, k], me_y).wait()

    def sum_rows(j, rs):
        k = j % SLOTS
        return v.chip[j % 2, rs, :] + v.yr[k, rs, :].astype(F32)

    lane_f = lax.broadcasted_iota(jnp.int32, (full, 256), 1)
    lane = lax.broadcasted_iota(jnp.int32, (full, 128), 1)

    def k_mask(h):
        return (
            ((lane_f >= 64 * h) & (lane_f < 64 * h + 64))
            | ((lane_f >= 192 + 3 * h) & (lane_f < 195 + 3 * h))
            | (lane_f >= 208)
        )

    def v_mask(h):
        return ((lane_f >= 64 * h + 64) & (lane_f < 64 * h + 128)) | (
            (lane_f >= 3 * h) & (lane_f < 3 * h + 3)
        )

    def by_head_k(a):
        return jnp.where(lane_f < 64, a[0], jnp.where(lane_f < 128, a[1], a[2]))

    def by_head_v(a):
        return jnp.where(lane_f < 128, a[0], jnp.where(lane_f < 192, a[1], a[2]))

    def put_masked(dst, val, mask):
        val = val.astype(F32)
        for h in range(3):
            dst[h] = jnp.where(mask(h), val, 0.0).astype(BF)

    def build_kv(layer, bk):
        v.kt[:, 0:128] = v.kvb[layer, bk, :, 0:128]
        mid = v.kvb[layer, bk, :, 128:256].astype(F32)
        v.kt[:, 128:256] = jnp.where(lane < 64, mid, kf[bk].astype(F32)).astype(BF)
        v.vt[:, 0:128] = jnp.where(lane < 64, jnp.where(lane < 9, 1.0, 0.0), mid).astype(BF)
        v.vt[:, 128:256] = v.kvb[layer, bk, :, 256:384]

    def splits(x):
        hi = x.astype(BF).astype(F32)
        mid = (x - hi).astype(BF).astype(F32)
        return hi, mid, (x - hi) - mid

    def group_send(src, dst, ss, rs):
        for k in range(1, nd):
            dev, _ = member(k)
            send(src, dst, ss.at[k], rs.at[own_b], dev)

    def group_wait(buf, layer, rs, k, ss):
        dev, bk = member(k)
        dst = buf.at[layer, bk]
        remote(dst, dst, ss.at[0], rs.at[bk], dev).wait_recv()

    halves = (lambda i: c, lambda i: 1 - c)

    def forward(layer):
        bias_q, bias_kv = v.spb[layer, 7:8, 0:256], v.spb[layer, 8:9, 0:384]

        def qkv(hf):
            r = nt(v.nb[layer, hf], v.wqb[layer])
            rs = pl.ds(pl.multiple_of(hf * two, 16), two)
            q = (r[:, 0:256] + bias_q).astype(BF).astype(F32) * 0.125
            v.qa[layer, rs, 0:128] = q[:, 0:128].astype(BF)
            clip = kf[own_b, rs, :].astype(F32) * (1.0 / BIG) + 1.0
            clip = jnp.where(lane[0:two] >= 80, clip, 0.0)
            v.qa[layer, rs, 128:256] = (q[:, 128:256] + clip).astype(BF)
            v.kvb[layer, own_b, rs, :] = (r[:, 256:640] + bias_kv).astype(BF)

        if layer == 0:
            forward_w(0, 1)
        gather_w(0, layer)
        if layer == 0:
            forward_w(1)
        qkv(c)
        share_wait(v.nb, layer, layer)
        qkv(1 - c)
        group_send(v.kvb.at[layer, own_b], v.kvb.at[layer, own_b], v.s_kvs.at[layer], v.s_kvr.at[layer])

        put_masked(v.ma, v.qa[layer], k_mask)
        v.mst[...] = jnp.full(v.mst.shape, -3e38, F32)
        v.lst[...] = jnp.zeros(v.lst.shape, F32)
        v.dqs[...] = jnp.zeros(v.dqs.shape, F32)

        def block(k, carry):
            zk, sk = (zi + k % half) % half, (s + k // half) % 2
            bk = zk + half * sk

            @pl.when(k > 0)
            def _():
                dst = v.kvb.at[layer, bk]
                remote(dst, dst, v.s_kvs.at[layer, 0], v.s_kvr.at[layer, bk], me_x).wait_recv()

            if layer == 0:

                @pl.when(k == 1)
                def _():
                    forward_w(2)

            build_kv(layer, bk)
            kt, vt = v.kt[...], v.vt[...]
            alphas, news = [], []
            for h in range(3):
                sc = nt(v.ma[h], kt)
                old = v.mst[h]
                new = jnp.maximum(old, jnp.max(sc, axis=1, keepdims=True))
                alpha = jnp.exp(old - new)
                p = jnp.exp(sc - new)
                v.mst[h] = new
                v.lst[h] = v.lst[h] * alpha + jnp.sum(p, axis=1, keepdims=True)
                hi = p.astype(BF)
                lo = (p - hi.astype(F32)).astype(BF)
                news.append(nn(hi, vt) + nn(lo, vt))
                alphas.append(alpha)
            v.dqs[...] = v.dqs[...] * by_head_v(alphas) + by_head_v(news)
            return carry

        block(0, 0)
        if layer == 0:
            ship(3)
        lax.fori_loop(1, nd, block, 0)

        att = v.dqs[...] * by_head_v([1.0 / v.lst[h] for h in range(3)])
        v.attf[layer] = att
        v.attb[layer] = att.astype(BF).reshape(2, two, 256)
        tile = v.qa[layer, :, 128:256].astype(F32)
        for h in range(3):
            for i, piece in enumerate(splits(-(v.mst[h] + jnp.log(v.lst[h])))):
                tile = jnp.where(lane == 64 + 3 * h + i, piece, tile)
        v.qa[layer, :, 128:256] = tile.astype(BF)
        gather_w(1, layer)
        sum_begin(2 * layer, lambda hf: nn(v.attb[layer, hf], v.wob[layer]))
        if layer == 1:
            for one in (1, 0):
                group_send(v.qa.at[one], v.qg.at[one, own_b], v.s_qs.at[one], v.s_qr.at[one])
        if layer == 0:
            forward_w(3, 0)
        sum_end(2 * layer)
        out_bias, gain2, shift2 = prow(layer, 4), prow(layer, 1), prow(layer, 3)

        def body(rs):
            hid = v.xres[rs, :] + sum_rows(2 * layer, rs) + out_bias
            v.hid[rs, :] = hid
            u, r = unit(hid)
            v.u2[layer, rs, :] = u
            v.r2[layer, rs, :] = r
            v.sb[layer, c, rs, :] = (u * gain2 + shift2).astype(BF)

        row_loop(body)
        share(v.sb, layer, 2 + layer)
        if layer == 0:
            forward_w(3, 1)
            forward_w(3, 2)
        gather_w(2, layer)
        bias_up = prow(layer, 6)

        def up(hf):
            v.gp[layer, hf] = nn(v.sb[layer, hf], v.wub[layer]) + bias_up

            def gelu(rs):
                u = v.gp[layer, hf, rs, :]
                phi = 0.5 * (1.0 + lax.erf(u * 0.7071067811865476))
                v.gl[layer, hf, rs, :] = (u * phi).astype(BF)
                v.gp[layer, hf, rs, :] = phi + u * (jnp.exp(-0.5 * u * u) * 0.3989422804014327)

            row_loop(gelu)

        up(c)
        share_wait(v.sb, layer, 2 + layer)
        up(1 - c)
        gather_w(3, layer)
        sum_begin(2 * layer + 1, lambda hf: nn(v.gl[layer, hf], v.wdb[layer]))

    def forward_end(layer):
        sum_end(2 * layer + 1)
        out_bias = prow(layer, 5)

        def body(rs):
            out = v.hid[rs, :] + sum_rows(2 * layer + 1, rs) + out_bias
            v.xres[rs, :] = out.astype(BF).astype(F32)

        row_loop(body)
        if layer == 0:
            norm_one(1)
        put_out(layer, layer, v.xres, acts)

    def put_out(i, layer, src, dst):
        v.oq[i] = src[q_own, :].astype(BF)
        here = keeps & (s == layer)

        @pl.when(here)
        def _():
            pltpu.make_async_copy(v.oq.at[i], dst.at[g], v.s_loc.at[8 + i]).start()

        @pl.when(jnp.logical_not(here))
        def _():
            remote(v.oq.at[i], dst.at[g], v.s_out.at[i, 0], v.s_out.at[i, 1 + g], (layer, own_b, t)).start()

    def put_out_wait(i, layer, dst):
        here = keeps & (s == layer)

        @pl.when(here)
        def _():
            pltpu.make_async_copy(v.oq.at[i], dst.at[g], v.s_loc.at[8 + i]).wait()

        @pl.when(jnp.logical_not(here))
        def _():
            remote(v.oq.at[i], dst.at[g], v.s_out.at[i, 0], v.s_out.at[i, 1 + g], (layer, own_b, t)).wait_send()

        @pl.when(s == layer)
        def _():
            def got(m):
                remote(v.oq.at[i], dst.at[m], v.s_out.at[i, 0], v.s_out.at[i, 1 + m], me_x).wait_recv()

            got(1 - g)

            @pl.when(g != s)
            def _():
                got(g)

    def grad_of(layer, key, left, right):
        first, n = shares(key, ff)[:2]
        for i in range(dim // 256):
            lo = i * 256
            v.gr[layer, lo : lo + 256, first : first + n] = tn(left[:, lo : lo + 256], right).astype(BF)

    def buf(name, layer, key):
        return b_[f"{name}{layer}{key}"]

    def swaps(layer, key):
        return MODES[layer, key] == "swap"

    def all_cols(key):
        return pl.ds(*shares(key, ff)[:2])

    def share_cols(key, e):
        first, _, stride, n = shares(key, ff)
        return pl.ds(pl.multiple_of(first + e * stride, 128), n)

    def slice_rows(k, d=0):
        return pl.multiple_of(((zi + d) % half + half * k) * part, 16)

    def swap_copy(layer, key):
        sem = buf("s_x", layer, key)
        return remote(
            v.gr.at[layer, :, share_cols(key, 1 - s)], buf("xr", layer, key), sem.at[0], sem.at[1], me_x
        )

    def run_copy(layer, key, d, k):
        sem, rs = buf("s_a", layer, key), pl.ds(slice_rows(k, d), part)
        if swaps(layer, key):
            src = buf("xr", layer, key).at[rs]
        else:
            src = v.gr.at[layer, rs, all_cols(key)]
        return remote(src, buf("ar", layer, key).at[d - 1, k], sem.at[0, d, k], sem.at[1, d, k], zpeer(d))

    def run_copies(layer, key):
        return [run_copy(layer, key, d, k) for d in range(1, half) for k in range(2)]

    def cross_copy(layer, key):
        sem = buf("s_b", layer, key)
        return remote(buf("bs", layer, key), buf("br", layer, key), sem.at[0], sem.at[1], me_x)

    def last_copy(layer, key):
        sem = buf("s_c", layer, key)
        return remote(buf("cs", layer, key), buf("cr", layer, key), sem.at[0], sem.at[1], me_o)

    def home_copy(layer, key):
        sem = buf("s_e", layer, key)
        return remote(buf("es", layer, key), buf("er", layer, key), sem.at[0], sem.at[1], me_x)

    def run_sum(layer, key, k, rs):
        own = pl.ds(pl.multiple_of(slice_rows(k) + rs.start, 16), RB)
        if swaps(layer, key):
            tot = buf("xr", layer, key)[own, :].astype(F32)
        else:
            tot = v.gr[layer, own, all_cols(key)].astype(F32)
        for d in range(1, half):
            tot = tot + buf("ar", layer, key)[d - 1, k, rs, :].astype(F32)
        return tot

    def out_of(layer, key, e):
        base = e * shares(key, ff)[2] if swaps(layer, key) else 0
        return dict(d=o_d, u=o_u, o=o_o, q=o_q, k=o_q)[key], base + 256 * (key == "k")

    def give(layer, key):
        if swaps(layer, key):
            swap_copy(layer, key).start()
        else:
            for cp in run_copies(layer, key):
                cp.start()

    def second(layer, key):
        if swaps(layer, key):
            swap_copy(layer, key).wait_recv()
            xr = buf("xr", layer, key)

            def body(rs):
                xr[rs, :] = (v.gr[layer, rs, share_cols(key, s)].astype(F32) + xr[rs, :].astype(F32)).astype(BF)

            row_loop(body, dim)
            for cp in run_copies(layer, key):
                cp.start()
            return

        for cp in run_copies(layer, key):
            cp.wait_recv()

        @pl.when(s != layer)
        def _():
            for k in range(2):

                def body(rs, k=k):
                    buf("bs", layer, key)[k, rs, :] = run_sum(layer, key, k, rs).astype(BF)

                row_loop(body, part)
            cross_copy(layer, key).start()

    def third(layer, key):
        cs = buf("cs", layer, key)
        if swaps(layer, key):
            for cp in run_copies(layer, key):
                cp.wait_recv()

            def body(rs):
                cs[rs, :] = run_sum(layer, key, 1 - g, rs).astype(BF)

            row_loop(body, part)
            last_copy(layer, key).start()
            return

        @pl.when(s == layer)
        def _():
            cross_copy(layer, key).wait_recv()
            br = buf("br", layer, key)

            def body(rs):
                cs[rs, :] = (run_sum(layer, key, 1 - g, rs) + br[1 - g, rs, :].astype(F32)).astype(BF)

            row_loop(body, part)
            last_copy(layer, key).start()

    def fourth(layer, key):
        cr = buf("cr", layer, key)
        out, at = out_of(layer, key, layer)

        @pl.when(s == layer)
        def _():
            last_copy(layer, key).wait_recv()

            def body(rs):
                tot = run_sum(layer, key, g, rs) + cr[rs, :].astype(F32)
                if not swaps(layer, key):
                    tot = tot + buf("br", layer, key)[g, rs, :].astype(F32)
                out[rs, at : at + tot.shape[1]] = tot

            row_loop(body, part)

        if swaps(layer, key):

            @pl.when(s != layer)
            def _():
                last_copy(layer, key).wait_recv()

                def body(rs):
                    tot = run_sum(layer, key, g, rs) + cr[rs, :].astype(F32)
                    buf("es", layer, key)[rs, :] = tot.astype(BF)

                row_loop(body, part)
                home_copy(layer, key).start()

    def fifth(layer, key):
        if swaps(layer, key):
            out, at = out_of(layer, key, 1 - layer)

            @pl.when(s == layer)
            def _():
                home_copy(layer, key).wait_recv()

                def body(rs):
                    got = buf("er", layer, key)[rs, :].astype(F32)
                    out[rs, at : at + got.shape[1]] = got

                row_loop(body, part)

    def grads_close():
        for (layer, key), mode in MODES.items():
            for cp in run_copies(layer, key):
                cp.wait_send()
            if mode == "swap":
                swap_copy(layer, key).wait_send()
                last_copy(layer, key).wait_send()

            @pl.when(s == layer)
            def _(layer=layer, key=key, mode=mode):
                if mode == "run":
                    last_copy(layer, key).wait_send()

            @pl.when(s != layer)
            def _(layer=layer, key=key, mode=mode):
                (home_copy if mode == "swap" else cross_copy)(layer, key).wait_send()

    def rows_of(buf, layer):
        x = buf[layer]
        return x.reshape(full, x.shape[-1])

    stages = (give, second, third, fourth, fifth)
    spots = {
        (1, 0): ("1 1du",),
        (1, 1): ("1 1o",),
        (1, 5): ("2 1du", "1 1q"),
        (1, 2): ("1 1k", "2 1o"),
        (0, 0): ("1 0du",),
        (0, 1): ("1 0o", "2 1qk", "3 1d"),
        (0, 5): ("1 0q", "2 0du", "3 1o"),
        (0, 2): ("1 0k", "2 0o", "2 0q"),
        (0, 3): ("3 0u", "2 0k", "3 0odq", "4 0u", "3 0k", "3 1u", "4 1d", "3 1qk", "4 1uo", "4 0doq", "5 1do"),
        (0, 4): ("5 0uo", "4 0k", "4 1qk"),
    }

    def serve(layer, spot):
        for line in spots.get((layer, spot), ()):
            for key in line[3:]:
                stages[int(line[0]) - 1](int(line[2]), key)

    def back_rows(layer, j, u_buf, r_buf, gain, base, at, extra=None):
        v.stt[...] = jnp.zeros(v.stt.shape, F32)

        def body(rs):
            gsec = sum_rows(j, rs)
            u, r = u_buf[layer, rs, :], r_buf[layer, rs, :]
            gg = gsec * gain
            res = r * (
                gg - jnp.mean(gg, axis=-1, keepdims=True) - u * jnp.mean(gg * u, axis=-1, keepdims=True)
            )
            inn = base[rs, :]
            out = inn + res
            at(rs, out)
            v.stt[0] += gsec * u
            v.stt[1] += gsec
            v.stt[2] += out
            v.stt[3] += inn

        row_loop(body)

    def backward_begin(layer):
        def d_second(hf):
            dgel = nt(v.dyb[layer, hf], v.wdb[layer])
            v.du[hf] = (dgel * v.gp[layer, hf]).astype(BF)
            return nt(v.du[hf], v.wub[layer])

        sum_begin(4 + 2 * (1 - layer), d_second)

    def backward(layer):
        j = 4 + 2 * (1 - layer)
        grad_of(layer, "d", rows_of(v.dyb, layer), rows_of(v.gl, layer))
        grad_of(layer, "u", rows_of(v.sb, layer), v.du[...].reshape(full, ff))
        ones = jnp.ones((8, full), BF)
        v.smo[layer, 6:7, :] = nn(ones, v.du[...].reshape(full, ff))[0:1]
        serve(layer, 0)
        sum_end(j)

        def at_two(rs, out):
            v.dhf[rs, :] = out
            v.dhb[layer, c, rs, :] = out.astype(BF)

        back_rows(layer, j, v.u2, v.r2, prow(layer, 1), v.dyf, at_two)
        share(v.dhb, layer, 4 + layer)
        for i, row in ((0, 1), (1, 3), (2, 4), (3, 5)):
            v.smo[layer, row : row + 1, :] = jnp.sum(v.stt[i], axis=0, keepdims=True)

        def d_att(hf):
            rs = pl.ds(pl.multiple_of(hf * two, 16), two)
            v.dgo[layer, rs, :] = nt(v.dhb[layer, hf], v.wob[layer]).astype(BF)

        d_att(c)
        share_wait(v.dhb, layer, 4 + layer)
        d_att(1 - c)
        dat = v.dgo[layer].astype(F32)
        prod = dat * v.attf[layer]
        tile = dat[:, 0:128]
        for h in range(3):
            real = (lane_f >= 64 * h + 64) & (lane_f < 64 * h + 128)
            delta = jnp.sum(jnp.where(real, prod, 0.0), axis=1, keepdims=True)
            for i, piece in enumerate(splits(-delta)):
                tile = jnp.where(lane == 3 * h + i, piece, tile)
        v.dgo[layer, :, 0:128] = tile.astype(BF)
        group_send(v.dgo.at[layer], v.dg.at[layer, own_b], v.s_ds.at[layer], v.s_dr.at[layer])
        grad_of(layer, "o", rows_of(v.dhb, layer), rows_of(v.attb, layer))
        serve(layer, 1)

        put_masked(v.ma, v.qa[layer], k_mask)
        put_masked(v.mb, v.dgo[layer], v_mask)
        v.dqs[...] = jnp.zeros(v.dqs.shape, F32)

        def query_block(bk, carry):
            build_kv(layer, bk)
            kt, vt = v.kt[...], v.vt[...]
            terms = []
            for h in range(3):
                p = jnp.exp(nt(v.ma[h], kt))
                ds = (p * nt(v.mb[h], vt)).astype(BF)
                terms.append(nn(ds, kt))
            v.dqs[...] += by_head_k(terms)
            return carry

        lax.fori_loop(0, nd, query_block, 0)
        for i in range(2):
            rs = slice(i * two, (i + 1) * two)
            v.gm[i, :, 0:128] = (v.dqs[rs, 0:128] * 0.125).astype(BF)
            v.gm[i, :, 128:256] = jnp.where(lane[rs] < 64, v.dqs[rs, 128:256] * 0.125, 0.0).astype(BF)
        grad_of(layer, "q", rows_of(v.nb, layer), v.gm[:, :, 0:256].reshape(full, 256))
        serve(layer, 5)

        build_kv(layer, own_b)
        put_masked(v.ma, v.kt[...], k_mask)
        put_masked(v.mb, v.vt[...], v_mask)
        v.dks[...] = jnp.zeros(v.dks.shape, F32)
        v.dvs[...] = jnp.zeros(v.dvs.shape, F32)

        def key_block(k, carry):
            zk, sk = (zi + k % half) % half, (s + k // half) % 2
            bk = zk + half * sk
            q_at, d_at = v.qg.at[layer, bk], v.dg.at[layer, bk]
            remote(q_at, q_at, v.s_qs.at[layer, 0], v.s_qr.at[layer, bk], me_x).wait_recv()
            remote(d_at, d_at, v.s_ds.at[layer, 0], v.s_dr.at[layer, bk], me_x).wait_recv()
            if big:
                cps = (
                    pltpu.make_async_copy(q_at, v.kt, v.s_loc.at[0]),
                    pltpu.make_async_copy(d_at, v.vt, v.s_loc.at[1]),
                )
                for cp in cps:
                    cp.start()
                for cp in cps:
                    cp.wait()
                key_terms(v.kt[...], v.vt[...])
            else:
                key_terms(q_at[...], d_at[...])
            return carry

        def key_terms(qt, dt):
            tk, tv = [], []
            for h in range(3):
                p = jnp.exp(nt(v.ma[h], qt))
                ds = (p * nt(v.mb[h], dt)).astype(BF)
                tv.append(nn(p.astype(BF), dt))
                tk.append(nn(ds, qt))
            v.dks[...] += by_head_k(tk)
            v.dvs[...] += by_head_v(tv)

        key_terms(v.qa[layer], v.dgo[layer])
        lax.fori_loop(1, nd, key_block, 0)

        for i in range(2):
            rs = slice(i * two, (i + 1) * two)
            v.gm[i, :, 256:384] = v.dks[rs, 0:128].astype(BF)
            v.gm[i, :, 384:512] = jnp.where(lane[rs] < 64, v.dks[rs, 128:256], v.dvs[rs, 0:128]).astype(BF)
            v.gm[i, :, 512:640] = v.dvs[rs, 128:256].astype(BF)
        sum_begin(j + 1, lambda hf: nn(v.gm[hf], v.wqb[layer]))
        grad_of(layer, "k", rows_of(v.nb, layer), v.gm[:, :, 256:640].reshape(full, 384))
        v.smo[layer, 7:8, :] = jnp.zeros((1, dim), F32)
        v.smo[layer, 7:8, 0:640] = nn(ones, v.gm[...].reshape(full, 640))[0:1]
        serve(layer, 2)
        sum_end(j + 1)

        def at_one(rs, out):
            low = out.astype(BF)
            v.dyf[rs, :] = low.astype(F32)
            if layer == 1:
                v.dyb[0, c, rs, :] = low

        back_rows(layer, j + 1, v.u1, v.r1, prow(layer, 0), v.dhf, at_one)
        for i, row in ((0, 0), (1, 2)):
            v.smo[layer, row : row + 1, :] = jnp.sum(v.stt[i], axis=0, keepdims=True)
        if layer == 1:
            share(v.dyb, 0, 7)
        put_out(2 + layer, layer, v.dyf, igs)

    norm_one(0)
    forward(0)
    forward_end(0)
    red(og, v.gq, 1)
    forward(1)
    red_wait(og, v.gq, 1)
    send(v.gq.at[0], v.gq.at[1], v.s_xy.at[2], v.s_xy.at[3], me_y)
    v.dyf[q_own, :] = v.gq[0].astype(F32)
    remote(v.gq.at[0], v.gq.at[1], v.s_xy.at[2], v.s_xy.at[3], me_y).wait_recv()
    v.dyf[q_oth, :] = v.gq[1].astype(F32)
    v.dyb[1, c] = v.dyf[...].astype(BF)
    share(v.dyb, 1, 6)
    share_wait(v.dyb, 1, 6)
    backward_begin(1)
    forward_end(1)
    backward(1)
    share_wait(v.dyb, 0, 7)
    backward_begin(0)
    backward(0)

    send(v.smo, v.smc, v.s_sm.at[0], v.s_sm.at[1], me_c)
    remote(v.smo, v.smc, v.s_sm.at[0], v.s_sm.at[1], me_c).wait_recv()
    rowid = lax.broadcasted_iota(jnp.int32, (8, dim), 0)
    for layer in range(2):
        v.smc[layer] = v.smo[layer] + jnp.where(rowid < 6, v.smc[layer], 0.0)
    for k in range(1, 2 * nd):
        other = (s * nd + z + k) % (2 * nd)
        so = other // nd
        send(v.smc.at[so], v.smr.at[k - 1], v.s_sms.at[k - 1], v.s_smr.at[k - 1], (so, other % nd, t))
    serve(0, 3)
    for k in range(1, 2 * nd):
        remote(v.smr.at[0], v.smr.at[k - 1], v.s_sms.at[k - 1], v.s_smr.at[k - 1], me_x).wait_recv()
    tot = v.smc[s]
    for k in range(1, 2 * nd):
        tot = tot + v.smr[k - 1]
    o_s[...] = tot
    serve(0, 4)

    for cp in late:
        cp.wait_send()

    grads_close()
    for i, src, dst in ((0, fr, v.xq), (1, og, v.gq)):

        @pl.when(keeps)
        def _(i=i, src=src, dst=dst):
            remote(src.at[1 - g], dst.at[0], v.s_red.at[i], v.s_red.at[2 + i], me_o).wait_send()

    for i in range(4):
        forward_w_end(i)
    put_out_wait(0, 0, acts)
    put_out_wait(1, 1, acts)
    put_out_wait(2, 0, igs)
    put_out_wait(3, 1, igs)


def lay_out(nd, a_in, i_in, q_in, u_in, o_in, d_in, sums, acts, igs, g_q, bias, g_o, g_u, upb, g_d, gain, shift, sq):
    for src, dst in ((a_in, acts), (i_in, igs), (u_in, g_u), (d_in, g_d)):
        dst[...] = src[...]
    z, t = lax.axis_index("dp"), lax.axis_index("tensor")
    part, dim = u_in.shape[0], sums.shape[1]
    hl = g_q.shape[2]
    heads, _, hw = bias.shape
    g_q[0] = q_in[:, 0:hl]
    g_q[1] = q_in[:, 256 : 256 + hl]
    g_q[2] = pltpu.roll(q_in[:, 384:640], 192, 1)[:, 0:hl]
    sq[0:part, :] = o_in[...]
    g_o[...] = sq[...].T[64 : 64 + hl, 0:part]

    def from_lane(lo, n):
        return pltpu.roll(sums[...], (dim - lo) % dim, 1)[:, 0:n]

    for h in range(heads):
        bias[h, 0:1, :] = from_lane(h * HD + z * hw, hw)[7:8]
        bias[h, 1:2, :] = from_lane(256 + hl + h * HD + z * hw, hw)[7:8]
        uw = upb.shape[2]
        upb[h] = from_lane((h * nd + z) * uw, uw)[6:7]
    norms = from_lane((z * 4 + t) * gain.shape[1], gain.shape[1])
    gain[...] = norms[0:2]
    shift[...] = norms[2:6]


def local(frames, out_grad, clip_ids, w_qkv, bias_qv, w_out, w_up, bias_up, w_down, ln_gain, shifts):
    rows, dim = frames.shape[1:]
    nd = lax.axis_size("dp")
    half = nd // 2
    z, t, s = lax.axis_index("dp"), lax.axis_index("tensor"), lax.axis_index("section")
    hl = w_qkv.shape[3]
    ff = w_up.shape[2]
    part = dim // nd
    wide = w_qkv[0].transpose(1, 2, 0).reshape(3 * hl, dim)
    clip = lax.dynamic_index_in_dim(clip_ids, z // half, 0, keepdims=False)
    clip = clip.reshape(nd, 4, rows)
    clip = jnp.stack([clip[:, 0], clip[:, 2], clip[:, 1], clip[:, 3]], axis=1).reshape(nd, 4 * rows)
    lane = jnp.arange(128)
    same = clip[:, :, None] == (lane - 80)[None, None, :]
    spot = lane >= 80
    k_feat = jnp.where(
        (lane >= 64) & (lane < 73), 1.0, jnp.where(spot & jnp.logical_not(same), -BIG, 0.0)
    ).astype(BF)
    plan = scratch_plan(nd, rows, dim, hl, ff)
    shape = jax.ShapeDtypeStruct
    anyspec = pl.BlockSpec(memory_space=pl.ANY)
    vspec = pl.BlockSpec(memory_space=pltpu.VMEM)
    gathered = {name: (2, nd, 4 * rows, 256) for name in ("qg", "dg")}
    big = nd > MOST
    if not big:
        plan.update({name: pltpu.VMEM(dims, BF) for name, dims in gathered.items()})
    outs = pl.pallas_call(
        functools.partial(mega, nd, (*gathered, *plan) if big else tuple(plan)),
        out_shape=(
            shape((2, rows, dim), BF),
            shape((2, rows, dim), BF),
            shape((part, 640), F32),
            shape((part, ff), F32),
            shape((part, 256), F32),
            shape((part, ff), F32),
            shape((8, dim), F32),
        )
        + tuple(shape(dims, BF) for dims in gathered.values()) * big,
        in_specs=[anyspec] * 6 + [vspec] * 5,
        out_specs=(anyspec,) * 2 + (vspec,) * 5 + (anyspec,) * (2 * big),
        scratch_shapes=list(plan.values()),
        compiler_params=pltpu.CompilerParams(
            collective_id=0, has_side_effects=True, vmem_limit_bytes=63 * 1024 * 1024
        ),
    )(frames, out_grad, wide, w_out[0], w_up[0], w_down[0], ln_gain[0], shifts[0], bias_up, bias_qv[0], k_feat)

    own, hw, uw = dim // (4 * nd), HD // nd, ff // (hl // HD) // nd
    heads = hl // HD
    acts, igs, g_q, bias, g_o, g_u, upb, g_d, gain, shift = pl.pallas_call(
        functools.partial(lay_out, nd),
        out_shape=(
            shape((2, rows, dim), BF),
            shape((2, rows, dim), BF),
            shape((3, part, hl), F32),
            shape((heads, 2, hw), F32),
            shape((hl, part), F32),
            shape((part, ff), F32),
            shape((heads, 1, uw), F32),
            shape((part, ff), F32),
            shape((2, own), F32),
            shape((4, own), F32),
        ),
        in_specs=[vspec] * 7,
        out_specs=(vspec,) * 10,
        scratch_shapes=[pltpu.VMEM((256, 256), F32)],
    )(*outs[:7])
    return (
        acts[None],
        igs[None],
        g_q.transpose(1, 0, 2)[None],
        bias.transpose(1, 0, 2)[None],
        g_o[None],
        g_u[None],
        upb.transpose(1, 0, 2),
        g_d.T[None],
        gain[None],
        shift[None],
    )


def solution(mesh):
    in_specs = (
        P(None, ("dp", "tensor"), None),
        P(None, ("dp", "tensor"), None),
        P(),
        P("section", None, None, "tensor"),
        P("section", None, "tensor"),
        P("section", "tensor", None),
        P("section", None, "tensor"),
        P("section", "tensor"),
        P("section", "tensor", None),
        P("section", None, None),
        P("section", None, None),
    )
    out_specs = (
        P("section", None, ("dp", "tensor"), None),
        P("section", None, ("dp", "tensor"), None),
        P("section", "dp", None, "tensor"),
        P("section", None, "tensor", "dp"),
        P("section", "tensor", "dp"),
        P("section", "dp", "tensor"),
        P("section", "tensor", "dp"),
        P("section", "tensor", "dp"),
        P("section", None, ("dp", "tensor")),
        P("section", None, ("dp", "tensor")),
    )
    return jax.shard_map(local, mesh=mesh, in_specs=in_specs, out_specs=out_specs, check_vma=False)
```

```python
import functools

import jax
import jax.numpy as jnp
from jax import lax
from jax.experimental import pallas as pl
from jax.experimental.pallas import tpu as pltpu
from jax.sharding import PartitionSpec as P

HD = 64
BIG = 2.0**100
MESH = pl.DeviceIdType.MESH
BF = jnp.bfloat16
F32 = jnp.float32
RB = 16
SLOTS = 4
MOST = 4


def nt(a, b):
    return lax.dot_general(a, b, (((1,), (1,)), ((), ())), preferred_element_type=F32)


def nn(a, b):
    return lax.dot_general(a, b, (((1,), (0,)), ((), ())), preferred_element_type=F32)


def tn(a, b):
    return lax.dot_general(a, b, (((0,), (0,)), ((), ())), preferred_element_type=F32)


def shares(key, ff):
    return {
        "d": (0, ff, ff // 2, ff // 2),
        "u": (ff, ff, ff // 2, ff // 2),
        "o": (2 * ff, 256, 128, 128),
        "q": (2 * ff + 256, 256, 128, 128),
        "k": (2 * ff + 512, 384, 0, 0),
    }[key]


MODES = {
    (1, "d"): "swap",
    (1, "u"): "run",
    (1, "o"): "swap",
    (1, "q"): "run",
    (1, "k"): "run",
    (0, "d"): "run",
    (0, "u"): "swap",
    (0, "o"): "swap",
    (0, "q"): "run",
    (0, "k"): "run",
}


def scratch_plan(nd, rows, dim, head_dim, ff):
    half = nd // 2
    full = 4 * rows
    two = 2 * rows
    part = dim // nd
    wide = 640 + ff + 256 + ff
    vm = pltpu.VMEM
    dma = pltpu.SemaphoreType.DMA
    plan = dict(
        wqb=vm((2, 640, dim), BF),
        wob=vm((2, 256, dim), BF),
        wub=vm((2, dim, ff), BF),
        wdb=vm((2, ff, dim), BF),
        spb=vm((2, 16, dim), F32),
        xq=vm((2, rows, dim), BF),
        gq=vm((2, rows, dim), BF),
        xres=vm((two, dim), F32),
        dyf=vm((two, dim), F32),
        dyb=vm((2, 2, two, dim), BF),
        nb=vm((2, 2, two, dim), BF),
        sb=vm((2, 2, two, dim), BF),
        hid=vm((two, dim), F32),
        u1=vm((2, two, dim), F32),
        u2=vm((2, two, dim), F32),
        r1=vm((2, two, 1), F32),
        r2=vm((2, two, 1), F32),
        qa=vm((2, full, 256), BF),
        kvb=vm((2, nd, full, 384), BF),
        kt=vm((full, 256), BF),
        vt=vm((full, 256), BF),
        dgo=vm((2, full, 256), BF),
        mst=vm((3, full, 1), F32),
        lst=vm((3, full, 1), F32),
        attf=vm((2, full, 256), F32),
        attb=vm((2, 2, two, 256), BF),
        gl=vm((2, 2, two, ff), BF),
        gp=vm((2, 2, two, ff), F32),
        du=vm((2, two, ff), BF),
        dhb=vm((2, 2, two, dim), BF),
        dhf=vm((two, dim), F32),
        gm=vm((2, two, 640), BF),
        ma=vm((3, full, 256), BF),
        mb=vm((3, full, 256), BF),
        dqs=vm((full, 256), F32),
        dks=vm((full, 256), F32),
        dvs=vm((full, 256), F32),
        cs=vm((two, dim), BF),
        cr=vm((SLOTS, two, dim), BF),
        ys=vm((2, two, dim), BF),
        yr=vm((SLOTS, two, dim), BF),
        chip=vm((2, two, dim), F32),
        gr=vm((2, dim, wide), BF),
        smo=vm((2, 8, dim), F32),
        smc=vm((2, 8, dim), F32),
        smr=vm((2 * nd - 1, 8, dim), F32),
        stt=vm((6, RB, dim), F32),
        oq=vm((4, rows, dim), BF),
        s_loc=dma((12,)),
        s_red=dma((4,)),
        s_xy=dma((4,)),
        s_wx=dma((2, 13)),
        s_wzs=dma((12, half)),
        s_wzr=dma((12, half)),
        s_ag=dma((2, 8)),
        s_cc=dma((2, SLOTS)),
        s_yy=dma((2, SLOTS, 2)),
        s_kvs=dma((2, nd, 2)),
        s_kvr=dma((2, nd, 2)),
        s_qs=dma((2, nd)),
        s_qr=dma((2, nd)),
        s_ds=dma((2, nd)),
        s_dr=dma((2, nd)),
        s_sm=dma((2,)),
        s_sms=dma((2 * nd - 1,)),
        s_smr=dma((2 * nd - 1,)),
        s_out=dma((4, 3)),
    )
    for (layer, key), mode in MODES.items():
        n = shares(key, ff)[1 if mode == "run" else 3]
        tag = f"{layer}{key}"
        if mode == "swap":
            plan["xr" + tag] = vm((dim, n), BF)
            plan["s_x" + tag] = dma((2,))
        else:
            plan["bs" + tag] = vm((2, part, n), BF)
            plan["br" + tag] = vm((2, part, n), BF)
            plan["s_b" + tag] = dma((2,))
        plan["ar" + tag] = vm((half - 1, 2, part, n), BF)
        plan["s_a" + tag] = dma((2, half, 2))
        plan["cs" + tag] = vm((part, n), BF)
        plan["cr" + tag] = vm((part, n), BF)
        plan["s_c" + tag] = dma((2,))
        if mode == "swap":
            plan["es" + tag] = vm((part, n), BF)
            plan["er" + tag] = vm((part, n), BF)
            plan["s_e" + tag] = dma((2,))
    return plan


def mega(nd, names, *refs):
    (fr, og, wq, wo, wu, wd, gains, moves, bup, bqv, kf) = refs[:11]
    (acts, igs, o_q, o_u, o_o, o_d, o_s) = refs[11:18]
    b_ = dict(zip(names, refs[18:]))
    big = nd > MOST

    class Bufs:
        pass

    v = Bufs()
    v.__dict__.update(b_)
    half = nd // 2
    rows, dim = fr.shape[1:]
    two, full = 2 * rows, 4 * rows
    ff = wu.shape[1]
    part = dim // nd
    s = lax.axis_index("section")
    z = lax.axis_index("dp")
    t = lax.axis_index("tensor")
    g, zi = z // half, z % half
    c, y = t % 2, t // 2
    own_b = zi + half * s
    zo = (z + half) % nd
    me_x = (1 - s, z, t)
    me_c = (s, z, t + 1 - 2 * c)
    me_y = (s, z, (t + 2) % 4)
    me_o = (s, zo, t)

    def zpeer(d):
        return (s, g * half + (zi + d) % half, t)

    def member(k):
        zk, sk = (zi + k % half) % half, (s + k // half) % 2
        return (sk, g * half + zk, t), zk + half * sk

    def remote(src, dst, ss, rs, dev):
        return pltpu.make_async_remote_copy(
            src_ref=src, dst_ref=dst, send_sem=ss, recv_sem=rs, device_id=dev, device_id_type=MESH
        )

    late = []

    def send(src, dst, ss, rs, dev):
        cp = remote(src, dst, ss, rs, dev)
        cp.start()
        late.append(cp)
        return cp

    loads = [
        pltpu.make_async_copy(wq.at[pl.ds(0, 192)], v.wqb.at[s, pl.ds(0, 192)], v.s_loc.at[0]),
        pltpu.make_async_copy(wq.at[pl.ds(192, 384)], v.wqb.at[s, pl.ds(256, 384)], v.s_loc.at[1]),
        pltpu.make_async_copy(wo, v.wob.at[s, pl.ds(64, 192)], v.s_loc.at[2]),
        pltpu.make_async_copy(wu, v.wub.at[s], v.s_loc.at[3]),
        pltpu.make_async_copy(wd, v.wdb.at[s], v.s_loc.at[4]),
    ]
    for cp in loads:
        cp.start()
    v.wqb[s, pl.ds(192, 64), :] = jnp.zeros((64, dim), BF)
    v.wob[s, pl.ds(0, 64), :] = jnp.zeros((64, dim), BF)
    hl = bqv.shape[1]
    v.spb[s, 0:2, :] = gains[...].astype(F32)
    v.spb[s, 2:6, :] = moves[...].astype(F32)
    v.spb[s, 6:7, :] = bup[...].astype(F32)
    v.spb[s, 7:16, :] = jnp.zeros((9, dim), F32)
    v.spb[s, 7:9, 0:hl] = bqv[...].astype(F32)
    v.spb[s, 8:16, :] = pltpu.roll(v.spb[s, 8:16, :], hl, 1)

    barrier = pltpu.get_barrier_semaphore()
    for k in range(1, 2 * nd):
        other = (s * nd + z + k) % (2 * nd)
        pl.semaphore_signal(barrier, inc=1, device_id=(other // nd, other % nd, t), device_id_type=MESH)
    for dev in (me_c, me_y):
        pl.semaphore_signal(barrier, inc=1, device_id=dev, device_id_type=MESH)
    pl.semaphore_wait(barrier, 2 * nd + 1)

    keeps = g == s

    def red(src, dst, i):
        @pl.when(keeps)
        def _():
            pltpu.make_async_copy(src.at[g], dst.at[0], v.s_loc.at[6 + i]).start()
            remote(src.at[1 - g], dst.at[0], v.s_red.at[i], v.s_red.at[2 + i], me_o).start()

    def red_wait(src, dst, i):
        @pl.when(keeps)
        def _():
            pltpu.make_async_copy(src.at[g], dst.at[0], v.s_loc.at[6 + i]).wait()

        @pl.when(jnp.logical_not(keeps))
        def _():
            remote(src.at[1 - g], dst.at[0], v.s_red.at[i], v.s_red.at[2 + i], me_o).wait_recv()

    red(fr, v.xq, 0)
    for cp in loads[:2]:
        cp.wait()
    mats = (v.wqb, v.wob, v.wub, v.wdb)

    def w_parts(i):
        n = (2, 2, 2, 3)[i]
        return n if mats[i].shape[1] // half % (16 * n) == 0 else 1

    def straight(i, e):
        return i == 3 and e == 2

    def w_rows(i, p, e):
        n = mats[i].shape[1] // half
        m = n // w_parts(i)
        return pl.ds(pl.multiple_of(p * n + e * m, 16), m)

    def ship(i):
        for e in range(w_parts(i)):
            src = mats[i].at[s, w_rows(i, zi, e)]
            send(src, src, v.s_wx.at[0, 3 * i + e], v.s_wx.at[1, 3 * i + e], me_x)
        for e in range(w_parts(i)):
            for d in range(1, half) if straight(i, e) else ():
                src = mats[i].at[s, w_rows(i, (zi + half - d) % half, e)]
                remote(src, src, v.s_wzs.at[3 * i + e, d], v.s_wzr.at[3 * i + e, d], me_x).start()

    send(v.spb.at[s], v.spb.at[s], v.s_wx.at[0, 12], v.s_wx.at[1, 12], me_x)
    ship(0)
    loads[2].wait()
    ship(1)
    loads[3].wait()
    ship(2)
    loads[4].wait()

    def w_copy(i, e, d, back=0):
        src = mats[i].at[1 - s, w_rows(i, (zi + back) % half, e)]
        return remote(src, src, v.s_wzs.at[3 * i + e, d], v.s_wzr.at[3 * i + e, d], zpeer(d))

    def forward_w(i, e=None):
        for e in range(w_parts(i)) if e is None else (e,):
            if e < w_parts(i):
                src = mats[i].at[1 - s, w_rows(i, zi, e)]
                remote(src, src, v.s_wx.at[0, 3 * i + e], v.s_wx.at[1, 3 * i + e], me_x).wait_recv()
                for d in () if straight(i, e) else range(1, half):
                    w_copy(i, e, d).start()

    def forward_w_end(i):
        for e in range(w_parts(i)):
            for d in range(1, half):
                w_copy(i, e, d).wait_send()

    def gather_w(i, layer):
        @pl.when(s != layer)
        def _():
            for e in range(w_parts(i)):
                for d in range(1, half):
                    w_copy(i, e, d, half - d).wait_recv()

    red_wait(fr, v.xq, 0)
    send(v.xq.at[0], v.xq.at[1], v.s_xy.at[0], v.s_xy.at[1], me_y)
    remote(v.spb.at[s], v.spb.at[s], v.s_wx.at[0, 12], v.s_wx.at[1, 12], me_x).wait_recv()
    q_own = pl.ds(pl.multiple_of(rows * y, 8), rows)
    q_oth = pl.ds(pl.multiple_of(rows * (1 - y), 8), rows)
    v.xres[q_own, :] = v.xq[0].astype(F32)
    forward_w(0, 0)
    remote(v.xq.at[0], v.xq.at[1], v.s_xy.at[0], v.s_xy.at[1], me_y).wait_recv()
    v.xres[q_oth, :] = v.xq[1].astype(F32)

    def prow(layer, i):
        return v.spb[layer, i : i + 1, :]

    def row_loop(fn, n=two, first=0):
        def step(i, carry):
            fn(pl.ds(pl.multiple_of(i * RB, RB), RB))
            return carry

        count = n // RB - first // RB
        lax.fori_loop(first // RB, n // RB, step, 0, unroll=count if n <= two else 4)

    def unit(x):
        cen = x - jnp.mean(x, axis=-1, keepdims=True)
        r = lax.rsqrt(jnp.mean(cen * cen, axis=-1, keepdims=True) + 1e-05)
        return cen * r, r

    def share(buf, layer, i):
        src = buf.at[layer, c]
        send(src, src, v.s_ag.at[0, i], v.s_ag.at[1, i], me_c)

    def share_wait(buf, layer, i):
        src = buf.at[layer, 1 - c]
        remote(src, src, v.s_ag.at[0, i], v.s_ag.at[1, i], me_c).wait_recv()

    def norm_one(layer):
        gain, shift = prow(layer, 0), prow(layer, 2)

        def body(rs):
            u, r = unit(v.xres[rs, :])
            v.u1[layer, rs, :] = u
            v.r1[layer, rs, :] = r
            v.nb[layer, c, rs, :] = (u * gain + shift).astype(BF)

        row_loop(body)
        share(v.nb, layer, layer)

    def sum_begin(j, term):
        k = j % SLOTS
        v.cs[...] = term(1 - c).astype(BF)
        cp = remote(v.cs, v.cr.at[k], v.s_cc.at[0, k], v.s_cc.at[1, k], me_c)
        cp.start()
        v.chip[j % 2] = term(c)
        cp.wait()

        def body(rs):
            tot = v.chip[j % 2, rs, :] + v.cr[k, rs, :].astype(F32)
            v.chip[j % 2, rs, :] = tot
            v.ys[j % 2, rs, :] = tot.astype(BF)

        for e in range(2):
            row_loop(body, cuts[e + 1], cuts[e])
            chip_copy(j, e).start()

    cuts = (0, (two // RB + 1) // 2 * RB, two)

    def chip_copy(j, e):
        k, rs = j % SLOTS, pl.ds(cuts[e], cuts[e + 1] - cuts[e])
        return remote(
            v.ys.at[j % 2, rs], v.yr.at[k, rs], v.s_yy.at[0, k, e], v.s_yy.at[1, k, e], me_y
        )

    def sum_end(j, body):
        for e in range(2):
            chip_copy(j, e).wait()
            row_loop(body, cuts[e + 1], cuts[e])

    def sum_rows(j, rs):
        k = j % SLOTS
        return v.chip[j % 2, rs, :] + v.yr[k, rs, :].astype(F32)

    lane_f = lax.broadcasted_iota(jnp.int32, (full, 256), 1)
    lane = lax.broadcasted_iota(jnp.int32, (full, 128), 1)

    def k_mask(h):
        return (
            ((lane_f >= 64 * h) & (lane_f < 64 * h + 64))
            | ((lane_f >= 192 + 3 * h) & (lane_f < 195 + 3 * h))
            | (lane_f >= 208)
        )

    def v_mask(h):
        return ((lane_f >= 64 * h + 64) & (lane_f < 64 * h + 128)) | (
            (lane_f >= 3 * h) & (lane_f < 3 * h + 3)
        )

    def by_head_k(a):
        return jnp.where(lane_f < 64, a[0], jnp.where(lane_f < 128, a[1], a[2]))

    def by_head_v(a):
        return jnp.where(lane_f < 128, a[0], jnp.where(lane_f < 192, a[1], a[2]))

    def put_masked(dst, val, mask):
        val = val.astype(F32)
        for h in range(3):
            dst[h] = jnp.where(mask(h), val, 0.0).astype(BF)

    def build_kv(layer, bk):
        v.kt[:, 0:128] = v.kvb[layer, bk, :, 0:128]
        mid = v.kvb[layer, bk, :, 128:256].astype(F32)
        v.kt[:, 128:256] = jnp.where(lane < 64, mid, kf[bk].astype(F32)).astype(BF)
        v.vt[:, 0:128] = jnp.where(lane < 64, jnp.where(lane < 9, 1.0, 0.0), mid).astype(BF)
        v.vt[:, 128:256] = v.kvb[layer, bk, :, 256:384]

    def splits(x):
        hi = x.astype(BF).astype(F32)
        mid = (x - hi).astype(BF).astype(F32)
        return hi, mid, (x - hi) - mid

    def group_send(src, dst, ss, rs):
        for k in range(1, nd):
            dev, _ = member(k)
            send(src, dst, ss.at[k], rs.at[own_b], dev)

    def group_wait(buf, layer, rs, k, ss):
        dev, bk = member(k)
        dst = buf.at[layer, bk]
        remote(dst, dst, ss.at[0], rs.at[bk], dev).wait_recv()

    halves = (lambda i: c, lambda i: 1 - c)

    def forward(layer):
        bias_q, bias_kv = v.spb[layer, 7:8, 0:256], v.spb[layer, 8:9, 0:384]

        def qkv(hf):
            r = nt(v.nb[layer, hf], v.wqb[layer])
            rs = pl.ds(pl.multiple_of(hf * two, 16), two)
            q = (r[:, 0:256] + bias_q).astype(BF).astype(F32) * 0.125
            v.qa[layer, rs, 0:128] = q[:, 0:128].astype(BF)
            clip = kf[own_b, rs, :].astype(F32) * (1.0 / BIG) + 1.0
            clip = jnp.where(lane[0:two] >= 80, clip, 0.0)
            v.qa[layer, rs, 128:256] = (q[:, 128:256] + clip).astype(BF)
            v.kvb[layer, own_b, rs, :] = (r[:, 256:640] + bias_kv).astype(BF)

        if layer == 0:
            forward_w(0, 1)
        gather_w(0, layer)
        if layer == 0:
            forward_w(1)
        def kv_send(hf):
            src = v.kvb.at[layer, own_b, pl.ds(pl.multiple_of(hf * two, 16), two)]
            for k in range(1, nd):
                send(src, src, v.s_kvs.at[layer, k, hf], v.s_kvr.at[layer, own_b, hf], member(k)[0])

        qkv(c)
        kv_send(c)
        share_wait(v.nb, layer, layer)
        qkv(1 - c)
        kv_send(1 - c)

        put_masked(v.ma, v.qa[layer], k_mask)
        v.mst[...] = jnp.full(v.mst.shape, -3e38, F32)
        v.lst[...] = jnp.zeros(v.lst.shape, F32)
        v.dqs[...] = jnp.zeros(v.dqs.shape, F32)

        def block(k, carry):
            zk, sk = (zi + k % half) % half, (s + k // half) % 2
            bk = zk + half * sk

            @pl.when(k > 0)
            def _():
                for e in range(2):
                    dst = v.kvb.at[layer, bk, pl.ds(e * two, two)]
                    remote(dst, dst, v.s_kvs.at[layer, 0, e], v.s_kvr.at[layer, bk, e], me_x).wait_recv()

            if layer == 0:

                @pl.when(k == 1)
                def _():
                    forward_w(2)

            build_kv(layer, bk)
            kt, vt = v.kt[...], v.vt[...]
            alphas, news = [], []
            for h in range(3):
                sc = nt(v.ma[h], kt)
                old = v.mst[h]
                new = jnp.maximum(old, jnp.max(sc, axis=1, keepdims=True))
                alpha = jnp.exp(old - new)
                p = jnp.exp(sc - new)
                v.mst[h] = new
                v.lst[h] = v.lst[h] * alpha + jnp.sum(p, axis=1, keepdims=True)
                hi = p.astype(BF)
                lo = (p - hi.astype(F32)).astype(BF)
                news.append(nn(hi, vt) + nn(lo, vt))
                alphas.append(alpha)
            v.dqs[...] = v.dqs[...] * by_head_v(alphas) + by_head_v(news)
            return carry

        block(0, 0)
        if layer == 0:
            ship(3)
        lax.fori_loop(1, nd, block, 0)

        att = v.dqs[...] * by_head_v([1.0 / v.lst[h] for h in range(3)])
        v.attf[layer] = att
        v.attb[layer] = att.astype(BF).reshape(2, two, 256)
        tile = v.qa[layer, :, 128:256].astype(F32)
        for h in range(3):
            for i, piece in enumerate(splits(-(v.mst[h] + jnp.log(v.lst[h])))):
                tile = jnp.where(lane == 64 + 3 * h + i, piece, tile)
        v.qa[layer, :, 128:256] = tile.astype(BF)
        gather_w(1, layer)
        sum_begin(2 * layer, lambda hf: nn(v.attb[layer, hf], v.wob[layer]))
        if layer == 1:
            for one in (1, 0):
                group_send(v.qa.at[one], v.qg.at[one, own_b], v.s_qs.at[one], v.s_qr.at[one])
        if layer == 0:
            forward_w(3, 0)
        out_bias, gain2, shift2 = prow(layer, 4), prow(layer, 1), prow(layer, 3)

        def body(rs):
            hid = v.xres[rs, :] + sum_rows(2 * layer, rs) + out_bias
            v.hid[rs, :] = hid
            u, r = unit(hid)
            v.u2[layer, rs, :] = u
            v.r2[layer, rs, :] = r
            v.sb[layer, c, rs, :] = (u * gain2 + shift2).astype(BF)

        sum_end(2 * layer, body)
        share(v.sb, layer, 2 + layer)
        if layer == 0:
            forward_w(3, 1)
            forward_w(3, 2)
        gather_w(2, layer)
        bias_up = prow(layer, 6)

        def up(hf):
            v.gp[layer, hf] = nn(v.sb[layer, hf], v.wub[layer]) + bias_up

            def gelu(rs):
                u = v.gp[layer, hf, rs, :]
                phi = 0.5 * (1.0 + lax.erf(u * 0.7071067811865476))
                v.gl[layer, hf, rs, :] = (u * phi).astype(BF)
                v.gp[layer, hf, rs, :] = phi + u * (jnp.exp(-0.5 * u * u) * 0.3989422804014327)

            row_loop(gelu)

        up(c)
        share_wait(v.sb, layer, 2 + layer)
        up(1 - c)
        gather_w(3, layer)
        sum_begin(2 * layer + 1, lambda hf: nn(v.gl[layer, hf], v.wdb[layer]))

    def forward_end(layer):
        out_bias = prow(layer, 5)

        def body(rs):
            out = v.hid[rs, :] + sum_rows(2 * layer + 1, rs) + out_bias
            v.xres[rs, :] = out.astype(BF).astype(F32)

        sum_end(2 * layer + 1, body)
        if layer == 0:
            norm_one(1)
        put_out(layer, layer, v.xres, acts)

    def put_out(i, layer, src, dst):
        v.oq[i] = src[q_own, :].astype(BF)
        here = keeps & (s == layer)

        @pl.when(here)
        def _():
            pltpu.make_async_copy(v.oq.at[i], dst.at[g], v.s_loc.at[8 + i]).start()

        @pl.when(jnp.logical_not(here))
        def _():
            remote(v.oq.at[i], dst.at[g], v.s_out.at[i, 0], v.s_out.at[i, 1 + g], (layer, own_b, t)).start()

    def put_out_wait(i, layer, dst):
        here = keeps & (s == layer)

        @pl.when(here)
        def _():
            pltpu.make_async_copy(v.oq.at[i], dst.at[g], v.s_loc.at[8 + i]).wait()

        @pl.when(jnp.logical_not(here))
        def _():
            remote(v.oq.at[i], dst.at[g], v.s_out.at[i, 0], v.s_out.at[i, 1 + g], (layer, own_b, t)).wait_send()

        @pl.when(s == layer)
        def _():
            def got(m):
                remote(v.oq.at[i], dst.at[m], v.s_out.at[i, 0], v.s_out.at[i, 1 + m], me_x).wait_recv()

            got(1 - g)

            @pl.when(g != s)
            def _():
                got(g)

    def grad_of(layer, key, left, right):
        first, n = shares(key, ff)[:2]
        for i in range(dim // 256):
            lo = i * 256
            v.gr[layer, lo : lo + 256, first : first + n] = tn(left[:, lo : lo + 256], right).astype(BF)

    def buf(name, layer, key):
        return b_[f"{name}{layer}{key}"]

    def swaps(layer, key):
        return MODES[layer, key] == "swap"

    def all_cols(key):
        return pl.ds(*shares(key, ff)[:2])

    def share_cols(key, e):
        first, _, stride, n = shares(key, ff)
        return pl.ds(pl.multiple_of(first + e * stride, 128), n)

    def slice_rows(k, d=0):
        return pl.multiple_of(((zi + d) % half + half * k) * part, 16)

    def swap_copy(layer, key):
        sem = buf("s_x", layer, key)
        return remote(
            v.gr.at[layer, :, share_cols(key, 1 - s)], buf("xr", layer, key), sem.at[0], sem.at[1], me_x
        )

    def run_copy(layer, key, d, k):
        sem, rs = buf("s_a", layer, key), pl.ds(slice_rows(k, d), part)
        if swaps(layer, key):
            src = buf("xr", layer, key).at[rs]
        else:
            src = v.gr.at[layer, rs, all_cols(key)]
        return remote(src, buf("ar", layer, key).at[d - 1, k], sem.at[0, d, k], sem.at[1, d, k], zpeer(d))

    def run_copies(layer, key):
        return [run_copy(layer, key, d, k) for d in range(1, half) for k in range(2)]

    def cross_copy(layer, key):
        sem = buf("s_b", layer, key)
        return remote(buf("bs", layer, key), buf("br", layer, key), sem.at[0], sem.at[1], me_x)

    def last_copy(layer, key):
        sem = buf("s_c", layer, key)
        return remote(buf("cs", layer, key), buf("cr", layer, key), sem.at[0], sem.at[1], me_o)

    def home_copy(layer, key):
        sem = buf("s_e", layer, key)
        return remote(buf("es", layer, key), buf("er", layer, key), sem.at[0], sem.at[1], me_x)

    def run_sum(layer, key, k, rs):
        own = pl.ds(pl.multiple_of(slice_rows(k) + rs.start, 16), RB)
        if swaps(layer, key):
            tot = buf("xr", layer, key)[own, :].astype(F32)
        else:
            tot = v.gr[layer, own, all_cols(key)].astype(F32)
        for d in range(1, half):
            tot = tot + buf("ar", layer, key)[d - 1, k, rs, :].astype(F32)
        return tot

    def out_of(layer, key, e):
        base = e * shares(key, ff)[2] if swaps(layer, key) else 0
        return dict(d=o_d, u=o_u, o=o_o, q=o_q, k=o_q)[key], base + 256 * (key == "k")

    def give(layer, key):
        if swaps(layer, key):
            swap_copy(layer, key).start()
        else:
            for cp in run_copies(layer, key):
                cp.start()

    def second(layer, key):
        if swaps(layer, key):
            swap_copy(layer, key).wait_recv()
            xr = buf("xr", layer, key)

            def body(rs):
                xr[rs, :] = (v.gr[layer, rs, share_cols(key, s)].astype(F32) + xr[rs, :].astype(F32)).astype(BF)

            row_loop(body, dim)
            for cp in run_copies(layer, key):
                cp.start()
            return

        for cp in run_copies(layer, key):
            cp.wait_recv()

        @pl.when(s != layer)
        def _():
            for k in range(2):

                def body(rs, k=k):
                    buf("bs", layer, key)[k, rs, :] = run_sum(layer, key, k, rs).astype(BF)

                row_loop(body, part)
            cross_copy(layer, key).start()

    def third(layer, key):
        cs = buf("cs", layer, key)
        if swaps(layer, key):
            for cp in run_copies(layer, key):
                cp.wait_recv()

            def body(rs):
                cs[rs, :] = run_sum(layer, key, 1 - g, rs).astype(BF)

            row_loop(body, part)
            last_copy(layer, key).start()
            return

        @pl.when(s == layer)
        def _():
            cross_copy(layer, key).wait_recv()
            br = buf("br", layer, key)

            def body(rs):
                cs[rs, :] = (run_sum(layer, key, 1 - g, rs) + br[1 - g, rs, :].astype(F32)).astype(BF)

            row_loop(body, part)
            last_copy(layer, key).start()

    def fourth(layer, key):
        cr = buf("cr", layer, key)
        out, at = out_of(layer, key, layer)

        @pl.when(s == layer)
        def _():
            last_copy(layer, key).wait_recv()

            def body(rs):
                tot = run_sum(layer, key, g, rs) + cr[rs, :].astype(F32)
                if not swaps(layer, key):
                    tot = tot + buf("br", layer, key)[g, rs, :].astype(F32)
                out[rs, at : at + tot.shape[1]] = tot

            row_loop(body, part)

        if swaps(layer, key):

            @pl.when(s != layer)
            def _():
                last_copy(layer, key).wait_recv()

                def body(rs):
                    tot = run_sum(layer, key, g, rs) + cr[rs, :].astype(F32)
                    buf("es", layer, key)[rs, :] = tot.astype(BF)

                row_loop(body, part)
                home_copy(layer, key).start()

    def fifth(layer, key):
        if swaps(layer, key):
            out, at = out_of(layer, key, 1 - layer)

            @pl.when(s == layer)
            def _():
                home_copy(layer, key).wait_recv()

                def body(rs):
                    got = buf("er", layer, key)[rs, :].astype(F32)
                    out[rs, at : at + got.shape[1]] = got

                row_loop(body, part)

    def grads_close():
        for (layer, key), mode in MODES.items():
            for cp in run_copies(layer, key):
                cp.wait_send()
            if mode == "swap":
                swap_copy(layer, key).wait_send()
                last_copy(layer, key).wait_send()

            @pl.when(s == layer)
            def _(layer=layer, key=key, mode=mode):
                if mode == "run":
                    last_copy(layer, key).wait_send()

            @pl.when(s != layer)
            def _(layer=layer, key=key, mode=mode):
                (home_copy if mode == "swap" else cross_copy)(layer, key).wait_send()

    def rows_of(buf, layer):
        x = buf[layer]
        return x.reshape(full, x.shape[-1])

    stages = (give, second, third, fourth, fifth)
    spots = {
        (1, 0): ("1 1du",),
        (1, 1): ("1 1o",),
        (1, 5): ("2 1du", "1 1q"),
        (1, 2): ("1 1k", "2 1o"),
        (0, 0): ("1 0du",),
        (0, 1): ("1 0o", "2 1qk", "3 1d"),
        (0, 5): ("1 0q", "2 0du", "3 1o"),
        (0, 2): ("1 0k", "2 0o", "2 0q"),
        (0, 3): ("3 0u", "2 0k", "3 0odq", "4 0u", "3 0k", "3 1u", "4 1d", "3 1qk", "4 1uo", "4 0doq", "5 1do"),
        (0, 4): ("5 0uo", "4 0k", "4 1qk"),
    }

    def serve(layer, spot):
        for line in spots.get((layer, spot), ()):
            for key in line[3:]:
                stages[int(line[0]) - 1](int(line[2]), key)

    def back_rows(layer, j, u_buf, r_buf, gain, base, at, extra=None):
        v.stt[...] = jnp.zeros(v.stt.shape, F32)

        def body(rs):
            gsec = sum_rows(j, rs)
            u, r = u_buf[layer, rs, :], r_buf[layer, rs, :]
            gg = gsec * gain
            res = r * (
                gg - jnp.mean(gg, axis=-1, keepdims=True) - u * jnp.mean(gg * u, axis=-1, keepdims=True)
            )
            inn = base[rs, :]
            out = inn + res
            at(rs, out)
            v.stt[0] += gsec * u
            v.stt[1] += gsec
            v.stt[2] += out
            v.stt[3] += inn

        sum_end(j, body)

    def backward_begin(layer):
        def d_second(hf):
            dgel = nt(v.dyb[layer, hf], v.wdb[layer])
            v.du[hf] = (dgel * v.gp[layer, hf]).astype(BF)
            return nt(v.du[hf], v.wub[layer])

        sum_begin(4 + 2 * (1 - layer), d_second)

    def backward(layer):
        j = 4 + 2 * (1 - layer)
        grad_of(layer, "d", rows_of(v.dyb, layer), rows_of(v.gl, layer))
        grad_of(layer, "u", rows_of(v.sb, layer), v.du[...].reshape(full, ff))
        ones = jnp.ones((8, full), BF)
        v.smo[layer, 6:7, :] = nn(ones, v.du[...].reshape(full, ff))[0:1]
        serve(layer, 0)

        def at_two(rs, out):
            v.dhf[rs, :] = out
            v.dhb[layer, c, rs, :] = out.astype(BF)

        back_rows(layer, j, v.u2, v.r2, prow(layer, 1), v.dyf, at_two)
        share(v.dhb, layer, 4 + layer)
        for i, row in ((0, 1), (1, 3), (2, 4), (3, 5)):
            v.smo[layer, row : row + 1, :] = jnp.sum(v.stt[i], axis=0, keepdims=True)

        def d_att(hf):
            rs = pl.ds(pl.multiple_of(hf * two, 16), two)
            v.dgo[layer, rs, :] = nt(v.dhb[layer, hf], v.wob[layer]).astype(BF)

        d_att(c)
        share_wait(v.dhb, layer, 4 + layer)
        d_att(1 - c)
        dat = v.dgo[layer].astype(F32)
        prod = dat * v.attf[layer]
        tile = dat[:, 0:128]
        for h in range(3):
            real = (lane_f >= 64 * h + 64) & (lane_f < 64 * h + 128)
            delta = jnp.sum(jnp.where(real, prod, 0.0), axis=1, keepdims=True)
            for i, piece in enumerate(splits(-delta)):
                tile = jnp.where(lane == 3 * h + i, piece, tile)
        v.dgo[layer, :, 0:128] = tile.astype(BF)
        group_send(v.dgo.at[layer], v.dg.at[layer, own_b], v.s_ds.at[layer], v.s_dr.at[layer])
        grad_of(layer, "o", rows_of(v.dhb, layer), rows_of(v.attb, layer))
        serve(layer, 1)

        put_masked(v.ma, v.qa[layer], k_mask)
        put_masked(v.mb, v.dgo[layer], v_mask)
        v.dqs[...] = jnp.zeros(v.dqs.shape, F32)

        def query_block(bk, carry):
            build_kv(layer, bk)
            kt, vt = v.kt[...], v.vt[...]
            terms = []
            for h in range(3):
                p = jnp.exp(nt(v.ma[h], kt))
                ds = (p * nt(v.mb[h], vt)).astype(BF)
                terms.append(nn(ds, kt))
            v.dqs[...] += by_head_k(terms)
            return carry

        lax.fori_loop(0, nd, query_block, 0)
        for i in range(2):
            rs = slice(i * two, (i + 1) * two)
            v.gm[i, :, 0:128] = (v.dqs[rs, 0:128] * 0.125).astype(BF)
            v.gm[i, :, 128:256] = jnp.where(lane[rs] < 64, v.dqs[rs, 128:256] * 0.125, 0.0).astype(BF)
        grad_of(layer, "q", rows_of(v.nb, layer), v.gm[:, :, 0:256].reshape(full, 256))
        serve(layer, 5)

        build_kv(layer, own_b)
        put_masked(v.ma, v.kt[...], k_mask)
        put_masked(v.mb, v.vt[...], v_mask)
        v.dks[...] = jnp.zeros(v.dks.shape, F32)
        v.dvs[...] = jnp.zeros(v.dvs.shape, F32)

        def key_block(k, carry):
            zk, sk = (zi + k % half) % half, (s + k // half) % 2
            bk = zk + half * sk
            q_at, d_at = v.qg.at[layer, bk], v.dg.at[layer, bk]
            remote(q_at, q_at, v.s_qs.at[layer, 0], v.s_qr.at[layer, bk], me_x).wait_recv()
            remote(d_at, d_at, v.s_ds.at[layer, 0], v.s_dr.at[layer, bk], me_x).wait_recv()
            if big:
                cps = (
                    pltpu.make_async_copy(q_at, v.kt, v.s_loc.at[0]),
                    pltpu.make_async_copy(d_at, v.vt, v.s_loc.at[1]),
                )
                for cp in cps:
                    cp.start()
                for cp in cps:
                    cp.wait()
                key_terms(v.kt[...], v.vt[...])
            else:
                key_terms(q_at[...], d_at[...])
            return carry

        def key_terms(qt, dt):
            tk, tv = [], []
            for h in range(3):
                p = jnp.exp(nt(v.ma[h], qt))
                ds = (p * nt(v.mb[h], dt)).astype(BF)
                tv.append(nn(p.astype(BF), dt))
                tk.append(nn(ds, qt))
            v.dks[...] += by_head_k(tk)
            v.dvs[...] += by_head_v(tv)

        key_terms(v.qa[layer], v.dgo[layer])
        lax.fori_loop(1, nd, key_block, 0)

        for i in range(2):
            rs = slice(i * two, (i + 1) * two)
            v.gm[i, :, 256:384] = v.dks[rs, 0:128].astype(BF)
            v.gm[i, :, 384:512] = jnp.where(lane[rs] < 64, v.dks[rs, 128:256], v.dvs[rs, 0:128]).astype(BF)
            v.gm[i, :, 512:640] = v.dvs[rs, 128:256].astype(BF)
        sum_begin(j + 1, lambda hf: nn(v.gm[hf], v.wqb[layer]))
        grad_of(layer, "k", rows_of(v.nb, layer), v.gm[:, :, 256:640].reshape(full, 384))
        v.smo[layer, 7:8, :] = jnp.zeros((1, dim), F32)
        v.smo[layer, 7:8, 0:640] = nn(ones, v.gm[...].reshape(full, 640))[0:1]
        serve(layer, 2)

        def at_one(rs, out):
            low = out.astype(BF)
            v.dyf[rs, :] = low.astype(F32)
            if layer == 1:
                v.dyb[0, c, rs, :] = low

        back_rows(layer, j + 1, v.u1, v.r1, prow(layer, 0), v.dhf, at_one)
        for i, row in ((0, 0), (1, 2)):
            v.smo[layer, row : row + 1, :] = jnp.sum(v.stt[i], axis=0, keepdims=True)
        if layer == 1:
            share(v.dyb, 0, 7)
        put_out(2 + layer, layer, v.dyf, igs)

    norm_one(0)
    forward(0)
    forward_end(0)
    red(og, v.gq, 1)
    forward(1)
    red_wait(og, v.gq, 1)
    send(v.gq.at[0], v.gq.at[1], v.s_xy.at[2], v.s_xy.at[3], me_y)
    v.dyf[q_own, :] = v.gq[0].astype(F32)
    remote(v.gq.at[0], v.gq.at[1], v.s_xy.at[2], v.s_xy.at[3], me_y).wait_recv()
    v.dyf[q_oth, :] = v.gq[1].astype(F32)
    v.dyb[1, c] = v.dyf[...].astype(BF)
    share(v.dyb, 1, 6)
    share_wait(v.dyb, 1, 6)
    backward_begin(1)
    forward_end(1)
    backward(1)
    share_wait(v.dyb, 0, 7)
    backward_begin(0)
    backward(0)

    send(v.smo, v.smc, v.s_sm.at[0], v.s_sm.at[1], me_c)
    remote(v.smo, v.smc, v.s_sm.at[0], v.s_sm.at[1], me_c).wait_recv()
    rowid = lax.broadcasted_iota(jnp.int32, (8, dim), 0)
    for layer in range(2):
        v.smc[layer] = v.smo[layer] + jnp.where(rowid < 6, v.smc[layer], 0.0)
    for k in range(1, 2 * nd):
        other = (s * nd + z + k) % (2 * nd)
        so = other // nd
        send(v.smc.at[so], v.smr.at[k - 1], v.s_sms.at[k - 1], v.s_smr.at[k - 1], (so, other % nd, t))
    serve(0, 3)
    for k in range(1, 2 * nd):
        remote(v.smr.at[0], v.smr.at[k - 1], v.s_sms.at[k - 1], v.s_smr.at[k - 1], me_x).wait_recv()
    tot = v.smc[s]
    for k in range(1, 2 * nd):
        tot = tot + v.smr[k - 1]
    o_s[...] = tot
    serve(0, 4)

    for cp in late:
        cp.wait_send()

    grads_close()
    for i, src, dst in ((0, fr, v.xq), (1, og, v.gq)):

        @pl.when(keeps)
        def _(i=i, src=src, dst=dst):
            remote(src.at[1 - g], dst.at[0], v.s_red.at[i], v.s_red.at[2 + i], me_o).wait_send()

    for i in range(4):
        forward_w_end(i)
    put_out_wait(0, 0, acts)
    put_out_wait(1, 1, acts)
    put_out_wait(2, 0, igs)
    put_out_wait(3, 1, igs)


def lay_out(nd, a_in, i_in, q_in, u_in, o_in, d_in, sums, acts, igs, g_q, bias, g_o, g_u, upb, g_d, gain, shift, sq):
    for src, dst in ((a_in, acts), (i_in, igs), (u_in, g_u), (d_in, g_d)):
        dst[...] = src[...]
    z, t = lax.axis_index("dp"), lax.axis_index("tensor")
    part, dim = u_in.shape[0], sums.shape[1]
    hl = g_q.shape[2]
    heads, _, hw = bias.shape
    g_q[0] = q_in[:, 0:hl]
    g_q[1] = q_in[:, 256 : 256 + hl]
    g_q[2] = pltpu.roll(q_in[:, 384:640], 192, 1)[:, 0:hl]
    sq[0:part, :] = o_in[...]
    g_o[...] = sq[...].T[64 : 64 + hl, 0:part]

    def from_lane(lo, n):
        return pltpu.roll(sums[...], (dim - lo) % dim, 1)[:, 0:n]

    for h in range(heads):
        bias[h, 0:1, :] = from_lane(h * HD + z * hw, hw)[7:8]
        bias[h, 1:2, :] = from_lane(256 + hl + h * HD + z * hw, hw)[7:8]
        uw = upb.shape[2]
        upb[h] = from_lane((h * nd + z) * uw, uw)[6:7]
    norms = from_lane((z * 4 + t) * gain.shape[1], gain.shape[1])
    gain[...] = norms[0:2]
    shift[...] = norms[2:6]


def local(frames, out_grad, clip_ids, w_qkv, bias_qv, w_out, w_up, bias_up, w_down, ln_gain, shifts):
    rows, dim = frames.shape[1:]
    nd = lax.axis_size("dp")
    half = nd // 2
    z, t, s = lax.axis_index("dp"), lax.axis_index("tensor"), lax.axis_index("section")
    hl = w_qkv.shape[3]
    ff = w_up.shape[2]
    part = dim // nd
    wide = w_qkv[0].transpose(1, 2, 0).reshape(3 * hl, dim)
    clip = lax.dynamic_index_in_dim(clip_ids, z // half, 0, keepdims=False)
    clip = clip.reshape(nd, 4, rows)
    clip = jnp.stack([clip[:, 0], clip[:, 2], clip[:, 1], clip[:, 3]], axis=1).reshape(nd, 4 * rows)
    lane = jnp.arange(128)
    same = clip[:, :, None] == (lane - 80)[None, None, :]
    spot = lane >= 80
    k_feat = jnp.where(
        (lane >= 64) & (lane < 73), 1.0, jnp.where(spot & jnp.logical_not(same), -BIG, 0.0)
    ).astype(BF)
    plan = scratch_plan(nd, rows, dim, hl, ff)
    shape = jax.ShapeDtypeStruct
    anyspec = pl.BlockSpec(memory_space=pl.ANY)
    vspec = pl.BlockSpec(memory_space=pltpu.VMEM)
    gathered = {name: (2, nd, 4 * rows, 256) for name in ("qg", "dg")}
    big = nd > MOST
    if not big:
        plan.update({name: pltpu.VMEM(dims, BF) for name, dims in gathered.items()})
    outs = pl.pallas_call(
        functools.partial(mega, nd, (*gathered, *plan) if big else tuple(plan)),
        out_shape=(
            shape((2, rows, dim), BF),
            shape((2, rows, dim), BF),
            shape((part, 640), F32),
            shape((part, ff), F32),
            shape((part, 256), F32),
            shape((part, ff), F32),
            shape((8, dim), F32),
        )
        + tuple(shape(dims, BF) for dims in gathered.values()) * big,
        in_specs=[anyspec] * 6 + [vspec] * 5,
        out_specs=(anyspec,) * 2 + (vspec,) * 5 + (anyspec,) * (2 * big),
        scratch_shapes=list(plan.values()),
        compiler_params=pltpu.CompilerParams(
            collective_id=0, has_side_effects=True, vmem_limit_bytes=63 * 1024 * 1024
        ),
    )(frames, out_grad, wide, w_out[0], w_up[0], w_down[0], ln_gain[0], shifts[0], bias_up, bias_qv[0], k_feat)

    own, hw, uw = dim // (4 * nd), HD // nd, ff // (hl // HD) // nd
    heads = hl // HD
    acts, igs, g_q, bias, g_o, g_u, upb, g_d, gain, shift = pl.pallas_call(
        functools.partial(lay_out, nd),
        out_shape=(
            shape((2, rows, dim), BF),
            shape((2, rows, dim), BF),
            shape((3, part, hl), F32),
            shape((heads, 2, hw), F32),
            shape((hl, part), F32),
            shape((part, ff), F32),
            shape((heads, 1, uw), F32),
            shape((part, ff), F32),
            shape((2, own), F32),
            shape((4, own), F32),
        ),
        in_specs=[vspec] * 7,
        out_specs=(vspec,) * 10,
        scratch_shapes=[pltpu.VMEM((256, 256), F32)],
    )(*outs[:7])
    return (
        acts[None],
        igs[None],
        g_q.transpose(1, 0, 2)[None],
        bias.transpose(1, 0, 2)[None],
        g_o[None],
        g_u[None],
        upb.transpose(1, 0, 2),
        g_d.T[None],
        gain[None],
        shift[None],
    )


def solution(mesh):
    in_specs = (
        P(None, ("dp", "tensor"), None),
        P(None, ("dp", "tensor"), None),
        P(),
        P("section", None, None, "tensor"),
        P("section", None, "tensor"),
        P("section", "tensor", None),
        P("section", None, "tensor"),
        P("section", "tensor"),
        P("section", "tensor", None),
        P("section", None, None),
        P("section", None, None),
    )
    out_specs = (
        P("section", None, ("dp", "tensor"), None),
        P("section", None, ("dp", "tensor"), None),
        P("section", "dp", None, "tensor"),
        P("section", None, "tensor", "dp"),
        P("section", "tensor", "dp"),
        P("section", "dp", "tensor"),
        P("section", "tensor", "dp"),
        P("section", "tensor", "dp"),
        P("section", None, ("dp", "tensor")),
        P("section", None, ("dp", "tensor")),
    )
    return jax.shard_map(local, mesh=mesh, in_specs=in_specs, out_specs=out_specs, check_vma=False)
```

```python
import functools

import jax
import jax.numpy as jnp
from jax import lax
from jax.experimental import pallas as pl
from jax.experimental.pallas import tpu as pltpu
from jax.sharding import PartitionSpec as P

HD = 64
BIG = 2.0**100
MESH = pl.DeviceIdType.MESH
BF = jnp.bfloat16
F32 = jnp.float32
RB = 16
SLOTS = 4
MOST = 4


def nt(a, b):
    return lax.dot_general(a, b, (((1,), (1,)), ((), ())), preferred_element_type=F32)


def nn(a, b):
    return lax.dot_general(a, b, (((1,), (0,)), ((), ())), preferred_element_type=F32)


def tn(a, b):
    return lax.dot_general(a, b, (((0,), (0,)), ((), ())), preferred_element_type=F32)


def shares(key, ff):
    return {
        "d": (0, ff, ff // 2, ff // 2),
        "u": (ff, ff, ff // 2, ff // 2),
        "o": (2 * ff, 256, 128, 128),
        "q": (2 * ff + 256, 256, 128, 128),
        "k": (2 * ff + 512, 384, 0, 0),
    }[key]


MODES = {
    (1, "d"): "swap",
    (1, "u"): "run",
    (1, "o"): "swap",
    (1, "q"): "run",
    (1, "k"): "run",
    (0, "d"): "run",
    (0, "u"): "swap",
    (0, "o"): "swap",
    (0, "q"): "run",
    (0, "k"): "run",
}


def scratch_plan(nd, rows, dim, head_dim, ff):
    half = nd // 2
    full = 4 * rows
    two = 2 * rows
    part = dim // nd
    wide = 640 + ff + 256 + ff
    vm = pltpu.VMEM
    dma = pltpu.SemaphoreType.DMA
    plan = dict(
        wqb=vm((2, 640, dim), BF),
        wob=vm((2, 256, dim), BF),
        wub=vm((2, dim, ff), BF),
        wdb=vm((2, ff, dim), BF),
        spb=vm((2, 16, dim), F32),
        xq=vm((2, rows, dim), BF),
        gq=vm((2, rows, dim), BF),
        xres=vm((two, dim), F32),
        dyf=vm((two, dim), F32),
        dyb=vm((2, 2, two, dim), BF),
        nb=vm((2, 2, two, dim), BF),
        sb=vm((2, 2, two, dim), BF),
        hid=vm((two, dim), F32),
        u1=vm((2, two, dim), F32),
        u2=vm((2, two, dim), F32),
        r1=vm((2, two, 1), F32),
        r2=vm((2, two, 1), F32),
        qa=vm((2, full, 256), BF),
        kvb=vm((2, nd, full, 384), BF),
        kt=vm((full, 256), BF),
        vt=vm((full, 256), BF),
        dgo=vm((2, full, 256), BF),
        mst=vm((3, full, 1), F32),
        lst=vm((3, full, 1), F32),
        attf=vm((2, full, 256), F32),
        attb=vm((2, 2, two, 256), BF),
        gl=vm((2, 2, two, ff), BF),
        gp=vm((2, 2, two, ff), F32),
        du=vm((2, two, ff), BF),
        dhb=vm((2, 2, two, dim), BF),
        dhf=vm((two, dim), F32),
        gm=vm((2, two, 640), BF),
        ma=vm((3, full, 256), BF),
        mb=vm((3, full, 256), BF),
        dqs=vm((full, 256), F32),
        dks=vm((full, 256), F32),
        dvs=vm((full, 256), F32),
        cs=vm((two, dim), BF),
        cr=vm((SLOTS, two, dim), BF),
        ys=vm((2, two, dim), BF),
        yr=vm((SLOTS, two, dim), BF),
        chip=vm((2, two, dim), F32),
        gr=vm((2, dim, wide), BF),
        smo=vm((2, 8, dim), F32),
        smc=vm((2, 8, dim), F32),
        smr=vm((2 * nd - 1, 8, dim), F32),
        stt=vm((6, RB, dim), F32),
        oq=vm((4, rows, dim), BF),
        s_loc=dma((12,)),
        s_red=dma((4,)),
        s_xy=dma((4,)),
        s_wx=dma((2, 13)),
        s_wzs=dma((12, half)),
        s_wzr=dma((12, half)),
        s_ag=dma((2, 8)),
        s_cc=dma((2, SLOTS)),
        s_yy=dma((2, SLOTS, 2)),
        s_kvs=dma((2, nd, 2)),
        s_kvr=dma((2, nd, 2)),
        s_qs=dma((2, nd)),
        s_qr=dma((2, nd)),
        s_ds=dma((2, nd)),
        s_dr=dma((2, nd)),
        s_sm=dma((2,)),
        s_sms=dma((2 * nd - 1,)),
        s_smr=dma((2 * nd - 1,)),
        s_out=dma((4, 3)),
    )
    for (layer, key), mode in MODES.items():
        n = shares(key, ff)[1 if mode == "run" else 3]
        tag = f"{layer}{key}"
        if mode == "swap":
            plan["xr" + tag] = vm((dim, n), BF)
            plan["s_x" + tag] = dma((2,))
        else:
            plan["bs" + tag] = vm((2, part, n), BF)
            plan["br" + tag] = vm((2, part, n), BF)
            plan["s_b" + tag] = dma((2,))
        plan["ar" + tag] = vm((half - 1, 2, part, n), BF)
        plan["s_a" + tag] = dma((2, half, 2))
        plan["cs" + tag] = vm((part, n), BF)
        plan["cr" + tag] = vm((part, n), BF)
        plan["s_c" + tag] = dma((2,))
        if mode == "swap":
            plan["es" + tag] = vm((part, n), BF)
            plan["er" + tag] = vm((part, n), BF)
            plan["s_e" + tag] = dma((2,))
    return plan


def mega(nd, names, *refs):
    (fr, og, wq, wo, wu, wd, gains, moves, bup, bqv, kf) = refs[:11]
    (acts, igs, o_q, o_u, o_o, o_d, o_s) = refs[11:18]
    b_ = dict(zip(names, refs[18:]))
    big = nd > MOST

    class Bufs:
        pass

    v = Bufs()
    v.__dict__.update(b_)
    half = nd // 2
    rows, dim = fr.shape[1:]
    two, full = 2 * rows, 4 * rows
    ff = wu.shape[1]
    part = dim // nd
    s = lax.axis_index("section")
    z = lax.axis_index("dp")
    t = lax.axis_index("tensor")
    g, zi = z // half, z % half
    c, y = t % 2, t // 2
    own_b = zi + half * s
    zo = (z + half) % nd
    me_x = (1 - s, z, t)
    me_c = (s, z, t + 1 - 2 * c)
    me_y = (s, z, (t + 2) % 4)
    me_o = (s, zo, t)

    def zpeer(d):
        return (s, g * half + (zi + d) % half, t)

    def member(k):
        zk, sk = (zi + k % half) % half, (s + k // half) % 2
        return (sk, g * half + zk, t), zk + half * sk

    def remote(src, dst, ss, rs, dev):
        return pltpu.make_async_remote_copy(
            src_ref=src, dst_ref=dst, send_sem=ss, recv_sem=rs, device_id=dev, device_id_type=MESH
        )

    late = []

    def send(src, dst, ss, rs, dev):
        cp = remote(src, dst, ss, rs, dev)
        cp.start()
        late.append(cp)
        return cp

    loads = [
        pltpu.make_async_copy(wq.at[pl.ds(0, 192)], v.wqb.at[s, pl.ds(0, 192)], v.s_loc.at[0]),
        pltpu.make_async_copy(wq.at[pl.ds(192, 384)], v.wqb.at[s, pl.ds(256, 384)], v.s_loc.at[1]),
        pltpu.make_async_copy(wo, v.wob.at[s, pl.ds(64, 192)], v.s_loc.at[2]),
        pltpu.make_async_copy(wu, v.wub.at[s], v.s_loc.at[3]),
        pltpu.make_async_copy(wd, v.wdb.at[s], v.s_loc.at[4]),
    ]
    for cp in loads:
        cp.start()
    v.wqb[s, pl.ds(192, 64), :] = jnp.zeros((64, dim), BF)
    v.wob[s, pl.ds(0, 64), :] = jnp.zeros((64, dim), BF)
    hl = bqv.shape[1]
    v.spb[s, 0:2, :] = gains[...].astype(F32)
    v.spb[s, 2:6, :] = moves[...].astype(F32)
    v.spb[s, 6:7, :] = bup[...].astype(F32)
    v.spb[s, 7:16, :] = jnp.zeros((9, dim), F32)
    v.spb[s, 7:9, 0:hl] = bqv[...].astype(F32)
    v.spb[s, 8:16, :] = pltpu.roll(v.spb[s, 8:16, :], hl, 1)

    barrier = pltpu.get_barrier_semaphore()
    for k in range(1, 2 * nd):
        other = (s * nd + z + k) % (2 * nd)
        pl.semaphore_signal(barrier, inc=1, device_id=(other // nd, other % nd, t), device_id_type=MESH)
    for dev in (me_c, me_y):
        pl.semaphore_signal(barrier, inc=1, device_id=dev, device_id_type=MESH)
    pl.semaphore_wait(barrier, 2 * nd + 1)

    keeps = g == s

    def red(src, dst, i):
        @pl.when(keeps)
        def _():
            pltpu.make_async_copy(src.at[g], dst.at[0], v.s_loc.at[6 + i]).start()
            remote(src.at[1 - g], dst.at[0], v.s_red.at[i], v.s_red.at[2 + i], me_o).start()

    def red_wait(src, dst, i):
        @pl.when(keeps)
        def _():
            pltpu.make_async_copy(src.at[g], dst.at[0], v.s_loc.at[6 + i]).wait()

        @pl.when(jnp.logical_not(keeps))
        def _():
            remote(src.at[1 - g], dst.at[0], v.s_red.at[i], v.s_red.at[2 + i], me_o).wait_recv()

    red(fr, v.xq, 0)
    for cp in loads[:2]:
        cp.wait()
    mats = (v.wqb, v.wob, v.wub, v.wdb)

    def w_parts(i):
        n = (2, 2, 2, 3)[i]
        return n if mats[i].shape[1] // half % (16 * n) == 0 else 1

    def straight(i, e):
        return i == 3 and e == 2

    def w_rows(i, p, e):
        n = mats[i].shape[1] // half
        m = n // w_parts(i)
        return pl.ds(pl.multiple_of(p * n + e * m, 16), m)

    def ship(i):
        for e in range(w_parts(i)):
            src = mats[i].at[s, w_rows(i, zi, e)]
            send(src, src, v.s_wx.at[0, 3 * i + e], v.s_wx.at[1, 3 * i + e], me_x)
        for e in range(w_parts(i)):
            for d in range(1, half) if straight(i, e) else ():
                src = mats[i].at[s, w_rows(i, (zi + half - d) % half, e)]
                remote(src, src, v.s_wzs.at[3 * i + e, d], v.s_wzr.at[3 * i + e, d], me_x).start()

    send(v.spb.at[s], v.spb.at[s], v.s_wx.at[0, 12], v.s_wx.at[1, 12], me_x)
    ship(0)
    loads[2].wait()
    ship(1)
    loads[3].wait()
    ship(2)
    loads[4].wait()

    def w_copy(i, e, d, back=0):
        src = mats[i].at[1 - s, w_rows(i, (zi + back) % half, e)]
        return remote(src, src, v.s_wzs.at[3 * i + e, d], v.s_wzr.at[3 * i + e, d], zpeer(d))

    def forward_w(i, e=None):
        for e in range(w_parts(i)) if e is None else (e,):
            if e < w_parts(i):
                src = mats[i].at[1 - s, w_rows(i, zi, e)]
                remote(src, src, v.s_wx.at[0, 3 * i + e], v.s_wx.at[1, 3 * i + e], me_x).wait_recv()
                for d in () if straight(i, e) else range(1, half):
                    w_copy(i, e, d).start()

    def forward_w_end(i):
        for e in range(w_parts(i)):
            for d in range(1, half):
                w_copy(i, e, d).wait_send()

    def gather_w(i, layer):
        @pl.when(s != layer)
        def _():
            for e in range(w_parts(i)):
                for d in range(1, half):
                    w_copy(i, e, d, half - d).wait_recv()

    red_wait(fr, v.xq, 0)
    send(v.xq.at[0], v.xq.at[1], v.s_xy.at[0], v.s_xy.at[1], me_y)
    remote(v.spb.at[s], v.spb.at[s], v.s_wx.at[0, 12], v.s_wx.at[1, 12], me_x).wait_recv()
    q_own = pl.ds(pl.multiple_of(rows * y, 8), rows)
    q_oth = pl.ds(pl.multiple_of(rows * (1 - y), 8), rows)
    v.xres[q_own, :] = v.xq[0].astype(F32)
    forward_w(0, 0)
    remote(v.xq.at[0], v.xq.at[1], v.s_xy.at[0], v.s_xy.at[1], me_y).wait_recv()
    v.xres[q_oth, :] = v.xq[1].astype(F32)

    def prow(layer, i):
        return v.spb[layer, i : i + 1, :]

    def row_loop(fn, n=two, first=0):
        def step(i, carry):
            fn(pl.ds(pl.multiple_of(i * RB, RB), RB))
            return carry

        count = n // RB - first // RB
        lax.fori_loop(first // RB, n // RB, step, 0, unroll=count if n <= two else 4)

    def unit(x):
        cen = x - jnp.mean(x, axis=-1, keepdims=True)
        r = lax.rsqrt(jnp.mean(cen * cen, axis=-1, keepdims=True) + 1e-05)
        return cen * r, r

    def share(buf, layer, i):
        src = buf.at[layer, c]
        send(src, src, v.s_ag.at[0, i], v.s_ag.at[1, i], me_c)

    def share_wait(buf, layer, i):
        src = buf.at[layer, 1 - c]
        remote(src, src, v.s_ag.at[0, i], v.s_ag.at[1, i], me_c).wait_recv()

    def norm_one(layer):
        gain, shift = prow(layer, 0), prow(layer, 2)

        def body(rs):
            u, r = unit(v.xres[rs, :])
            v.u1[layer, rs, :] = u
            v.r1[layer, rs, :] = r
            v.nb[layer, c, rs, :] = (u * gain + shift).astype(BF)

        row_loop(body)
        share(v.nb, layer, layer)

    def sum_begin(j, term):
        k = j % SLOTS
        v.cs[...] = term(1 - c).astype(BF)
        cp = remote(v.cs, v.cr.at[k], v.s_cc.at[0, k], v.s_cc.at[1, k], me_c)
        cp.start()
        v.chip[j % 2] = term(c)
        cp.wait()

        def body(rs):
            tot = v.chip[j % 2, rs, :] + v.cr[k, rs, :].astype(F32)
            v.chip[j % 2, rs, :] = tot
            v.ys[j % 2, rs, :] = tot.astype(BF)

        for e in range(2):
            row_loop(body, cuts[e + 1], cuts[e])
            chip_copy(j, e).start()

    cuts = (0, (two // RB + 1) // 2 * RB, two)

    def chip_copy(j, e):
        k, rs = j % SLOTS, pl.ds(cuts[e], cuts[e + 1] - cuts[e])
        return remote(
            v.ys.at[j % 2, rs], v.yr.at[k, rs], v.s_yy.at[0, k, e], v.s_yy.at[1, k, e], me_y
        )

    def sum_end(j, body):
        for e in range(2):
            chip_copy(j, e).wait()
            row_loop(body, cuts[e + 1], cuts[e])

    def sum_rows(j, rs):
        k = j % SLOTS
        return v.chip[j % 2, rs, :] + v.yr[k, rs, :].astype(F32)

    lane_f = lax.broadcasted_iota(jnp.int32, (full, 256), 1)
    lane = lax.broadcasted_iota(jnp.int32, (full, 128), 1)

    def k_mask(h):
        return (
            ((lane_f >= 64 * h) & (lane_f < 64 * h + 64))
            | ((lane_f >= 192 + 3 * h) & (lane_f < 195 + 3 * h))
            | (lane_f >= 208)
        )

    def v_mask(h):
        return ((lane_f >= 64 * h + 64) & (lane_f < 64 * h + 128)) | (
            (lane_f >= 3 * h) & (lane_f < 3 * h + 3)
        )

    def by_head_k(a):
        return jnp.where(lane_f < 64, a[0], jnp.where(lane_f < 128, a[1], a[2]))

    def by_head_v(a):
        return jnp.where(lane_f < 128, a[0], jnp.where(lane_f < 192, a[1], a[2]))

    def put_masked(dst, val, mask):
        val = val.astype(F32)
        for h in range(3):
            dst[h] = jnp.where(mask(h), val, 0.0).astype(BF)

    def build_kv(layer, bk):
        v.kt[:, 0:128] = v.kvb[layer, bk, :, 0:128]
        mid = v.kvb[layer, bk, :, 128:256].astype(F32)
        v.kt[:, 128:256] = jnp.where(lane < 64, mid, kf[bk].astype(F32)).astype(BF)
        v.vt[:, 0:128] = jnp.where(lane < 64, jnp.where(lane < 9, 1.0, 0.0), mid).astype(BF)
        v.vt[:, 128:256] = v.kvb[layer, bk, :, 256:384]

    def splits(x):
        hi = x.astype(BF).astype(F32)
        mid = (x - hi).astype(BF).astype(F32)
        return hi, mid, (x - hi) - mid

    def group_send(src, dst, ss, rs):
        for k in range(nd - 1, 0, -1):
            dev, _ = member(k)
            send(src, dst, ss.at[k], rs.at[own_b], dev)

    def group_wait(buf, layer, rs, k, ss):
        dev, bk = member(k)
        dst = buf.at[layer, bk]
        remote(dst, dst, ss.at[0], rs.at[bk], dev).wait_recv()

    halves = (lambda i: c, lambda i: 1 - c)

    def forward(layer):
        bias_q, bias_kv = v.spb[layer, 7:8, 0:256], v.spb[layer, 8:9, 0:384]

        def qkv(hf):
            r = nt(v.nb[layer, hf], v.wqb[layer])
            rs = pl.ds(pl.multiple_of(hf * two, 16), two)
            q = (r[:, 0:256] + bias_q).astype(BF).astype(F32) * 0.125
            v.qa[layer, rs, 0:128] = q[:, 0:128].astype(BF)
            clip = kf[own_b, rs, :].astype(F32) * (1.0 / BIG) + 1.0
            clip = jnp.where(lane[0:two] >= 80, clip, 0.0)
            v.qa[layer, rs, 128:256] = (q[:, 128:256] + clip).astype(BF)
            v.kvb[layer, own_b, rs, :] = (r[:, 256:640] + bias_kv).astype(BF)

        if layer == 0:
            forward_w(0, 1)
        gather_w(0, layer)
        if layer == 0:
            forward_w(1)
        def kv_send(hf):
            src = v.kvb.at[layer, own_b, pl.ds(pl.multiple_of(hf * two, 16), two)]
            for k in range(nd - 1, 0, -1):
                send(src, src, v.s_kvs.at[layer, k, hf], v.s_kvr.at[layer, own_b, hf], member(k)[0])

        qkv(c)
        kv_send(c)
        share_wait(v.nb, layer, layer)
        qkv(1 - c)
        kv_send(1 - c)

        put_masked(v.ma, v.qa[layer], k_mask)
        v.mst[...] = jnp.full(v.mst.shape, -3e38, F32)
        v.lst[...] = jnp.zeros(v.lst.shape, F32)
        v.dqs[...] = jnp.zeros(v.dqs.shape, F32)

        def block(k, carry):
            zk, sk = (zi + k % half) % half, (s + k // half) % 2
            bk = zk + half * sk

            @pl.when(k > 0)
            def _():
                for e in range(2):
                    dst = v.kvb.at[layer, bk, pl.ds(e * two, two)]
                    remote(dst, dst, v.s_kvs.at[layer, 0, e], v.s_kvr.at[layer, bk, e], me_x).wait_recv()

            if layer == 0:

                @pl.when(k == 1)
                def _():
                    forward_w(2)

            build_kv(layer, bk)
            kt, vt = v.kt[...], v.vt[...]
            alphas, news = [], []
            for h in range(3):
                sc = nt(v.ma[h], kt)
                old = v.mst[h]
                new = jnp.maximum(old, jnp.max(sc, axis=1, keepdims=True))
                alpha = jnp.exp(old - new)
                p = jnp.exp(sc - new)
                v.mst[h] = new
                v.lst[h] = v.lst[h] * alpha + jnp.sum(p, axis=1, keepdims=True)
                hi = p.astype(BF)
                lo = (p - hi.astype(F32)).astype(BF)
                news.append(nn(hi, vt) + nn(lo, vt))
                alphas.append(alpha)
            v.dqs[...] = v.dqs[...] * by_head_v(alphas) + by_head_v(news)
            return carry

        block(0, 0)
        if layer == 0:
            ship(3)
        lax.fori_loop(1, nd, block, 0)

        att = v.dqs[...] * by_head_v([1.0 / v.lst[h] for h in range(3)])
        v.attf[layer] = att
        v.attb[layer] = att.astype(BF).reshape(2, two, 256)
        tile = v.qa[layer, :, 128:256].astype(F32)
        for h in range(3):
            for i, piece in enumerate(splits(-(v.mst[h] + jnp.log(v.lst[h])))):
                tile = jnp.where(lane == 64 + 3 * h + i, piece, tile)
        v.qa[layer, :, 128:256] = tile.astype(BF)
        gather_w(1, layer)
        sum_begin(2 * layer, lambda hf: nn(v.attb[layer, hf], v.wob[layer]))
        if layer == 1:
            for one in (1, 0):
                group_send(v.qa.at[one], v.qg.at[one, own_b], v.s_qs.at[one], v.s_qr.at[one])
        if layer == 0:
            forward_w(3, 0)
        out_bias, gain2, shift2 = prow(layer, 4), prow(layer, 1), prow(layer, 3)

        def body(rs):
            hid = v.xres[rs, :] + sum_rows(2 * layer, rs) + out_bias
            v.hid[rs, :] = hid
            u, r = unit(hid)
            v.u2[layer, rs, :] = u
            v.r2[layer, rs, :] = r
            v.sb[layer, c, rs, :] = (u * gain2 + shift2).astype(BF)

        sum_end(2 * layer, body)
        share(v.sb, layer, 2 + layer)
        if layer == 0:
            forward_w(3, 1)
            forward_w(3, 2)
        gather_w(2, layer)
        bias_up = prow(layer, 6)

        def up(hf):
            v.gp[layer, hf] = nn(v.sb[layer, hf], v.wub[layer]) + bias_up

            def gelu(rs):
                u = v.gp[layer, hf, rs, :]
                phi = 0.5 * (1.0 + lax.erf(u * 0.7071067811865476))
                v.gl[layer, hf, rs, :] = (u * phi).astype(BF)
                v.gp[layer, hf, rs, :] = phi + u * (jnp.exp(-0.5 * u * u) * 0.3989422804014327)

            row_loop(gelu)

        up(c)
        share_wait(v.sb, layer, 2 + layer)
        up(1 - c)
        gather_w(3, layer)
        sum_begin(2 * layer + 1, lambda hf: nn(v.gl[layer, hf], v.wdb[layer]))

    def forward_end(layer):
        out_bias = prow(layer, 5)

        def body(rs):
            out = v.hid[rs, :] + sum_rows(2 * layer + 1, rs) + out_bias
            v.xres[rs, :] = out.astype(BF).astype(F32)

        sum_end(2 * layer + 1, body)
        if layer == 0:
            norm_one(1)
        put_out(layer, layer, v.xres, acts)

    def put_out(i, layer, src, dst):
        v.oq[i] = src[q_own, :].astype(BF)
        here = keeps & (s == layer)

        @pl.when(here)
        def _():
            pltpu.make_async_copy(v.oq.at[i], dst.at[g], v.s_loc.at[8 + i]).start()

        @pl.when(jnp.logical_not(here))
        def _():
            remote(v.oq.at[i], dst.at[g], v.s_out.at[i, 0], v.s_out.at[i, 1 + g], (layer, own_b, t)).start()

    def put_out_wait(i, layer, dst):
        here = keeps & (s == layer)

        @pl.when(here)
        def _():
            pltpu.make_async_copy(v.oq.at[i], dst.at[g], v.s_loc.at[8 + i]).wait()

        @pl.when(jnp.logical_not(here))
        def _():
            remote(v.oq.at[i], dst.at[g], v.s_out.at[i, 0], v.s_out.at[i, 1 + g], (layer, own_b, t)).wait_send()

        @pl.when(s == layer)
        def _():
            def got(m):
                remote(v.oq.at[i], dst.at[m], v.s_out.at[i, 0], v.s_out.at[i, 1 + m], me_x).wait_recv()

            got(1 - g)

            @pl.when(g != s)
            def _():
                got(g)

    def grad_of(layer, key, left, right):
        first, n = shares(key, ff)[:2]
        for i in range(dim // 256):
            lo = i * 256
            v.gr[layer, lo : lo + 256, first : first + n] = tn(left[:, lo : lo + 256], right).astype(BF)

    def buf(name, layer, key):
        return b_[f"{name}{layer}{key}"]

    def swaps(layer, key):
        return MODES[layer, key] == "swap"

    def all_cols(key):
        return pl.ds(*shares(key, ff)[:2])

    def share_cols(key, e):
        first, _, stride, n = shares(key, ff)
        return pl.ds(pl.multiple_of(first + e * stride, 128), n)

    def slice_rows(k, d=0):
        return pl.multiple_of(((zi + d) % half + half * k) * part, 16)

    def swap_copy(layer, key):
        sem = buf("s_x", layer, key)
        return remote(
            v.gr.at[layer, :, share_cols(key, 1 - s)], buf("xr", layer, key), sem.at[0], sem.at[1], me_x
        )

    def run_copy(layer, key, d, k):
        sem, rs = buf("s_a", layer, key), pl.ds(slice_rows(k, d), part)
        if swaps(layer, key):
            src = buf("xr", layer, key).at[rs]
        else:
            src = v.gr.at[layer, rs, all_cols(key)]
        return remote(src, buf("ar", layer, key).at[d - 1, k], sem.at[0, d, k], sem.at[1, d, k], zpeer(d))

    def run_copies(layer, key):
        return [run_copy(layer, key, d, k) for d in range(1, half) for k in range(2)]

    def cross_copy(layer, key):
        sem = buf("s_b", layer, key)
        return remote(buf("bs", layer, key), buf("br", layer, key), sem.at[0], sem.at[1], me_x)

    def last_copy(layer, key):
        sem = buf("s_c", layer, key)
        return remote(buf("cs", layer, key), buf("cr", layer, key), sem.at[0], sem.at[1], me_o)

    def home_copy(layer, key):
        sem = buf("s_e", layer, key)
        return remote(buf("es", layer, key), buf("er", layer, key), sem.at[0], sem.at[1], me_x)

    def run_sum(layer, key, k, rs):
        own = pl.ds(pl.multiple_of(slice_rows(k) + rs.start, 16), RB)
        if swaps(layer, key):
            tot = buf("xr", layer, key)[own, :].astype(F32)
        else:
            tot = v.gr[layer, own, all_cols(key)].astype(F32)
        for d in range(1, half):
            tot = tot + buf("ar", layer, key)[d - 1, k, rs, :].astype(F32)
        return tot

    def out_of(layer, key, e):
        base = e * shares(key, ff)[2] if swaps(layer, key) else 0
        return dict(d=o_d, u=o_u, o=o_o, q=o_q, k=o_q)[key], base + 256 * (key == "k")

    def give(layer, key):
        if swaps(layer, key):
            swap_copy(layer, key).start()
        else:
            for cp in run_copies(layer, key):
                cp.start()

    def second(layer, key):
        if swaps(layer, key):
            swap_copy(layer, key).wait_recv()
            xr = buf("xr", layer, key)

            def body(rs):
                xr[rs, :] = (v.gr[layer, rs, share_cols(key, s)].astype(F32) + xr[rs, :].astype(F32)).astype(BF)

            row_loop(body, dim)
            for cp in run_copies(layer, key):
                cp.start()
            return

        for cp in run_copies(layer, key):
            cp.wait_recv()

        @pl.when(s != layer)
        def _():
            for k in range(2):

                def body(rs, k=k):
                    buf("bs", layer, key)[k, rs, :] = run_sum(layer, key, k, rs).astype(BF)

                row_loop(body, part)
            cross_copy(layer, key).start()

    def third(layer, key):
        cs = buf("cs", layer, key)
        if swaps(layer, key):
            for cp in run_copies(layer, key):
                cp.wait_recv()

            def body(rs):
                cs[rs, :] = run_sum(layer, key, 1 - g, rs).astype(BF)

            row_loop(body, part)
            last_copy(layer, key).start()
            return

        @pl.when(s == layer)
        def _():
            cross_copy(layer, key).wait_recv()
            br = buf("br", layer, key)

            def body(rs):
                cs[rs, :] = (run_sum(layer, key, 1 - g, rs) + br[1 - g, rs, :].astype(F32)).astype(BF)

            row_loop(body, part)
            last_copy(layer, key).start()

    def fourth(layer, key):
        cr = buf("cr", layer, key)
        out, at = out_of(layer, key, layer)

        @pl.when(s == layer)
        def _():
            last_copy(layer, key).wait_recv()

            def body(rs):
                tot = run_sum(layer, key, g, rs) + cr[rs, :].astype(F32)
                if not swaps(layer, key):
                    tot = tot + buf("br", layer, key)[g, rs, :].astype(F32)
                out[rs, at : at + tot.shape[1]] = tot

            row_loop(body, part)

        if swaps(layer, key):

            @pl.when(s != layer)
            def _():
                last_copy(layer, key).wait_recv()

                def body(rs):
                    tot = run_sum(layer, key, g, rs) + cr[rs, :].astype(F32)
                    buf("es", layer, key)[rs, :] = tot.astype(BF)

                row_loop(body, part)
                home_copy(layer, key).start()

    def fifth(layer, key):
        if swaps(layer, key):
            out, at = out_of(layer, key, 1 - layer)

            @pl.when(s == layer)
            def _():
                home_copy(layer, key).wait_recv()

                def body(rs):
                    got = buf("er", layer, key)[rs, :].astype(F32)
                    out[rs, at : at + got.shape[1]] = got

                row_loop(body, part)

    def grads_close():
        for (layer, key), mode in MODES.items():
            for cp in run_copies(layer, key):
                cp.wait_send()
            if mode == "swap":
                swap_copy(layer, key).wait_send()
                last_copy(layer, key).wait_send()

            @pl.when(s == layer)
            def _(layer=layer, key=key, mode=mode):
                if mode == "run":
                    last_copy(layer, key).wait_send()

            @pl.when(s != layer)
            def _(layer=layer, key=key, mode=mode):
                (home_copy if mode == "swap" else cross_copy)(layer, key).wait_send()

    def rows_of(buf, layer):
        x = buf[layer]
        return x.reshape(full, x.shape[-1])

    stages = (give, second, third, fourth, fifth)
    spots = {
        (1, 0): ("1 1du",),
        (1, 1): ("1 1o",),
        (1, 5): ("2 1du", "1 1q"),
        (1, 2): ("1 1k", "2 1o"),
        (0, 0): ("1 0du",),
        (0, 1): ("1 0o", "2 1qk", "3 1d"),
        (0, 5): ("1 0q", "2 0du", "3 1o"),
        (0, 2): ("1 0k", "2 0o", "2 0q"),
        (0, 3): ("3 0u", "2 0k", "3 0odq", "4 0u", "3 0k", "3 1u", "4 1d", "3 1qk", "4 1uo", "4 0doq", "5 1do"),
        (0, 4): ("5 0uo", "4 0k", "4 1qk"),
    }

    def serve(layer, spot):
        for line in spots.get((layer, spot), ()):
            for key in line[3:]:
                stages[int(line[0]) - 1](int(line[2]), key)

    def back_rows(layer, j, u_buf, r_buf, gain, base, at, extra=None):
        v.stt[...] = jnp.zeros(v.stt.shape, F32)

        def body(rs):
            gsec = sum_rows(j, rs)
            u, r = u_buf[layer, rs, :], r_buf[layer, rs, :]
            gg = gsec * gain
            res = r * (
                gg - jnp.mean(gg, axis=-1, keepdims=True) - u * jnp.mean(gg * u, axis=-1, keepdims=True)
            )
            inn = base[rs, :]
            out = inn + res
            at(rs, out)
            v.stt[0] += gsec * u
            v.stt[1] += gsec
            v.stt[2] += out
            v.stt[3] += inn

        sum_end(j, body)

    def backward_begin(layer):
        def d_second(hf):
            dgel = nt(v.dyb[layer, hf], v.wdb[layer])
            v.du[hf] = (dgel * v.gp[layer, hf]).astype(BF)
            return nt(v.du[hf], v.wub[layer])

        sum_begin(4 + 2 * (1 - layer), d_second)

    def backward(layer):
        j = 4 + 2 * (1 - layer)
        grad_of(layer, "d", rows_of(v.dyb, layer), rows_of(v.gl, layer))
        grad_of(layer, "u", rows_of(v.sb, layer), v.du[...].reshape(full, ff))
        ones = jnp.ones((8, full), BF)
        v.smo[layer, 6:7, :] = nn(ones, v.du[...].reshape(full, ff))[0:1]
        serve(layer, 0)

        def at_two(rs, out):
            v.dhf[rs, :] = out
            v.dhb[layer, c, rs, :] = out.astype(BF)

        back_rows(layer, j, v.u2, v.r2, prow(layer, 1), v.dyf, at_two)
        share(v.dhb, layer, 4 + layer)
        for i, row in ((0, 1), (1, 3), (2, 4), (3, 5)):
            v.smo[layer, row : row + 1, :] = jnp.sum(v.stt[i], axis=0, keepdims=True)

        def d_att(hf):
            rs = pl.ds(pl.multiple_of(hf * two, 16), two)
            v.dgo[layer, rs, :] = nt(v.dhb[layer, hf], v.wob[layer]).astype(BF)

        d_att(c)
        share_wait(v.dhb, layer, 4 + layer)
        d_att(1 - c)
        dat = v.dgo[layer].astype(F32)
        prod = dat * v.attf[layer]
        tile = dat[:, 0:128]
        for h in range(3):
            real = (lane_f >= 64 * h + 64) & (lane_f < 64 * h + 128)
            delta = jnp.sum(jnp.where(real, prod, 0.0), axis=1, keepdims=True)
            for i, piece in enumerate(splits(-delta)):
                tile = jnp.where(lane == 3 * h + i, piece, tile)
        v.dgo[layer, :, 0:128] = tile.astype(BF)
        group_send(v.dgo.at[layer], v.dg.at[layer, own_b], v.s_ds.at[layer], v.s_dr.at[layer])
        grad_of(layer, "o", rows_of(v.dhb, layer), rows_of(v.attb, layer))
        serve(layer, 1)

        put_masked(v.ma, v.qa[layer], k_mask)
        put_masked(v.mb, v.dgo[layer], v_mask)
        v.dqs[...] = jnp.zeros(v.dqs.shape, F32)

        def query_block(bk, carry):
            build_kv(layer, bk)
            kt, vt = v.kt[...], v.vt[...]
            terms = []
            for h in range(3):
                p = jnp.exp(nt(v.ma[h], kt))
                ds = (p * nt(v.mb[h], vt)).astype(BF)
                terms.append(nn(ds, kt))
            v.dqs[...] += by_head_k(terms)
            return carry

        lax.fori_loop(0, nd, query_block, 0)
        for i in range(2):
            rs = slice(i * two, (i + 1) * two)
            v.gm[i, :, 0:128] = (v.dqs[rs, 0:128] * 0.125).astype(BF)
            v.gm[i, :, 128:256] = jnp.where(lane[rs] < 64, v.dqs[rs, 128:256] * 0.125, 0.0).astype(BF)
        grad_of(layer, "q", rows_of(v.nb, layer), v.gm[:, :, 0:256].reshape(full, 256))
        serve(layer, 5)

        build_kv(layer, own_b)
        put_masked(v.ma, v.kt[...], k_mask)
        put_masked(v.mb, v.vt[...], v_mask)
        v.dks[...] = jnp.zeros(v.dks.shape, F32)
        v.dvs[...] = jnp.zeros(v.dvs.shape, F32)

        def key_block(k, carry):
            zk, sk = (zi + k % half) % half, (s + k // half) % 2
            bk = zk + half * sk
            q_at, d_at = v.qg.at[layer, bk], v.dg.at[layer, bk]
            remote(q_at, q_at, v.s_qs.at[layer, 0], v.s_qr.at[layer, bk], me_x).wait_recv()
            remote(d_at, d_at, v.s_ds.at[layer, 0], v.s_dr.at[layer, bk], me_x).wait_recv()
            if big:
                cps = (
                    pltpu.make_async_copy(q_at, v.kt, v.s_loc.at[0]),
                    pltpu.make_async_copy(d_at, v.vt, v.s_loc.at[1]),
                )
                for cp in cps:
                    cp.start()
                for cp in cps:
                    cp.wait()
                key_terms(v.kt[...], v.vt[...])
            else:
                key_terms(q_at[...], d_at[...])
            return carry

        def key_terms(qt, dt):
            tk, tv = [], []
            for h in range(3):
                p = jnp.exp(nt(v.ma[h], qt))
                ds = (p * nt(v.mb[h], dt)).astype(BF)
                tv.append(nn(p.astype(BF), dt))
                tk.append(nn(ds, qt))
            v.dks[...] += by_head_k(tk)
            v.dvs[...] += by_head_v(tv)

        key_terms(v.qa[layer], v.dgo[layer])
        lax.fori_loop(1, nd, key_block, 0)

        for i in range(2):
            rs = slice(i * two, (i + 1) * two)
            v.gm[i, :, 256:384] = v.dks[rs, 0:128].astype(BF)
            v.gm[i, :, 384:512] = jnp.where(lane[rs] < 64, v.dks[rs, 128:256], v.dvs[rs, 0:128]).astype(BF)
            v.gm[i, :, 512:640] = v.dvs[rs, 128:256].astype(BF)
        sum_begin(j + 1, lambda hf: nn(v.gm[hf], v.wqb[layer]))
        grad_of(layer, "k", rows_of(v.nb, layer), v.gm[:, :, 256:640].reshape(full, 384))
        v.smo[layer, 7:8, :] = jnp.zeros((1, dim), F32)
        v.smo[layer, 7:8, 0:640] = nn(ones, v.gm[...].reshape(full, 640))[0:1]
        serve(layer, 2)

        def at_one(rs, out):
            low = out.astype(BF)
            v.dyf[rs, :] = low.astype(F32)
            if layer == 1:
                v.dyb[0, c, rs, :] = low

        back_rows(layer, j + 1, v.u1, v.r1, prow(layer, 0), v.dhf, at_one)
        for i, row in ((0, 0), (1, 2)):
            v.smo[layer, row : row + 1, :] = jnp.sum(v.stt[i], axis=0, keepdims=True)
        if layer == 1:
            share(v.dyb, 0, 7)
        put_out(2 + layer, layer, v.dyf, igs)

    norm_one(0)
    forward(0)
    forward_end(0)
    red(og, v.gq, 1)
    forward(1)
    red_wait(og, v.gq, 1)
    send(v.gq.at[0], v.gq.at[1], v.s_xy.at[2], v.s_xy.at[3], me_y)
    v.dyf[q_own, :] = v.gq[0].astype(F32)
    remote(v.gq.at[0], v.gq.at[1], v.s_xy.at[2], v.s_xy.at[3], me_y).wait_recv()
    v.dyf[q_oth, :] = v.gq[1].astype(F32)
    v.dyb[1, c] = v.dyf[...].astype(BF)
    share(v.dyb, 1, 6)
    share_wait(v.dyb, 1, 6)
    backward_begin(1)
    forward_end(1)
    backward(1)
    share_wait(v.dyb, 0, 7)
    backward_begin(0)
    backward(0)

    send(v.smo, v.smc, v.s_sm.at[0], v.s_sm.at[1], me_c)
    remote(v.smo, v.smc, v.s_sm.at[0], v.s_sm.at[1], me_c).wait_recv()
    rowid = lax.broadcasted_iota(jnp.int32, (8, dim), 0)
    for layer in range(2):
        v.smc[layer] = v.smo[layer] + jnp.where(rowid < 6, v.smc[layer], 0.0)
    for k in range(1, 2 * nd):
        other = (s * nd + z + k) % (2 * nd)
        so = other // nd
        send(v.smc.at[so], v.smr.at[k - 1], v.s_sms.at[k - 1], v.s_smr.at[k - 1], (so, other % nd, t))
    serve(0, 3)
    for k in range(1, 2 * nd):
        remote(v.smr.at[0], v.smr.at[k - 1], v.s_sms.at[k - 1], v.s_smr.at[k - 1], me_x).wait_recv()
    tot = v.smc[s]
    for k in range(1, 2 * nd):
        tot = tot + v.smr[k - 1]
    o_s[...] = tot
    serve(0, 4)

    for cp in late:
        cp.wait_send()

    grads_close()
    for i, src, dst in ((0, fr, v.xq), (1, og, v.gq)):

        @pl.when(keeps)
        def _(i=i, src=src, dst=dst):
            remote(src.at[1 - g], dst.at[0], v.s_red.at[i], v.s_red.at[2 + i], me_o).wait_send()

    for i in range(4):
        forward_w_end(i)
    put_out_wait(0, 0, acts)
    put_out_wait(1, 1, acts)
    put_out_wait(2, 0, igs)
    put_out_wait(3, 1, igs)


def lay_out(nd, a_in, i_in, q_in, u_in, o_in, d_in, sums, acts, igs, g_q, bias, g_o, g_u, upb, g_d, gain, shift, sq):
    for src, dst in ((a_in, acts), (i_in, igs), (u_in, g_u), (d_in, g_d)):
        dst[...] = src[...]
    z, t = lax.axis_index("dp"), lax.axis_index("tensor")
    part, dim = u_in.shape[0], sums.shape[1]
    hl = g_q.shape[2]
    heads, _, hw = bias.shape
    g_q[0] = q_in[:, 0:hl]
    g_q[1] = q_in[:, 256 : 256 + hl]
    g_q[2] = pltpu.roll(q_in[:, 384:640], 192, 1)[:, 0:hl]
    sq[0:part, :] = o_in[...]
    g_o[...] = sq[...].T[64 : 64 + hl, 0:part]

    def from_lane(lo, n):
        return pltpu.roll(sums[...], (dim - lo) % dim, 1)[:, 0:n]

    for h in range(heads):
        bias[h, 0:1, :] = from_lane(h * HD + z * hw, hw)[7:8]
        bias[h, 1:2, :] = from_lane(256 + hl + h * HD + z * hw, hw)[7:8]
        uw = upb.shape[2]
        upb[h] = from_lane((h * nd + z) * uw, uw)[6:7]
    norms = from_lane((z * 4 + t) * gain.shape[1], gain.shape[1])
    gain[...] = norms[0:2]
    shift[...] = norms[2:6]


def local(frames, out_grad, clip_ids, w_qkv, bias_qv, w_out, w_up, bias_up, w_down, ln_gain, shifts):
    rows, dim = frames.shape[1:]
    nd = lax.axis_size("dp")
    half = nd // 2
    z, t, s = lax.axis_index("dp"), lax.axis_index("tensor"), lax.axis_index("section")
    hl = w_qkv.shape[3]
    ff = w_up.shape[2]
    part = dim // nd
    wide = w_qkv[0].transpose(1, 2, 0).reshape(3 * hl, dim)
    clip = lax.dynamic_index_in_dim(clip_ids, z // half, 0, keepdims=False)
    clip = clip.reshape(nd, 4, rows)
    clip = jnp.stack([clip[:, 0], clip[:, 2], clip[:, 1], clip[:, 3]], axis=1).reshape(nd, 4 * rows)
    lane = jnp.arange(128)
    same = clip[:, :, None] == (lane - 80)[None, None, :]
    spot = lane >= 80
    k_feat = jnp.where(
        (lane >= 64) & (lane < 73), 1.0, jnp.where(spot & jnp.logical_not(same), -BIG, 0.0)
    ).astype(BF)
    plan = scratch_plan(nd, rows, dim, hl, ff)
    shape = jax.ShapeDtypeStruct
    anyspec = pl.BlockSpec(memory_space=pl.ANY)
    vspec = pl.BlockSpec(memory_space=pltpu.VMEM)
    gathered = {name: (2, nd, 4 * rows, 256) for name in ("qg", "dg")}
    big = nd > MOST
    if not big:
        plan.update({name: pltpu.VMEM(dims, BF) for name, dims in gathered.items()})
    outs = pl.pallas_call(
        functools.partial(mega, nd, (*gathered, *plan) if big else tuple(plan)),
        out_shape=(
            shape((2, rows, dim), BF),
            shape((2, rows, dim), BF),
            shape((part, 640), F32),
            shape((part, ff), F32),
            shape((part, 256), F32),
            shape((part, ff), F32),
            shape((8, dim), F32),
        )
        + tuple(shape(dims, BF) for dims in gathered.values()) * big,
        in_specs=[anyspec] * 6 + [vspec] * 5,
        out_specs=(anyspec,) * 2 + (vspec,) * 5 + (anyspec,) * (2 * big),
        scratch_shapes=list(plan.values()),
        compiler_params=pltpu.CompilerParams(
            collective_id=0, has_side_effects=True, vmem_limit_bytes=63 * 1024 * 1024
        ),
    )(frames, out_grad, wide, w_out[0], w_up[0], w_down[0], ln_gain[0], shifts[0], bias_up, bias_qv[0], k_feat)

    own, hw, uw = dim // (4 * nd), HD // nd, ff // (hl // HD) // nd
    heads = hl // HD
    acts, igs, g_q, bias, g_o, g_u, upb, g_d, gain, shift = pl.pallas_call(
        functools.partial(lay_out, nd),
        out_shape=(
            shape((2, rows, dim), BF),
            shape((2, rows, dim), BF),
            shape((3, part, hl), F32),
            shape((heads, 2, hw), F32),
            shape((hl, part), F32),
            shape((part, ff), F32),
            shape((heads, 1, uw), F32),
            shape((part, ff), F32),
            shape((2, own), F32),
            shape((4, own), F32),
        ),
        in_specs=[vspec] * 7,
        out_specs=(vspec,) * 10,
        scratch_shapes=[pltpu.VMEM((256, 256), F32)],
    )(*outs[:7])
    return (
        acts[None],
        igs[None],
        g_q.transpose(1, 0, 2)[None],
        bias.transpose(1, 0, 2)[None],
        g_o[None],
        g_u[None],
        upb.transpose(1, 0, 2),
        g_d.T[None],
        gain[None],
        shift[None],
    )


def solution(mesh):
    in_specs = (
        P(None, ("dp", "tensor"), None),
        P(None, ("dp", "tensor"), None),
        P(),
        P("section", None, None, "tensor"),
        P("section", None, "tensor"),
        P("section", "tensor", None),
        P("section", None, "tensor"),
        P("section", "tensor"),
        P("section", "tensor", None),
        P("section", None, None),
        P("section", None, None),
    )
    out_specs = (
        P("section", None, ("dp", "tensor"), None),
        P("section", None, ("dp", "tensor"), None),
        P("section", "dp", None, "tensor"),
        P("section", None, "tensor", "dp"),
        P("section", "tensor", "dp"),
        P("section", "dp", "tensor"),
        P("section", "tensor", "dp"),
        P("section", "tensor", "dp"),
        P("section", None, ("dp", "tensor")),
        P("section", None, ("dp", "tensor")),
    )
    return jax.shard_map(local, mesh=mesh, in_specs=in_specs, out_specs=out_specs, check_vma=False)
```
